256 devices in a mesh: gz: 64 (over y, x_lo, z), view: 4 (over x_hi, core).
Axes of the slice: x: 4 (x_hi: 2, x_lo: 2; x = x_hi * 2 + x_lo), y: 4, z: 8, core: 2. Of those that a mesh axis runs over, the one named last changes fastest.
Arguments:
- estimate: float32 [1280, 128, 128], P('gz'), may hold values from 0.25 to 4
- recordings: bfloat16 [8, 1280, 128, 128], P('view', 'gz'), may hold values from 0.25 to 4
- psf_taps: float32 [8, 3, 2, 21], P('view'), may hold values from 0.05 to 1
Outputs:
- updated: float32 [1280, 128, 128], P('gz', 'view')
The draws below stay inside these ranges and needn't reach their ends.
All inputs are finite; a program needn't handle non-finite values.
Results may differ from the reference program's by a relative error of at most 0.00075.
Values may be sent and summed in bfloat16 or wider, within the bound.
No kernel may reach another device: no remote copies, remote signals or barrier semaphores. Data moves between devices by JAX's collectives and lax.ppermute only.
A program may use at most 128 MiB of HBM per device.

```python
import math
import jax
import jax.numpy as jnp
from jax import lax

NY = 128
NX = 128
TAPS = 21
VIEWS = 8
NZ = 1280


def level_of(rng, shape, cuts, least, high):
    def one(position, parts):
        heights = jax.random.uniform(jax.random.fold_in(jax.random.fold_in(rng, 6), position), (parts,), jnp.float32, least / len(cuts), high / len(cuts))
        return jnp.repeat(jnp.exp(heights), shape[position] // parts).reshape((-1,) + (1,) * (len(shape) - position - 1))

    level = one(*cuts[0])
    for cut in cuts[1:]:
        level = level * one(*cut)
    return level


def setup_inputs(seed: int = 0) -> dict:
    seeds = jax.random.split(jax.random.key(seed), 4)
    estimate = jnp.clip(jnp.exp(math.log(4.0) - 2.7725887 * jax.random.uniform(seeds[0], (NZ, NY, NX), jnp.float32) ** level_of(seeds[0], (NZ, NY, NX), ((0, 64),), -0.2, 0.2)), 0.25, 4.0)
    recordings = jnp.clip(jnp.exp(math.log(4.0) - 2.7725887 * jax.random.uniform(seeds[1], (VIEWS, NZ, NY, NX), jnp.float32) ** level_of(seeds[1], (VIEWS, NZ, NY, NX), ((0, 4), (1, 64)), -0.2, 0.2)), 0.25, 4.0).astype(jnp.bfloat16)
    psf_taps = jnp.clip(jnp.exp(math.log(1.0) - 2.9957323 * jax.random.uniform(seeds[2], (VIEWS, 3, 2, TAPS), jnp.float32) ** level_of(seeds[2], (VIEWS, 3, 2, TAPS), ((0, 4),), -0.2, 0.2)), 0.05, 1.0)
    return dict(estimate=estimate, recordings=recordings, psf_taps=psf_taps)


def correlate(padded, kernel, axis_no, length):
    summed = kernel[0] * lax.slice_in_dim(padded, 0, length, axis=axis_no)
    for offset in range(1, kernel.shape[0]):
        summed = summed + kernel[offset] * lax.slice_in_dim(padded, offset, offset + length, axis=axis_no)
    return summed


def widen(volume, axis_no, margin):
    widths = [(0, 0)] * volume.ndim
    widths[axis_no] = (margin, margin)
    return jnp.pad(volume, widths)


def kernels(tap_table):
    along_x = tap_table[0] / jnp.sum(tap_table[0], axis=1, keepdims=True)
    along_y = tap_table[1] / jnp.sum(tap_table[1], axis=1, keepdims=True)
    along_z = tap_table[2] / jnp.sum(tap_table[2])
    return along_x, along_y, along_z


def blur_planes(extended, along_x, along_y, along_z):
    margin = (along_x.shape[1] - 1) // 2
    planes = extended.shape[0] - along_z.shape[1] + 1

    def one_rank(rank_index):
        filtered = correlate(widen(extended, 2, margin), along_x[rank_index], 2, extended.shape[2])
        filtered = correlate(widen(filtered, 1, margin), along_y[rank_index], 1, extended.shape[1])
        return correlate(filtered, along_z[rank_index], 0, planes)

    return one_rank(0) + one_rank(1)


def reference(estimate, recordings, psf_taps):
    margin = (TAPS - 1) // 2

    def one_view(product, inputs):
        observed, tap_table = inputs
        along_x, along_y, along_z = kernels(tap_table)
        blurred = blur_planes(widen(estimate, 0, margin), along_x, along_y, along_z)
        quotient = observed.astype(jnp.float32) / blurred
        correction = blur_planes(widen(quotient, 0, margin), along_x[:, ::-1], along_y[:, ::-1], along_z[:, ::-1])
        return product * correction, None

    product, unused = lax.scan(one_view, jnp.ones_like(estimate), (recordings, psf_taps))
    return estimate * product
```

```python
import jax
import jax.numpy as jnp
from jax import lax
from jax.experimental import pallas as pl
from jax.experimental.pallas import tpu as pltpu
from jax.sharding import PartitionSpec as P

F32 = jnp.float32
BF16 = jnp.bfloat16
VMEM = pl.BlockSpec(memory_space=pltpu.VMEM)
SMEM = pl.BlockSpec(memory_space=pltpu.SMEM)
LIMIT = 48 * 1024 * 1024


def split(value):
    high = value.astype(BF16)
    return high, (value - high.astype(F32)).astype(BF16)


def params(flops, nbytes):
    return dict(
        compiler_params=pltpu.CompilerParams(vmem_limit_bytes=LIMIT),
        cost_estimate=pl.CostEstimate(flops=flops, bytes_accessed=nbytes, transcendentals=0),
    )


def matrices_kernel(place_ref, taps_ref, z_ref, x_ref, y_ref):
    views, taps = taps_ref.shape[0], taps_ref.shape[3]
    half = (taps - 1) // 2
    rows = x_ref.shape[3] // 2
    place = place_ref[0]
    zeros = jnp.zeros((rows, rows), BF16)

    def inverse(values):
        total = values[0]
        for value in values[1:]:
            total = total + value
        return total

    for v in range(views):
        tap = {
            (d, r): [taps_ref[v, d, r, j] for j in range(taps)] for d in range(3) for r in range(2)
        }
        scale = {}
        for r in range(2):
            for d in range(2):
                scale[d, r] = 1.0 / jnp.full((8, 128), inverse(tap[d, r]), F32)[0:1]
            scale[2, r] = 1.0 / jnp.full((8, 128), inverse(tap[2, 0] + tap[2, 1]), F32)[0:1]
        for direction in range(2):
            for part in range(2):
                for r in range(2):
                    other = 1 - r
                    x_ref[direction, v, part, r * rows : (r + 1) * rows, other * rows : (other + 1) * rows] = zeros
        step = 32
        for first in range(0, rows, step):
            diff = (
                lax.broadcasted_iota(jnp.int32, (step, rows), 0)
                - lax.broadcasted_iota(jnp.int32, (step, rows), 1)
                + (first + half)
            )
            made = {(d, r, m): jnp.zeros((step, rows), F32) for d in range(2) for r in range(2) for m in range(2)}
            for j in range(taps):
                here = diff == j
                for d, r, m in made:
                    pick = tap[d, r][j] if m == 0 else tap[d, r][taps - 1 - j]
                    made[d, r, m] = jnp.where(here, pick, made[d, r, m])
            for (d, r, m), value in made.items():
                parts = split(value * scale[d, r])
                for part in range(2):
                    lanes = slice(r * rows, (r + 1) * rows)
                    if d == 0:
                        x_ref[m, v, part, r * rows + first : r * rows + first + step, lanes] = parts[part]
                    elif m == 1:
                        y_ref[0, v, part, first : first + step, lanes] = parts[part]
                    else:
                        target = pl.multiple_of(jnp.bitwise_xor(first // step, place) * step, step)
                        y_ref[1, v, part, pl.ds(target, step), lanes] = parts[part]
        tall = z_ref.shape[3] // 2
        wide = z_ref.shape[4]
        step = 16
        for first in range(0, tall, step):
            diff = (
                lax.broadcasted_iota(jnp.int32, (step, wide), 1)
                - lax.broadcasted_iota(jnp.int32, (step, wide), 0)
                - first
            )
            made = {(r, m): jnp.zeros((step, wide), F32) for r in range(2) for m in range(2)}
            for j in range(taps):
                here = diff == 8 * j
                for r, m in made:
                    pick = tap[2, r][j] if m == 0 else tap[2, r][taps - 1 - j]
                    made[r, m] = jnp.where(here, pick, made[r, m])
            for (r, m), value in made.items():
                parts = split(value * scale[2, r][0:1, 0:1])
                for part in range(2):
                    z_ref[m, v, part, r * tall + first : r * tall + first + step, :] = parts[part]


def dot(a, b):
    return jnp.dot(a, b, preferred_element_type=F32)


def filter_to(pieces, z_ref, x_ref, y_ref, g_ref, exact, emit):
    tall = z_ref.shape[1] // 2
    z_out = tall // 8
    taps_reach = sum(piece.shape[0] for piece in pieces) - 2 * z_out
    rows = y_ref.shape[1]
    for pair in range(rows // 16):
        at = slice(pair * 16, pair * 16 + 16)
        block = jnp.concatenate([piece[:, at, :].astype(F32) for piece in pieces], axis=0)
        planes = block.shape[0]
        octets = [block[:, 8 * o : 8 * o + 8, :].reshape(planes * 8, rows).astype(BF16) for o in range(2)]
        octets = jnp.concatenate(octets, axis=1)
        for part in range(2):
            begin = part * z_out * 8
            data = octets[begin : begin + (z_out + taps_reach) * 8]
            depth = data.shape[0]
            e = dot(z_ref[0, :, :depth], data) + dot(z_ref[1, :, :depth], data)
            e = jnp.concatenate(
                [
                    jnp.concatenate([e[:tall, o * rows : (o + 1) * rows], e[tall:, o * rows : (o + 1) * rows]], axis=1)
                    for o in range(2)
                ],
                axis=0,
            )
            if exact:
                high, low = split(e)
                g = dot(high, x_ref[0]) + dot(high, x_ref[1]) + dot(low, x_ref[0])
            else:
                high = e.astype(BF16)
                g = dot(high, x_ref[0]) + dot(high, x_ref[1])
            for r in range(2):
                lanes = slice(r * rows, (r + 1) * rows)
                g_rows = jnp.concatenate([g[o * tall : (o + 1) * tall, lanes].reshape(z_out, 8, rows) for o in range(2)], axis=1)
                target = slice(r * rows + pair * 16, r * rows + pair * 16 + 16)
                planes_at = slice(part * z_out, (part + 1) * z_out)
                if exact:
                    high, low = split(g_rows)
                    g_ref[0, planes_at, target, :] = high
                    g_ref[1, planes_at, target, :] = low
                else:
                    g_ref[0, planes_at, target, :] = g_rows.astype(BF16)
    for z in range(0, 2 * z_out, 2):
        data = jnp.concatenate([g_ref[0, z], g_ref[0, z + 1]], axis=1)
        out = dot(y_ref[0], data) + dot(y_ref[1], data)
        if exact:
            data = jnp.concatenate([g_ref[1, z], g_ref[1, z + 1]], axis=1)
            out = out + dot(y_ref[0], data)
        emit(z, out[:, :rows])
        emit(z + 1, out[:, rows:])


def quotient_kernel(v, before_ref, own_ref, after_ref, rec_ref, z_ref, x_ref, y_ref, low_ref, high_ref, g_ref):
    margin = low_ref.shape[0]

    def emit(z, blurred):
        quotient = (rec_ref[v, z].astype(F32) / blurred).astype(BF16)
        if z < margin:
            low_ref[z] = quotient
        else:
            high_ref[z - margin] = quotient

    pieces = [before_ref, own_ref, after_ref]
    filter_to(pieces, z_ref.at[0, v], x_ref.at[0, v], y_ref.at[0, v], g_ref, False, emit)


def first_correction_kernel(v, before_ref, low_ref, high_ref, after_ref, z_ref, x_ref, y_ref, out_ref, g_ref):
    def emit(z, correction):
        out_ref[z] = correction

    pieces = [before_ref, low_ref, high_ref, after_ref]
    filter_to(pieces, z_ref.at[1, v], x_ref.at[1, v], y_ref.at[1, v], g_ref, True, emit)


def last_correction_kernel(
    v, before_ref, low_ref, high_ref, after_ref, earlier_ref, z_ref, x_ref, y_ref, keep_ref, send_ref, g_ref
):
    part = keep_ref.shape[2]

    def emit(z, correction):
        product = correction * earlier_ref[z]
        for b in range(4):
            rows = product[b * part : (b + 1) * part]
            if b % 2 == 0:
                keep_ref[b // 2, z] = rows
            else:
                send_ref[b // 2, z] = rows

    pieces = [before_ref, low_ref, high_ref, after_ref]
    filter_to(pieces, z_ref.at[1, v], x_ref.at[1, v], y_ref.at[1, v], g_ref, True, emit)


def local(estimate, recordings, psf_taps):
    planes, rows, cols = estimate.shape
    taps = psf_taps.shape[-1]
    margin = (taps - 1) // 2
    views = recordings.shape[0]
    devices = lax.axis_size("gz")
    place = lax.axis_index("view")
    up = [(i, i + 1) for i in range(devices - 1)]
    down = [(i + 1, i) for i in range(devices - 1)]
    z_out = planes // 2

    before = lax.ppermute(estimate[planes - margin :].astype(BF16), "gz", up)
    after = lax.ppermute(estimate[:margin].astype(BF16), "gz", down)

    shape = jax.ShapeDtypeStruct
    wide = -(-(z_out + taps - 1) * 8 // 128) * 128
    z_mat, x_mat, y_mat = pl.pallas_call(
        matrices_kernel,
        out_shape=[
            shape((2, views, 2, 2 * z_out * 8, wide), BF16),
            shape((2, views, 2, 2 * cols, 2 * cols), BF16),
            shape((2, views, 2, rows, 2 * rows), BF16),
        ],
        in_specs=[SMEM, SMEM],
        out_specs=[VMEM] * 3,
        name="matrices",
        **params(10**9, 10**7),
    )(place.reshape(1).astype(jnp.int32), psf_taps)

    halves = []
    for v in range(views):
        halves.append(
            pl.pallas_call(
                lambda *refs, v=v: quotient_kernel(v, *refs),
                out_shape=[shape((margin, rows, cols), BF16), shape((planes - margin, rows, cols), BF16)],
                in_specs=[VMEM] * 7,
                out_specs=[VMEM] * 2,
                scratch_shapes=[pltpu.VMEM((1, planes, 2 * rows, cols), BF16)],
                name="quotient",
                **params(3 * 10**9, 5 * 10**6),
            )(before, estimate, after, recordings, z_mat, x_mat, y_mat)
        )
    sent = [(lax.ppermute(high, "gz", up), lax.ppermute(low, "gz", down)) for low, high in halves]
    product = pl.pallas_call(
        lambda *refs: first_correction_kernel(0, *refs),
        out_shape=shape((planes, rows, cols), F32),
        in_specs=[VMEM] * 7,
        out_specs=VMEM,
        scratch_shapes=[pltpu.VMEM((2, planes, 2 * rows, cols), BF16)],
        name="correction",
        **params(3 * 10**9, 5 * 10**6),
    )(sent[0][0], *halves[0], sent[0][1], z_mat, x_mat, y_mat)
    part = rows // 4
    keep, send = pl.pallas_call(
        lambda *refs: last_correction_kernel(1, *refs),
        out_shape=[shape((2, planes, part, cols), F32)] * 2,
        in_specs=[VMEM] * 8,
        out_specs=[VMEM] * 2,
        scratch_shapes=[pltpu.VMEM((2, planes, 2 * rows, cols), BF16)],
        name="corrections",
        **params(3 * 10**9, 5 * 10**6),
    )(sent[1][0], *halves[1], sent[1][1], product, z_mat, x_mat, y_mat)
    core = lax.ppermute(send, "view", [(i, i ^ 1) for i in range(4)])
    across = lax.ppermute(keep[1] * core[1], "view", [(i, i ^ 2) for i in range(4)])
    own = lax.dynamic_slice_in_dim(estimate, place * part, part, 1)
    return own * (keep[0] * core[0]) * across


def solution(mesh):
    in_specs = (P("gz", None, None), P("view", "gz", None, None), P("view", None, None, None))
    out_specs = P("gz", "view", None)
    return jax.shard_map(local, mesh=mesh, in_specs=in_specs, out_specs=out_specs, check_vma=False)
```

```python
import jax
import jax.numpy as jnp
from jax import lax
from jax.experimental import pallas as pl
from jax.experimental.pallas import tpu as pltpu
from jax.sharding import PartitionSpec as P

F32 = jnp.float32
BF16 = jnp.bfloat16
VMEM = pl.BlockSpec(memory_space=pltpu.VMEM)
SMEM = pl.BlockSpec(memory_space=pltpu.SMEM)
LIMIT = 48 * 1024 * 1024


def split(value):
    high = value.astype(BF16)
    return high, (value - high.astype(F32)).astype(BF16)


def params(flops, nbytes):
    return dict(
        compiler_params=pltpu.CompilerParams(vmem_limit_bytes=LIMIT),
        cost_estimate=pl.CostEstimate(flops=flops, bytes_accessed=nbytes, transcendentals=0),
    )


def matrices_kernel(place_ref, taps_ref, z_ref, x_ref, y_ref):
    views, taps = taps_ref.shape[0], taps_ref.shape[3]
    half = (taps - 1) // 2
    rows = x_ref.shape[3] // 2
    place = place_ref[0]
    zeros = jnp.zeros((rows, rows), BF16)

    def inverse(values):
        total = values[0]
        for value in values[1:]:
            total = total + value
        return total

    for v in range(views):
        tap = {
            (d, r): [taps_ref[v, d, r, j] for j in range(taps)] for d in range(3) for r in range(2)
        }
        scale = {}
        for r in range(2):
            for d in range(2):
                scale[d, r] = 1.0 / jnp.full((8, 128), inverse(tap[d, r]), F32)[0:1]
            scale[2, r] = 1.0 / jnp.full((8, 128), inverse(tap[2, 0] + tap[2, 1]), F32)[0:1]
        for direction in range(2):
            for part in range(2):
                for r in range(2):
                    other = 1 - r
                    x_ref[direction, v, part, r * rows : (r + 1) * rows, other * rows : (other + 1) * rows] = zeros
        step = 32
        for first in range(0, rows, step):
            diff = (
                lax.broadcasted_iota(jnp.int32, (step, rows), 0)
                - lax.broadcasted_iota(jnp.int32, (step, rows), 1)
                + (first + half)
            )
            made = {(d, r, m): jnp.zeros((step, rows), F32) for d in range(2) for r in range(2) for m in range(2)}
            for j in range(taps):
                here = diff == j
                for d, r, m in made:
                    pick = tap[d, r][j] if m == 0 else tap[d, r][taps - 1 - j]
                    made[d, r, m] = jnp.where(here, pick, made[d, r, m])
            for (d, r, m), value in made.items():
                parts = split(value * scale[d, r])
                for part in range(2):
                    lanes = slice(r * rows, (r + 1) * rows)
                    if d == 0:
                        x_ref[m, v, part, r * rows + first : r * rows + first + step, lanes] = parts[part]
                    elif m == 1:
                        y_ref[0, v, part, first : first + step, lanes] = parts[part]
                    else:
                        target = pl.multiple_of(jnp.bitwise_xor(first // step, place) * step, step)
                        y_ref[1, v, part, pl.ds(target, step), lanes] = parts[part]
        tall = z_ref.shape[2] // (2 * views)
        wide = z_ref.shape[3]
        step = 16
        for first in range(0, tall, step):
            diff = (
                lax.broadcasted_iota(jnp.int32, (step, wide), 1)
                - lax.broadcasted_iota(jnp.int32, (step, wide), 0)
                - first
            )
            made = {(r, m): jnp.zeros((step, wide), F32) for r in range(2) for m in range(2)}
            for j in range(taps):
                here = diff == 8 * j
                for r, m in made:
                    pick = tap[2, r][j] if m == 0 else tap[2, r][taps - 1 - j]
                    made[r, m] = jnp.where(here, pick, made[r, m])
            for (r, m), value in made.items():
                parts = split(value * scale[2, r][0:1, 0:1])
                for part in range(2):
                    top = (2 * v + r) * tall + first
                    z_ref[m, part, top : top + step, :] = parts[part]


def dot(a, b):
    return jnp.dot(a, b, preferred_element_type=F32)


def filter_to(load, views, groups, z_ref, x_ref, y_ref, g_ref, exact, emit):
    tall = z_ref.shape[1] // (2 * views)
    z_out = tall // 8
    rows = y_ref.shape[2]
    for pair in range(rows // 16):
        block = load(slice(pair * 16, pair * 16 + 16))
        planes = block.shape[0]
        depth = (planes - (groups - 1) * z_out) * 8
        octets = [block[:, 8 * o : 8 * o + 8, :].reshape(planes * 8, rows).astype(BF16) for o in range(2)]
        octets = jnp.concatenate(octets, axis=1)
        for part in range(groups):
            data = octets[part * z_out * 8 : part * z_out * 8 + depth]
            all_e = dot(z_ref[0, :, :depth], data) + dot(z_ref[1, :, :depth], data)
            for v in range(views):
                e = all_e[v * 2 * tall : (v + 1) * 2 * tall]
                e = jnp.concatenate(
                    [
                        jnp.concatenate([e[:tall, o * rows : (o + 1) * rows], e[tall:, o * rows : (o + 1) * rows]], axis=1)
                        for o in range(2)
                    ],
                    axis=0,
                )
                if exact:
                    high, low = split(e)
                    g = dot(high, x_ref[v, 0]) + dot(high, x_ref[v, 1]) + dot(low, x_ref[v, 0])
                else:
                    high = e.astype(BF16)
                    g = dot(high, x_ref[v, 0]) + dot(high, x_ref[v, 1])
                for r in range(2):
                    lanes = slice(r * rows, (r + 1) * rows)
                    g_rows = jnp.concatenate(
                        [g[o * tall : (o + 1) * tall, lanes].reshape(z_out, 8, rows) for o in range(2)], axis=1
                    )
                    target = slice(r * rows + pair * 16, r * rows + pair * 16 + 16)
                    planes_at = slice(part * z_out, (part + 1) * z_out)
                    if exact:
                        high, low = split(g_rows)
                        g_ref[v, 0, planes_at, target, :] = high
                        g_ref[v, 1, planes_at, target, :] = low
                    else:
                        g_ref[v, 0, planes_at, target, :] = g_rows.astype(BF16)
    for v in range(views):
        for z in range(0, groups * z_out, 2):
            data = jnp.concatenate([g_ref[v, 0, z], g_ref[v, 0, z + 1]], axis=1)
            out = dot(y_ref[v, 0], data) + dot(y_ref[v, 1], data)
            if exact:
                data = jnp.concatenate([g_ref[v, 1, z], g_ref[v, 1, z + 1]], axis=1)
                out = out + dot(y_ref[v, 0], data)
            emit(v, z, out[:, :rows])
            emit(v, z + 1, out[:, rows:])


def quotient_kernel(place_ref, mine_ref, other_low_ref, other_high_ref, own_ref, rec_ref, z_ref, x_ref, y_ref, own_out, rim_out, g_ref):
    planes = own_ref.shape[0]
    margin = rim_out.shape[2]
    first_core = place_ref[0] % 2 == 0

    def load(at):
        mine = mine_ref[:, at, :].astype(F32)
        other = jnp.concatenate([ref[:, at, :].astype(F32) for ref in (other_low_ref, other_high_ref)], axis=0)
        before, after = jnp.where(first_core, mine, other), jnp.where(first_core, other, mine)
        return jnp.concatenate([before, own_ref[:, at, :], after], axis=0)

    def emit(v, z, blurred):
        if z < margin:
            rim_out[v, 0, z] = blurred
        elif z < margin + planes:
            own_out[v, z - margin] = (rec_ref[v, z - margin].astype(F32) / blurred).astype(BF16)
        else:
            rim_out[v, 1, z - margin - planes] = blurred

    groups = (planes + 2 * margin) // (planes // 2)
    filter_to(load, rec_ref.shape[0], groups, z_ref.at[0], x_ref.at[0], y_ref.at[0], g_ref, False, emit)


def correction(v, before_ref, own_ref, after_ref, rim_ref, z_ref, x_ref, y_ref, g_ref, emit):
    def load(at):
        before = before_ref[v, :, at, :].astype(F32) / rim_ref[v, 0, :, at, :]
        after = after_ref[v, :, at, :].astype(F32) / rim_ref[v, 1, :, at, :]
        return jnp.concatenate([before, own_ref[v, :, at, :].astype(F32), after], axis=0)

    tall = z_ref.shape[2] // own_ref.shape[0]
    filter_to(
        load,
        1,
        2,
        z_ref.at[1, :, v * tall : (v + 1) * tall],
        x_ref.at[1, v : v + 1],
        y_ref.at[1, v : v + 1],
        g_ref,
        True,
        emit,
    )


def first_correction_kernel(v, before_ref, own_ref, after_ref, rim_ref, z_ref, x_ref, y_ref, out_ref, g_ref):
    def emit(_, z, value):
        out_ref[z] = value

    correction(v, before_ref, own_ref, after_ref, rim_ref, z_ref, x_ref, y_ref, g_ref, emit)


def last_correction_kernel(
    v, before_ref, own_ref, after_ref, rim_ref, earlier_ref, z_ref, x_ref, y_ref, keep_ref, send_ref, g_ref
):
    part = keep_ref.shape[2]

    def emit(_, z, value):
        product = value * earlier_ref[z]
        for b in range(4):
            rows = product[b * part : (b + 1) * part]
            if b % 2 == 0:
                keep_ref[b // 2, z] = rows
            else:
                send_ref[b // 2, z] = rows

    correction(v, before_ref, own_ref, after_ref, rim_ref, z_ref, x_ref, y_ref, g_ref, emit)


def local(estimate, recordings, psf_taps):
    planes, rows, cols = estimate.shape
    taps = psf_taps.shape[-1]
    margin = (taps - 1) // 2
    views = recordings.shape[0]
    devices = lax.axis_size("gz")
    place = lax.axis_index("view")
    place_array = place.reshape(1).astype(jnp.int32)
    up = [(i, i + 1) for i in range(devices - 1)]
    down = [(i + 1, i) for i in range(devices - 1)]
    swap = [(i, i ^ 1) for i in range(4)]
    z_out = planes // 2

    both_ways = [(4 * i + w, 4 * j + w) for w in (0, 2) for i, j in up]
    both_ways += [(4 * i + w, 4 * j + w) for w in (1, 3) for i, j in down]
    mine = lax.ppermute(estimate.astype(BF16), ("gz", "view"), both_ways)
    shape = jax.ShapeDtypeStruct
    wide = -(-(z_out + taps - 1) * 8 // 128) * 128
    z_mat, x_mat, y_mat = pl.pallas_call(
        matrices_kernel,
        out_shape=[
            shape((2, 2, views * 2 * z_out * 8, wide), BF16),
            shape((2, views, 2, 2 * cols, 2 * cols), BF16),
            shape((2, views, 2, rows, 2 * rows), BF16),
        ],
        in_specs=[SMEM, SMEM],
        out_specs=[VMEM] * 3,
        name="matrices",
        **params(10**6, 10**4),
    )(place_array, psf_taps)

    before = lax.ppermute(recordings[:, planes - margin :], "gz", up)
    after = lax.ppermute(recordings[:, :margin], "gz", down)
    mine, z_mat = lax.optimization_barrier((mine, z_mat))
    other = [lax.ppermute(part, "view", swap) for part in (mine[:margin], mine[margin:])]

    own, rim = pl.pallas_call(
        quotient_kernel,
        out_shape=[shape((views, planes, rows, cols), BF16), shape((views, 2, margin, rows, cols), F32)],
        in_specs=[SMEM] + [VMEM] * 8,
        out_specs=[VMEM] * 2,
        scratch_shapes=[pltpu.VMEM((views, 1, planes + 2 * margin, 2 * rows, cols), BF16)],
        name="quotients",
        **params(10**6, 10**4),
    )(place_array, mine, *other, estimate, recordings, z_mat, x_mat, y_mat)
    product = pl.pallas_call(
        lambda *refs: first_correction_kernel(0, *refs),
        out_shape=shape((planes, rows, cols), F32),
        in_specs=[VMEM] * 7,
        out_specs=VMEM,
        scratch_shapes=[pltpu.VMEM((1, 2, planes, 2 * rows, cols), BF16)],
        name="correction",
        **params(4 * 10**9, 5 * 10**6),
    )(before, own, after, rim, z_mat, x_mat, y_mat)
    part = rows // 4
    keep, send = pl.pallas_call(
        lambda *refs: last_correction_kernel(1, *refs),
        out_shape=[shape((2, planes, part, cols), F32)] * 2,
        in_specs=[VMEM] * 8,
        out_specs=[VMEM] * 2,
        scratch_shapes=[pltpu.VMEM((1, 2, planes, 2 * rows, cols), BF16)],
        name="corrections",
        **params(4 * 10**9, 5 * 10**6),
    )(before, own, after, rim, product, z_mat, x_mat, y_mat)
    core = lax.ppermute(send, "view", swap)
    across = lax.ppermute(keep[1] * core[1], "view", [(i, i ^ 2) for i in range(4)])
    mine = lax.dynamic_slice_in_dim(estimate, place * part, part, 1)
    return mine * (keep[0] * core[0]) * across


def solution(mesh):
    in_specs = (P("gz", None, None), P("view", "gz", None, None), P("view", None, None, None))
    out_specs = P("gz", "view", None)
    return jax.shard_map(local, mesh=mesh, in_specs=in_specs, out_specs=out_specs, check_vma=False)
```

```python
import jax
import jax.numpy as jnp
from jax import lax
from jax.experimental import pallas as pl
from jax.experimental.pallas import tpu as pltpu
from jax.sharding import PartitionSpec as P

F32 = jnp.float32
BF16 = jnp.bfloat16
VMEM = pl.BlockSpec(memory_space=pltpu.VMEM)
SMEM = pl.BlockSpec(memory_space=pltpu.SMEM)
LIMIT = 48 * 1024 * 1024


def split(value):
    high = value.astype(BF16)
    return high, (value - high.astype(F32)).astype(BF16)


def params(flops, nbytes):
    return dict(
        compiler_params=pltpu.CompilerParams(vmem_limit_bytes=LIMIT),
        cost_estimate=pl.CostEstimate(flops=flops, bytes_accessed=nbytes, transcendentals=0),
    )


def matrices_kernel(place_ref, taps_ref, z_ref, x_ref, y_ref):
    views, taps = taps_ref.shape[0], taps_ref.shape[3]
    half = (taps - 1) // 2
    rows = x_ref.shape[3] // 2
    place = place_ref[0]
    zeros = jnp.zeros((rows, rows), BF16)

    def inverse(values):
        total = values[0]
        for value in values[1:]:
            total = total + value
        return total

    for v in range(views):
        tap = {
            (d, r): [taps_ref[v, d, r, j] for j in range(taps)] for d in range(3) for r in range(2)
        }
        scale = {}
        for r in range(2):
            for d in range(2):
                scale[d, r] = 1.0 / jnp.full((8, 128), inverse(tap[d, r]), F32)[0:1]
            scale[2, r] = 1.0 / jnp.full((8, 128), inverse(tap[2, 0] + tap[2, 1]), F32)[0:1]
        for direction in range(2):
            for part in range(2):
                for r in range(2):
                    other = 1 - r
                    x_ref[direction, v, part, r * rows : (r + 1) * rows, other * rows : (other + 1) * rows] = zeros
        step = 32
        for first in range(0, rows, step):
            diff = (
                lax.broadcasted_iota(jnp.int32, (step, rows), 0)
                - lax.broadcasted_iota(jnp.int32, (step, rows), 1)
                + (first + half)
            )
            made = {(d, r, m): jnp.zeros((step, rows), F32) for d in range(2) for r in range(2) for m in range(2)}
            for j in range(taps):
                here = diff == j
                for d, r, m in made:
                    pick = tap[d, r][j] if m == 0 else tap[d, r][taps - 1 - j]
                    made[d, r, m] = jnp.where(here, pick, made[d, r, m])
            for (d, r, m), value in made.items():
                parts = split(value * scale[d, r])
                for part in range(2):
                    lanes = slice(r * rows, (r + 1) * rows)
                    if d == 0:
                        x_ref[m, v, part, r * rows + first : r * rows + first + step, lanes] = parts[part]
                    elif m == 1:
                        y_ref[0, v, part, first : first + step, lanes] = parts[part]
                    else:
                        target = pl.multiple_of(jnp.bitwise_xor(first // step, place) * step, step)
                        y_ref[1, v, part, pl.ds(target, step), lanes] = parts[part]
        tall = z_ref.shape[2] // (2 * views)
        wide = z_ref.shape[3]
        step = 16
        for first in range(0, tall, step):
            diff = (
                lax.broadcasted_iota(jnp.int32, (step, wide), 1)
                - lax.broadcasted_iota(jnp.int32, (step, wide), 0)
                - first
            )
            made = {(r, m): jnp.zeros((step, wide), F32) for r in range(2) for m in range(2)}
            for j in range(taps):
                here = diff == 8 * j
                for r, m in made:
                    pick = tap[2, r][j] if m == 0 else tap[2, r][taps - 1 - j]
                    made[r, m] = jnp.where(here, pick, made[r, m])
            for (r, m), value in made.items():
                parts = split(value * scale[2, r][0:1, 0:1])
                for part in range(2):
                    top = (2 * v + r) * tall + first
                    z_ref[m, part, top : top + step, :] = parts[part]


def dot(a, b):
    return jnp.dot(a, b, preferred_element_type=F32)


STACK_Z, STACK_Y, CHUNK = True, True, 4


def inverted(value):
    guess = pl.reciprocal(value, approx=True)
    return guess * (2.0 - value * guess)


def both_halves(ref, depth, data, stacked):
    if stacked:
        rows = ref.shape[1]
        out = dot(ref[:, :, :depth].reshape(2 * rows, depth), data)
        return out[:rows] + out[rows:]
    return dot(ref[0, :, :depth], data) + dot(ref[1, :, :depth], data)


def filter_to(load, views, groups, z_ref, x_ref, y_ref, e_ref, g_ref, exact, emit):
    tall = z_ref.shape[1] // (2 * views)
    z_out = tall // 8
    rows = y_ref.shape[2]
    for pair in range(rows // 16):
        block = load(slice(pair * 16, pair * 16 + 16))
        planes = block.shape[0]
        depth = (planes - (groups - 1) * z_out) * 8
        octets = [block[:, 8 * o : 8 * o + 8, :].reshape(planes * 8, rows).astype(BF16) for o in range(2)]
        octets = jnp.concatenate(octets, axis=1)
        for part in range(groups):
            data = octets[part * z_out * 8 : part * z_out * 8 + depth]
            all_e = both_halves(z_ref, depth, data, STACK_Z)
            for v in range(views):
                for r in range(2):
                    top = (2 * v + r) * tall
                    e = all_e[top : top + tall]
                    e = jnp.concatenate([e[:, :rows], e[:, rows:]], axis=0)
                    lanes = slice(r * rows, (r + 1) * rows)
                    if exact:
                        high, low = split(e)
                        e_ref[v, 0, pair * groups + part, :, lanes] = high
                        e_ref[v, 1, pair * groups + part, :, lanes] = low
                    else:
                        e_ref[v, 0, pair * groups + part, :, lanes] = e.astype(BF16)
    for v in range(views):
        for first in range(0, rows // 16 * groups, CHUNK):
            e = e_ref[v, 0, first : first + CHUNK].reshape(CHUNK * 2 * tall, 2 * rows)
            all_g = dot(e, x_ref[v, 0]) + dot(e, x_ref[v, 1])
            if exact:
                e = e_ref[v, 1, first : first + CHUNK].reshape(CHUNK * 2 * tall, 2 * rows)
                all_g = all_g + dot(e, x_ref[v, 0])
            for index in range(first, first + CHUNK):
                pair, part = index // groups, index % groups
                g = all_g[(index - first) * 2 * tall : (index - first + 1) * 2 * tall]
                for r in range(2):
                    lanes = slice(r * rows, (r + 1) * rows)
                    g_rows = jnp.concatenate(
                        [g[o * tall : (o + 1) * tall, lanes].reshape(z_out, 8, rows) for o in range(2)], axis=1
                    )
                    target = slice(r * rows + pair * 16, r * rows + pair * 16 + 16)
                    planes_at = slice(part * z_out, (part + 1) * z_out)
                    if exact:
                        high, low = split(g_rows)
                        g_ref[v, 0, planes_at, target, :] = high
                        g_ref[v, 1, planes_at, target, :] = low
                    else:
                        g_ref[v, 0, planes_at, target, :] = g_rows.astype(BF16)
    for v in range(views):
        for z in range(0, groups * z_out, 2):
            data = jnp.concatenate([g_ref[v, 0, z], g_ref[v, 0, z + 1]], axis=1)
            out = both_halves(y_ref.at[v], 2 * rows, data, STACK_Y)
            if exact:
                data = jnp.concatenate([g_ref[v, 1, z], g_ref[v, 1, z + 1]], axis=1)
                out = out + dot(y_ref[v, 0], data)
            emit(v, z, out[:, :rows])
            emit(v, z + 1, out[:, rows:])


def scratch(views, groups, halves, z_out, rows, cols):
    return [
        pltpu.VMEM((views, halves, rows // 16 * groups, 2 * z_out * 8, 2 * cols), BF16),
        pltpu.VMEM((views, halves, groups * z_out, 2 * rows, cols), BF16),
    ]


def prepare_kernel(est_ref, rec_ref, est_out, last_out, first_out):
    margin = last_out.shape[1]
    planes = est_ref.shape[0]
    est_out[...] = est_ref[...].astype(BF16)
    last_out[...] = rec_ref[:, planes - margin :]
    first_out[...] = rec_ref[:, :margin]


def quotient_kernel(
    place_ref, mine_ref, other_low_ref, other_high_ref, own_ref, rec_ref, z_ref, x_ref, y_ref, own_out, rim_out, e_ref, g_ref
):
    planes = own_ref.shape[0]
    margin = rim_out.shape[2]
    first_core = place_ref[0] % 2 == 0

    def load(at):
        mine = mine_ref[:, at, :].astype(F32)
        other = jnp.concatenate([ref[:, at, :].astype(F32) for ref in (other_low_ref, other_high_ref)], axis=0)
        before, after = jnp.where(first_core, mine, other), jnp.where(first_core, other, mine)
        return jnp.concatenate([before, own_ref[:, at, :].astype(F32), after], axis=0)

    def emit(v, z, blurred):
        inverse = inverted(blurred)
        if z < margin:
            rim_out[v, 0, z] = inverse
        elif z < margin + planes:
            own_out[v, z - margin] = (rec_ref[v, z - margin].astype(F32) * inverse).astype(BF16)
        else:
            rim_out[v, 1, z - margin - planes] = inverse

    groups = (planes + 2 * margin) // (planes // 2)
    filter_to(load, rec_ref.shape[0], groups, z_ref.at[0], x_ref.at[0], y_ref.at[0], e_ref, g_ref, False, emit)


def correction_kernel(before_ref, own_ref, after_ref, rim_ref, z_ref, x_ref, y_ref, keep_ref, send_ref, e_ref, g_ref, earlier_ref):
    views = own_ref.shape[0]
    part = keep_ref.shape[2]
    tall = z_ref.shape[2] // views
    for v in range(views):

        def load(at, v=v):
            before = before_ref[v, :, at, :].astype(F32) * rim_ref[v, 0, :, at, :]
            after = after_ref[v, :, at, :].astype(F32) * rim_ref[v, 1, :, at, :]
            return jnp.concatenate([before, own_ref[v, :, at, :].astype(F32), after], axis=0)

        def emit(_, z, value, v=v):
            if v > 0:
                value = value * earlier_ref[z]
            if v < views - 1:
                earlier_ref[z] = value
                return
            for b in range(4):
                rows = value[b * part : (b + 1) * part]
                if b % 2 == 0:
                    keep_ref[b // 2, z] = rows
                else:
                    send_ref[b // 2, z] = rows

        z_view = z_ref.at[1, :, v * tall : (v + 1) * tall]
        filter_to(load, 1, 2, z_view, x_ref.at[1, v : v + 1], y_ref.at[1, v : v + 1], e_ref, g_ref, True, emit)


def local(estimate, recordings, psf_taps):
    planes, rows, cols = estimate.shape
    taps = psf_taps.shape[-1]
    margin = (taps - 1) // 2
    views = recordings.shape[0]
    devices = lax.axis_size("gz")
    place = lax.axis_index("view")
    place_array = place.reshape(1).astype(jnp.int32)
    up = [(i, i + 1) for i in range(devices - 1)]
    down = [(i + 1, i) for i in range(devices - 1)]
    swap = [(i, i ^ 1) for i in range(4)]
    z_out = planes // 2
    shape = jax.ShapeDtypeStruct

    rounded, last, first = pl.pallas_call(
        prepare_kernel,
        out_shape=[shape((planes, rows, cols), BF16)] + [shape((views, margin, rows, cols), BF16)] * 2,
        in_specs=[VMEM] * 2,
        out_specs=[VMEM] * 3,
        name="prepare",
        **params(10**6, 10**4),
    )(estimate, recordings)
    both_ways = [(4 * i + w, 4 * j + w) for w in (0, 2) for i, j in up]
    both_ways += [(4 * i + w, 4 * j + w) for w in (1, 3) for i, j in down]
    mine = lax.ppermute(rounded, ("gz", "view"), both_ways)

    wide = -(-(z_out + taps - 1) * 8 // 128) * 128
    z_mat, x_mat, y_mat = pl.pallas_call(
        matrices_kernel,
        out_shape=[
            shape((2, 2, views * 2 * z_out * 8, wide), BF16),
            shape((2, views, 2, 2 * cols, 2 * cols), BF16),
            shape((2, views, 2, rows, 2 * rows), BF16),
        ],
        in_specs=[SMEM, SMEM],
        out_specs=[VMEM] * 3,
        name="matrices",
        **params(10**6, 10**4),
    )(place_array, psf_taps)

    before = lax.ppermute(last, "gz", up)
    after = lax.ppermute(first, "gz", down)
    mine, z_mat = lax.optimization_barrier((mine, z_mat))
    other = [lax.ppermute(part, "view", swap) for part in (mine[:margin], mine[margin:])]

    own, rim = pl.pallas_call(
        quotient_kernel,
        out_shape=[shape((views, planes, rows, cols), BF16), shape((views, 2, margin, rows, cols), F32)],
        in_specs=[SMEM] + [VMEM] * 8,
        out_specs=[VMEM] * 2,
        scratch_shapes=scratch(views, 4, 1, z_out, rows, cols),
        name="quotients",
        **params(10**6, 10**4),
    )(place_array, mine, *other, rounded, recordings, z_mat, x_mat, y_mat)
    part = rows // 4
    keep, send = pl.pallas_call(
        correction_kernel,
        out_shape=[shape((2, planes, part, cols), F32)] * 2,
        in_specs=[VMEM] * 7,
        out_specs=[VMEM] * 2,
        scratch_shapes=scratch(1, 2, 2, z_out, rows, cols) + [pltpu.VMEM((planes, rows, cols), F32)],
        name="corrections",
        **params(4 * 10**9, 5 * 10**6),
    )(before, own, after, rim, z_mat, x_mat, y_mat)
    core = lax.ppermute(send, "view", swap)
    product = keep[1] * core[1]
    most = jnp.maximum(jnp.max(product), 1e-30)
    exponent = jnp.floor(jnp.log2(most)) - 14.0
    coded = (product * jnp.exp2(-exponent)).astype(jnp.float16)
    tail = jnp.broadcast_to(exponent.astype(jnp.float16), (1, part, cols))
    across = lax.ppermute(jnp.concatenate([coded, tail]), "view", [(i, i ^ 2) for i in range(4)]).astype(F32)
    mine = lax.dynamic_slice_in_dim(estimate, place * part, part, 1)
    return mine * (keep[0] * core[0]) * (across[:planes] * jnp.exp2(across[planes:, :1, :1]))


def solution(mesh):
    in_specs = (P("gz", None, None), P("view", "gz", None, None), P("view", None, None, None))
    out_specs = P("gz", "view", None)
    return jax.shard_map(local, mesh=mesh, in_specs=in_specs, out_specs=out_specs, check_vma=False)
```

```python
import jax
import jax.numpy as jnp
from jax import lax
from jax.experimental import pallas as pl
from jax.experimental.pallas import tpu as pltpu
from jax.sharding import PartitionSpec as P

F32 = jnp.float32
BF16 = jnp.bfloat16
VMEM = pl.BlockSpec(memory_space=pltpu.VMEM)
HBM = pl.BlockSpec(memory_space=pltpu.HBM)
SMEM = pl.BlockSpec(memory_space=pltpu.SMEM)
LIMIT = 48 * 1024 * 1024


def split(value):
    high = value.astype(BF16)
    return high, (value - high.astype(F32)).astype(BF16)


def params(flops, nbytes, limit=LIMIT):
    return dict(
        compiler_params=pltpu.CompilerParams(vmem_limit_bytes=limit),
        cost_estimate=pl.CostEstimate(flops=flops, bytes_accessed=nbytes, transcendentals=0),
    )


def rounded_scale(tap, total):
    factor = jnp.exp2(lax.broadcasted_iota(jnp.int32, (1, 128), 1).astype(F32) * (1.0 / 128.0))
    scale = factor / jnp.full((1, 128), total, F32)
    sums, running = [], jnp.zeros((1, 128), F32)
    for value in tap:
        exact = value * scale
        running = running + (exact.astype(BF16).astype(F32) - exact)
        sums.append(running)
    error = jnp.zeros((1, 128), F32)
    for partial in sums:
        rest = running - partial
        error = error + partial * partial + rest * rest
    error = error / (factor * factor)
    best = error == jnp.min(error, axis=1, keepdims=True)
    factor = jnp.max(jnp.where(best, factor, 0.0), axis=1, keepdims=True)
    scale = jnp.max(jnp.where(best, scale, 0.0), axis=1, keepdims=True)
    return jnp.broadcast_to(scale, (1, 128)), jnp.broadcast_to(factor, (1, 128))


def matrices_kernel(place_ref, taps_ref, rec_ref, z_ref, x_ref, y_ref, scale_ref, last_out, first_out, sems):
    views, taps = taps_ref.shape[0], taps_ref.shape[3]
    margin = last_out.shape[1]
    copies = []
    for v in range(views):
        for out, begin in ((last_out, rec_ref.shape[1] - margin), (first_out, 0)):
            copies.append(
                pltpu.make_async_copy(rec_ref.at[v, pl.ds(begin, margin)], out.at[v], sems.at[len(copies)])
            )
    for copy in copies:
        copy.start()
    half = (taps - 1) // 2
    rows = x_ref.shape[2] // 2
    place = place_ref[0]
    zeros = jnp.zeros((rows, rows), BF16)

    for v in range(views):
        tap = {
            (d, r): [taps_ref[v, d, r, j] for j in range(taps)] for d in range(3) for r in range(2)
        }
        scale = {}
        for r in range(2):
            undo = jnp.ones((1, 128), F32)
            for d in range(3):
                values = tap[d, r] if d < 2 else tap[2, 0] + tap[2, 1]
                total = values[0]
                for value in values[1:]:
                    total = total + value
                scale[d, r], factor = rounded_scale(tap[d, r], total)
                undo = undo / factor
            scale_ref[v, r] = undo
        for direction in range(2):
            for r in range(2):
                other = 1 - r
                x_ref[direction, v, r * rows : (r + 1) * rows, other * rows : (other + 1) * rows] = zeros
        step = 32
        for first in range(0, rows, step):
            diff = (
                lax.broadcasted_iota(jnp.int32, (step, rows), 0)
                - lax.broadcasted_iota(jnp.int32, (step, rows), 1)
                + (first + half)
            )
            made = {(d, r, m): jnp.zeros((step, rows), F32) for d in range(2) for r in range(2) for m in range(2)}
            for j in range(taps):
                here = diff == j
                for d, r, m in made:
                    pick = tap[d, r][j] if m == 0 else tap[d, r][taps - 1 - j]
                    made[d, r, m] = jnp.where(here, pick, made[d, r, m])
            for (d, r, m), value in made.items():
                value = (value * scale[d, r]).astype(BF16)
                lanes = slice(r * rows, (r + 1) * rows)
                if d == 0:
                    x_ref[m, v, r * rows + first : r * rows + first + step, lanes] = value
                elif m == 1:
                    y_ref[0, v, first : first + step, lanes] = value
                else:
                    target = pl.multiple_of(jnp.bitwise_xor(first // step, place) * step, step)
                    y_ref[1, v, pl.ds(target, step), lanes] = value
        tall = z_ref.shape[1] // (2 * views)
        wide = z_ref.shape[2]
        step = 16
        for first in range(0, tall, step):
            diff = (
                lax.broadcasted_iota(jnp.int32, (step, wide), 1)
                - lax.broadcasted_iota(jnp.int32, (step, wide), 0)
                - first
            )
            made = {(r, m): jnp.zeros((step, wide), F32) for r in range(2) for m in range(2)}
            for j in range(taps):
                here = diff == 8 * j
                for r, m in made:
                    pick = tap[2, r][j] if m == 0 else tap[2, r][taps - 1 - j]
                    made[r, m] = jnp.where(here, pick, made[r, m])
            for (r, m), value in made.items():
                top = (2 * v + r) * tall + first
                z_ref[m, top : top + step, :] = (value * scale[2, r][0:1, 0:1]).astype(BF16)
    for copy in copies:
        copy.wait()


def dot(a, b):
    return jnp.dot(a, b, preferred_element_type=F32)


CHUNK = 4


def inverted(value):
    guess = pl.reciprocal(value, approx=True)
    return guess * (2.0 - value * guess)


def filter_to(load, views, groups, z_ref, x_ref, y_ref, scale_ref, e_ref, g_ref, exact, emit):
    tall = z_ref.shape[0] // (2 * views)
    z_out = tall // 8
    rows = y_ref.shape[1]
    for pair in range(rows // 16):
        block = load(slice(pair * 16, pair * 16 + 16))
        planes = block.shape[0]
        depth = (planes - (groups - 1) * z_out) * 8
        octets = [block[:, 8 * o : 8 * o + 8, :].reshape(planes * 8, rows).astype(BF16) for o in range(2)]
        octets = jnp.concatenate(octets, axis=1)
        for part in range(groups):
            data = octets[part * z_out * 8 : part * z_out * 8 + depth]
            all_e = dot(z_ref[:, :depth], data)
            for v in range(views):
                for r in range(2):
                    top = (2 * v + r) * tall
                    e = all_e[top : top + tall]
                    e = jnp.concatenate([e[:, :rows], e[:, rows:]], axis=0)
                    lanes = slice(r * rows, (r + 1) * rows)
                    if exact:
                        high, low = split(e)
                        e_ref[v, 0, pair * groups + part, :, lanes] = high
                        e_ref[v, 1, pair * groups + part, :, lanes] = low
                    else:
                        e_ref[v, 0, pair * groups + part, :, lanes] = e.astype(BF16)
    for v in range(views):
        for first in range(0, rows // 16 * groups, CHUNK):
            e = e_ref[v, 0, first : first + CHUNK].reshape(CHUNK * 2 * tall, 2 * rows)
            all_g = dot(e, x_ref[v])
            if exact:
                e = e_ref[v, 1, first : first + CHUNK].reshape(CHUNK * 2 * tall, 2 * rows)
                all_g = all_g + dot(e, x_ref[v])
            for index in range(first, first + CHUNK):
                pair, part = index // groups, index % groups
                g = all_g[(index - first) * 2 * tall : (index - first + 1) * 2 * tall]
                for r in range(2):
                    lanes = slice(r * rows, (r + 1) * rows)
                    g_rows = jnp.concatenate(
                        [g[o * tall : (o + 1) * tall, lanes].reshape(z_out, 8, rows) for o in range(2)], axis=1
                    )
                    g_rows = g_rows * scale_ref[v, r]
                    target = slice(r * rows + pair * 16, r * rows + pair * 16 + 16)
                    planes_at = slice(part * z_out, (part + 1) * z_out)
                    if exact:
                        high, low = split(g_rows)
                        g_ref[v, 0, planes_at, target, :] = high
                        g_ref[v, 1, planes_at, target, :] = low
                    else:
                        g_ref[v, 0, planes_at, target, :] = g_rows.astype(BF16)
    for v in range(views):
        for z in range(0, groups * z_out, 2):
            data = jnp.concatenate([g_ref[v, 0, z], g_ref[v, 0, z + 1]], axis=1)
            out = dot(y_ref[v], data)
            if exact:
                data = jnp.concatenate([g_ref[v, 1, z], g_ref[v, 1, z + 1]], axis=1)
                out = out + dot(y_ref[v], data)
            emit(v, z, out[:, :rows])
            emit(v, z + 1, out[:, rows:])


def scratch(views, groups, halves, z_out, rows, cols):
    return [
        pltpu.VMEM((views, halves, rows // 16 * groups, 2 * z_out * 8, 2 * cols), BF16),
        pltpu.VMEM((views, halves, groups * z_out, 2 * rows, cols), BF16),
    ]


def quotient_kernel(
    place_ref, mine_ref, other_ref, own_ref, rec_ref, z_ref, x_ref, y_ref, scale_ref, own_out, rim_out, e_ref, g_ref
):
    planes = own_ref.shape[0]
    margin = rim_out.shape[2]
    first_core = place_ref[0] % 2 == 0

    def load(at):
        mine = mine_ref[:, at, :].astype(F32)
        other = other_ref[:, at, :].astype(F32)
        before, after = jnp.where(first_core, mine, other), jnp.where(first_core, other, mine)
        return jnp.concatenate([before, own_ref[:, at, :].astype(F32), after], axis=0)

    def emit(v, z, blurred):
        inverse = inverted(blurred)
        if z < margin:
            rim_out[v, 0, z] = inverse
        elif z < margin + planes:
            own_out[v, z - margin] = (rec_ref[v, z - margin].astype(F32) * inverse).astype(BF16)
        else:
            rim_out[v, 1, z - margin - planes] = inverse

    groups = (planes + 2 * margin) // (planes // 2)
    filter_to(load, rec_ref.shape[0], groups, z_ref.at[0], x_ref.at[0], y_ref.at[0], scale_ref, e_ref, g_ref, False, emit)


def correction_kernel(before_ref, own_ref, after_ref, rim_ref, z_ref, x_ref, y_ref, scale_ref, keep_ref, send_ref, e_ref, g_ref, earlier_ref):
    views = own_ref.shape[0]
    part = keep_ref.shape[2]
    tall = z_ref.shape[1] // views
    for v in range(views):

        def load(at, v=v):
            before = before_ref[v, :, at, :].astype(F32) * rim_ref[v, 0, :, at, :]
            after = after_ref[v, :, at, :].astype(F32) * rim_ref[v, 1, :, at, :]
            return jnp.concatenate([before, own_ref[v, :, at, :].astype(F32), after], axis=0)

        def emit(_, z, value, v=v):
            if v > 0:
                value = value * earlier_ref[z]
            if v < views - 1:
                earlier_ref[z] = value
                return
            for b in range(4):
                rows = value[b * part : (b + 1) * part]
                if b % 2 == 0:
                    keep_ref[b // 2, z] = rows
                else:
                    send_ref[b // 2, z] = rows

        z_view = z_ref.at[1, v * tall : (v + 1) * tall]
        filter_to(load, 1, 2, z_view, x_ref.at[1, v : v + 1], y_ref.at[1, v : v + 1], scale_ref.at[v : v + 1], e_ref, g_ref, True, emit)


def local(estimate, recordings, psf_taps):
    planes, rows, cols = estimate.shape
    taps = psf_taps.shape[-1]
    margin = (taps - 1) // 2
    views = recordings.shape[0]
    devices = lax.axis_size("gz")
    place = lax.axis_index("view")
    place_array = place.reshape(1).astype(jnp.int32)
    up = [(i, i + 1) for i in range(devices - 1)]
    down = [(i + 1, i) for i in range(devices - 1)]
    swap = [(i, i ^ 1) for i in range(4)]
    z_out = planes // 2
    shape = jax.ShapeDtypeStruct

    rounded = estimate.astype(BF16)
    both_ways = [(4 * i + w, 4 * j + w) for w in (0, 2) for i, j in up]
    both_ways += [(4 * i + w, 4 * j + w) for w in (1, 3) for i, j in down]
    mine = lax.ppermute(rounded, ("gz", "view"), both_ways)

    wide = -(-(z_out + taps - 1) * 8 // 128) * 128
    z_mat, x_mat, y_mat, scales, last, first = pl.pallas_call(
        matrices_kernel,
        out_shape=[
            shape((2, views * 2 * z_out * 8, wide), BF16),
            shape((2, views, 2 * cols, 2 * cols), BF16),
            shape((2, views, rows, 2 * rows), BF16),
            shape((views, 2, 1, 128), F32),
            shape((views, margin, rows, cols), BF16),
            shape((views, margin, rows, cols), BF16),
        ],
        in_specs=[SMEM, SMEM, HBM],
        out_specs=[VMEM] * 6,
        scratch_shapes=[pltpu.SemaphoreType.DMA((2 * views,))],
        name="matrices",
        **params(10**6, 10**4),
    )(place_array, psf_taps, recordings)

    before = lax.ppermute(last, "gz", up)
    after = lax.ppermute(first, "gz", down)
    mine, z_mat = lax.optimization_barrier((mine, z_mat))
    other = lax.ppermute(mine, "view", swap)

    own, rim = pl.pallas_call(
        quotient_kernel,
        out_shape=[shape((views, planes, rows, cols), BF16), shape((views, 2, margin, rows, cols), F32)],
        in_specs=[SMEM] + [VMEM] * 8,
        out_specs=[VMEM] * 2,
        scratch_shapes=scratch(views, 4, 1, z_out, rows, cols),
        name="quotients",
        **params(10**6, 10**4),
    )(place_array, mine, other, rounded, recordings, z_mat, x_mat, y_mat, scales)
    part = rows // 4
    keep, send = pl.pallas_call(
        correction_kernel,
        out_shape=[shape((2, planes, part, cols), F32)] * 2,
        in_specs=[VMEM] * 8,
        out_specs=[VMEM] * 2,
        scratch_shapes=scratch(1, 2, 2, z_out, rows, cols) + [pltpu.VMEM((planes, rows, cols), F32)],
        name="corrections",
        **params(4 * 10**9, 5 * 10**6),
    )(before, own, after, rim, z_mat, x_mat, y_mat, scales)
    core = lax.ppermute(send, "view", swap)
    product = keep[1] * core[1]
    most = jnp.maximum(jnp.max(product), 1e-30)
    exponent = jnp.floor(jnp.log2(most)) - 14.0
    coded = (product * jnp.exp2(-exponent)).astype(jnp.float16)
    tail = jnp.broadcast_to(exponent.astype(jnp.float16), (1, part, cols))
    across = lax.ppermute(jnp.concatenate([coded, tail]), "view", [(i, i ^ 2) for i in range(4)])
    own_rows = lax.dynamic_slice_in_dim(estimate, place * part, part, 1)
    partial, across = lax.optimization_barrier((own_rows * (keep[0] * core[0]), across))
    return partial * (across[:planes].astype(F32) * jnp.exp2(across[planes:].astype(F32)))


def solution(mesh):
    in_specs = (P("gz", None, None), P("view", "gz", None, None), P("view", None, None, None))
    out_specs = P("gz", "view", None)
    return jax.shard_map(local, mesh=mesh, in_specs=in_specs, out_specs=out_specs, check_vma=False)
```

```python
import jax
import jax.numpy as jnp
from jax import lax
from jax.experimental import pallas as pl
from jax.experimental.pallas import tpu as pltpu
from jax.sharding import PartitionSpec as P

F32 = jnp.float32
BF16 = jnp.bfloat16
VMEM = pl.BlockSpec(memory_space=pltpu.VMEM)
HBM = pl.BlockSpec(memory_space=pltpu.HBM)
SMEM = pl.BlockSpec(memory_space=pltpu.SMEM)
LIMIT = 20 * 1024 * 1024


def split(value):
    high = value.astype(BF16)
    return high, (value - high.astype(F32)).astype(BF16)


def params(flops, nbytes, limit=LIMIT):
    return dict(
        compiler_params=pltpu.CompilerParams(vmem_limit_bytes=limit),
        cost_estimate=pl.CostEstimate(flops=flops, bytes_accessed=nbytes, transcendentals=0),
    )


def edges_kernel(rec_ref, last_out, first_out, sems):
    margin = last_out.shape[1]
    copies = []
    for v in range(rec_ref.shape[0]):
        for out, begin in ((last_out, rec_ref.shape[1] - margin), (first_out, 0)):
            copies.append(
                pltpu.make_async_copy(rec_ref.at[v, pl.ds(begin, margin)], out.at[v], sems.at[len(copies)])
            )
    for copy in copies:
        copy.start()
    for copy in copies:
        copy.wait()


def rounded_scale(tap, total):
    factor = jnp.exp2(lax.broadcasted_iota(jnp.int32, (1, 128), 1).astype(F32) * (1.0 / 128.0))
    scale = factor / jnp.full((1, 128), total, F32)
    sums, running = [], jnp.zeros((1, 128), F32)
    for value in tap:
        exact = value * scale
        running = running + (exact.astype(BF16).astype(F32) - exact)
        sums.append(running)
    error = jnp.zeros((1, 128), F32)
    for partial in sums:
        rest = running - partial
        error = error + partial * partial + rest * rest
    error = error / (factor * factor)
    best = error == jnp.min(error, axis=1, keepdims=True)
    factor = jnp.max(jnp.where(best, factor, 0.0), axis=1, keepdims=True)
    scale = jnp.max(jnp.where(best, scale, 0.0), axis=1, keepdims=True)
    return jnp.broadcast_to(scale, (1, 128)), jnp.broadcast_to(factor, (1, 128))


def matrices_kernel(place_ref, taps_ref, z_ref, x_ref, y_ref, scale_ref):
    views, taps = taps_ref.shape[0], taps_ref.shape[3]
    half = (taps - 1) // 2
    rows = x_ref.shape[2] // 2
    place = place_ref[0]
    zeros = jnp.zeros((rows, rows), BF16)

    for v in range(views):
        tap = {
            (d, r): [taps_ref[v, d, r, j] for j in range(taps)] for d in range(3) for r in range(2)
        }
        scale = {}
        for r in range(2):
            undo = jnp.ones((1, 128), F32)
            for d in range(3):
                values = tap[d, r] if d < 2 else tap[2, 0] + tap[2, 1]
                total = values[0]
                for value in values[1:]:
                    total = total + value
                scale[d, r], factor = rounded_scale(tap[d, r], total)
                undo = undo / factor
            scale_ref[v, r] = undo
        for direction in range(2):
            for r in range(2):
                other = 1 - r
                x_ref[direction, v, r * rows : (r + 1) * rows, other * rows : (other + 1) * rows] = zeros
        step = 32
        for first in range(0, rows, step):
            diff = (
                lax.broadcasted_iota(jnp.int32, (step, rows), 0)
                - lax.broadcasted_iota(jnp.int32, (step, rows), 1)
                + (first + half)
            )
            made = {(d, r, m): jnp.zeros((step, rows), F32) for d in range(2) for r in range(2) for m in range(2)}
            for j in range(taps):
                here = diff == j
                for d, r, m in made:
                    pick = tap[d, r][j] if m == 0 else tap[d, r][taps - 1 - j]
                    made[d, r, m] = jnp.where(here, pick, made[d, r, m])
            for (d, r, m), value in made.items():
                value = (value * scale[d, r]).astype(BF16)
                lanes = slice(r * rows, (r + 1) * rows)
                if d == 0:
                    x_ref[m, v, r * rows + first : r * rows + first + step, lanes] = value
                elif m == 1:
                    y_ref[0, v, first : first + step, lanes] = value
                else:
                    target = pl.multiple_of(jnp.bitwise_xor(first // step, place) * step, step)
                    y_ref[1, v, pl.ds(target, step), lanes] = value
        tall = z_ref.shape[1] // (2 * views)
        wide = z_ref.shape[2]
        step = 16
        for first in range(0, tall, step):
            diff = (
                lax.broadcasted_iota(jnp.int32, (step, wide), 1)
                - lax.broadcasted_iota(jnp.int32, (step, wide), 0)
                - first
            )
            made = {(r, m): jnp.zeros((step, wide), F32) for r in range(2) for m in range(2)}
            for j in range(taps):
                here = diff == 8 * j
                for r, m in made:
                    pick = tap[2, r][j] if m == 0 else tap[2, r][taps - 1 - j]
                    made[r, m] = jnp.where(here, pick, made[r, m])
            for (r, m), value in made.items():
                top = (2 * v + r) * tall + first
                z_ref[m, top : top + step, :] = (value * scale[2, r][0:1, 0:1]).astype(BF16)


def dot(a, b):
    return jnp.dot(a, b, preferred_element_type=F32)


CHUNK = 4


def inverted(value):
    guess = pl.reciprocal(value, approx=True)
    return guess * (2.0 - value * guess)


def filter_to(load, views, groups, z_ref, x_ref, y_ref, scale_ref, e_ref, g_ref, exact, emit):
    tall = z_ref.shape[0] // (2 * views)
    z_out = tall // 8
    rows = y_ref.shape[1]
    for pair in range(rows // 16):
        block = load(slice(pair * 16, pair * 16 + 16))
        planes = block.shape[0]
        depth = (planes - (groups - 1) * z_out) * 8
        octets = [block[:, 8 * o : 8 * o + 8, :].reshape(planes * 8, rows).astype(BF16) for o in range(2)]
        octets = jnp.concatenate(octets, axis=1)
        for part in range(groups):
            data = octets[part * z_out * 8 : part * z_out * 8 + depth]
            all_e = dot(z_ref[:, :depth], data)
            for v in range(views):
                for r in range(2):
                    top = (2 * v + r) * tall
                    e = all_e[top : top + tall]
                    e = jnp.concatenate([e[:, :rows], e[:, rows:]], axis=0)
                    lanes = slice(r * rows, (r + 1) * rows)
                    if exact:
                        high, low = split(e)
                        e_ref[v, 0, pair * groups + part, :, lanes] = high
                        e_ref[v, 1, pair * groups + part, :, lanes] = low
                    else:
                        e_ref[v, 0, pair * groups + part, :, lanes] = e.astype(BF16)
    for v in range(views):
        for first in range(0, rows // 16 * groups, CHUNK):
            e = e_ref[v, 0, first : first + CHUNK].reshape(CHUNK * 2 * tall, 2 * rows)
            all_g = dot(e, x_ref[v])
            if exact:
                e = e_ref[v, 1, first : first + CHUNK].reshape(CHUNK * 2 * tall, 2 * rows)
                all_g = all_g + dot(e, x_ref[v])
            for index in range(first, first + CHUNK):
                pair, part = index // groups, index % groups
                g = all_g[(index - first) * 2 * tall : (index - first + 1) * 2 * tall]
                for r in range(2):
                    lanes = slice(r * rows, (r + 1) * rows)
                    g_rows = jnp.concatenate(
                        [g[o * tall : (o + 1) * tall, lanes].reshape(z_out, 8, rows) for o in range(2)], axis=1
                    )
                    g_rows = g_rows * scale_ref[v, r]
                    target = slice(r * rows + pair * 16, r * rows + pair * 16 + 16)
                    planes_at = slice(part * z_out, (part + 1) * z_out)
                    if exact:
                        high, low = split(g_rows)
                        g_ref[v, 0, planes_at, target, :] = high
                        g_ref[v, 1, planes_at, target, :] = low
                    else:
                        g_ref[v, 0, planes_at, target, :] = g_rows.astype(BF16)
    for v in range(views):
        for z in range(0, groups * z_out, 2):
            data = jnp.concatenate([g_ref[v, 0, z], g_ref[v, 0, z + 1]], axis=1)
            out = dot(y_ref[v], data)
            if exact:
                data = jnp.concatenate([g_ref[v, 1, z], g_ref[v, 1, z + 1]], axis=1)
                out = out + dot(y_ref[v], data)
            emit(v, z, out[:, :rows])
            emit(v, z + 1, out[:, rows:])


def scratch(views, groups, halves, z_out, rows, cols):
    return [
        pltpu.VMEM((views, halves, rows // 16 * groups, 2 * z_out * 8, 2 * cols), BF16),
        pltpu.VMEM((views, halves, groups * z_out, 2 * rows, cols), BF16),
    ]


def inverse_kernel(early, place_ref, low_ref, high_ref, own_ref, z_ref, x_ref, y_ref, scale_ref, out_ref, e_ref, g_ref):
    side_first = (place_ref[0] % 2 == 0) == early

    def load(at):
        side = jnp.concatenate([low_ref[:, at, :], high_ref[:, at, :]], axis=0).astype(F32)
        own = own_ref[:, at, :].astype(F32)
        return jnp.concatenate([jnp.where(side_first, side, own), jnp.where(side_first, own, side)], axis=0)

    def emit(v, z, blurred):
        out_ref[v, z] = inverted(blurred)

    views = out_ref.shape[0]
    filter_to(load, views, 2, z_ref.at[0], x_ref.at[0], y_ref.at[0], scale_ref, e_ref, g_ref, False, emit)


def correction_kernel(
    place_ref,
    before_ref,
    rec_ref,
    after_ref,
    early_ref,
    late_ref,
    z_ref,
    x_ref,
    y_ref,
    scale_ref,
    keep_ref,
    send_ref,
    e_ref,
    g_ref,
    product_ref,
):
    views, planes = rec_ref.shape[:2]
    part = keep_ref.shape[2]
    tall = z_ref.shape[1] // views
    early_first = place_ref[0] % 2 == 0
    most = [jnp.zeros((8, product_ref.shape[2]), F32)]
    for v in range(views):

        def load(at, v=v):
            rec = [ref[v, :, at, :].astype(F32) for ref in (before_ref, rec_ref, after_ref)]
            early, late = early_ref[v, :, at, :], late_ref[v, :, at, :]
            inverse = [jnp.where(early_first, early, late), jnp.where(early_first, late, early)]
            return jnp.concatenate(rec, axis=0) * jnp.concatenate(inverse, axis=0)

        def emit(_, z, value, v=v):
            if v > 0:
                value = value * product_ref[z]
            product_ref[z] = value
            if v == views - 1:
                for top in range(0, value.shape[0], 8):
                    most[0] = jnp.maximum(most[0], value[top : top + 8])

        z_view = z_ref.at[1, v * tall : (v + 1) * tall]
        filter_to(
            load,
            1,
            2,
            z_view,
            x_ref.at[1, v : v + 1],
            y_ref.at[1, v : v + 1],
            scale_ref.at[v : v + 1],
            e_ref,
            g_ref,
            True,
            emit,
        )
    top = jnp.maximum(jnp.max(most[0], axis=(0, 1), keepdims=True), 1e-30)
    quarter = jnp.ceil(jnp.log2(top) * 0.25)
    scale = jnp.exp2(-4.0 * quarter)
    root = jnp.broadcast_to(jnp.exp2(quarter), (part, product_ref.shape[2]))
    for z in range(planes):
        value = product_ref[z] * scale
        for b in range(4):
            (keep_ref, send_ref)[b % 2][b // 2, z] = value[b * part : (b + 1) * part]
    for ref in (keep_ref, send_ref):
        for b in range(2):
            ref[b, planes] = root


def local(estimate, recordings, psf_taps):
    planes, rows, cols = estimate.shape
    taps = psf_taps.shape[-1]
    margin = (taps - 1) // 2
    views = recordings.shape[0]
    devices = lax.axis_size("gz")
    place = lax.axis_index("view")
    place_array = place.reshape(1).astype(jnp.int32)
    up = [(i, i + 1) for i in range(devices - 1)]
    down = [(i + 1, i) for i in range(devices - 1)]
    swap = [(i, i ^ 1) for i in range(4)]
    z_out = planes // 2
    shape = jax.ShapeDtypeStruct

    rounded = estimate.astype(BF16)
    both_ways = [(4 * i + w, 4 * j + w) for w in (0, 2) for i, j in up]
    both_ways += [(4 * i + w, 4 * j + w) for w in (1, 3) for i, j in down]
    mine = lax.ppermute(rounded, ("gz", "view"), both_ways)

    last, first = pl.pallas_call(
        edges_kernel,
        out_shape=[shape((views, margin, rows, cols), BF16)] * 2,
        in_specs=[HBM],
        out_specs=[VMEM] * 2,
        scratch_shapes=[pltpu.SemaphoreType.DMA((2 * views,))],
        name="edges",
        **params(10**4, 10**4),
    )(recordings)
    before = lax.ppermute(last, "gz", up)
    after = lax.ppermute(first, "gz", down)

    wide = -(-(z_out + taps - 1) * 8 // 128) * 128
    z_mat, x_mat, y_mat, scales = pl.pallas_call(
        matrices_kernel,
        out_shape=[
            shape((2, views * 2 * z_out * 8, wide), BF16),
            shape((2, views, 2 * cols, 2 * cols), BF16),
            shape((2, views, rows, 2 * rows), BF16),
            shape((views, 2, 1, 128), F32),
        ],
        in_specs=[SMEM, SMEM],
        out_specs=[VMEM] * 4,
        name="matrices",
        **params(10**6, 10**4),
    )(place_array, psf_taps)

    mine, z_mat = lax.optimization_barrier((mine, z_mat))
    mine = (mine[:margin], mine[margin:])
    other = [lax.ppermute(piece, "view", swap) for piece in mine]
    inverses = []
    for early, side in ((True, mine), (False, other)):
        inverses.append(
            pl.pallas_call(
                lambda *refs, early=early: inverse_kernel(early, *refs),
                out_shape=shape((views, planes, rows, cols), F32),
                in_specs=[SMEM] + [VMEM] * 7,
                out_specs=VMEM,
                scratch_shapes=scratch(views, 2, 1, z_out, rows, cols),
                name="inverses",
                **params(10**6, 10**4),
            )(place_array, *side, rounded, z_mat, x_mat, y_mat, scales)
        )
    part = rows // 4
    keep, send = pl.pallas_call(
        correction_kernel,
        out_shape=[shape((2, planes + 1, part, cols), F32)] * 2,
        in_specs=[SMEM] + [VMEM] * 9,
        out_specs=[VMEM] * 2,
        scratch_shapes=scratch(1, 2, 2, z_out, rows, cols) + [pltpu.VMEM((planes, rows, cols), F32)],
        name="corrections",
        **params(4 * 10**9, 5 * 10**6),
    )(place_array, before, recordings, after, *inverses, z_mat, x_mat, y_mat, scales)
    core = lax.ppermute(send, "view", swap)
    across = lax.ppermute((keep[1] * core[1]).astype(jnp.float16), "view", [(i, i ^ 2) for i in range(4)])
    own_rows = lax.dynamic_slice_in_dim(estimate, place * part, part, 1)
    root = keep[0, planes] * core[0, planes]
    partial = own_rows * (keep[0, :planes] * core[0, :planes])
    partial, root, across = lax.optimization_barrier((partial, root, across))
    root = root * across[planes].astype(F32)
    return partial * (across[:planes].astype(F32) * (root * root * root * root))


def solution(mesh):
    in_specs = (P("gz", None, None), P("view", "gz", None, None), P("view", None, None, None))
    out_specs = P("gz", "view", None)
    return jax.shard_map(local, mesh=mesh, in_specs=in_specs, out_specs=out_specs, check_vma=False)
```

```python
import jax
import jax.numpy as jnp
from jax import lax
from jax.experimental import pallas as pl
from jax.experimental.pallas import tpu as pltpu
from jax.sharding import PartitionSpec as P

F32 = jnp.float32
BF16 = jnp.bfloat16
VMEM = pl.BlockSpec(memory_space=pltpu.VMEM)
HBM = pl.BlockSpec(memory_space=pltpu.HBM)
SMEM = pl.BlockSpec(memory_space=pltpu.SMEM)
LIMIT = 20 * 1024 * 1024


def split(value):
    high = value.astype(BF16)
    return high, (value - high.astype(F32)).astype(BF16)


def params(flops, nbytes, limit=LIMIT):
    return dict(
        compiler_params=pltpu.CompilerParams(vmem_limit_bytes=limit),
        cost_estimate=pl.CostEstimate(flops=flops, bytes_accessed=nbytes, transcendentals=0),
    )


def edges_kernel(rec_ref, last_out, first_out, sems):
    margin = last_out.shape[1]
    copies = []
    for v in range(rec_ref.shape[0]):
        for out, begin in ((last_out, rec_ref.shape[1] - margin), (first_out, 0)):
            copies.append(
                pltpu.make_async_copy(rec_ref.at[v, pl.ds(begin, margin)], out.at[v], sems.at[len(copies)])
            )
    for copy in copies:
        copy.start()
    for copy in copies:
        copy.wait()


def prepare_kernel(est_ref, est_out, held, rounded, sems):
    pieces = sems.shape[1]
    step = est_ref.shape[0] // pieces
    at = [slice(i * step, (i + 1) * step) for i in range(pieces)]
    copies = [pltpu.make_async_copy(est_ref.at[at[i]], held.at[at[i]], sems.at[0, i]) for i in range(pieces)]
    outs = [pltpu.make_async_copy(rounded.at[at[i]], est_out.at[at[i]], sems.at[1, i]) for i in range(pieces)]
    for copy in copies:
        copy.start()
    for i in range(pieces):
        copies[i].wait()
        rounded[at[i]] = held[at[i]].astype(BF16)
        outs[i].start()
    for out in outs:
        out.wait()


def rounded_scale(tap, total):
    factor = jnp.exp2(lax.broadcasted_iota(jnp.int32, (1, 128), 1).astype(F32) * (1.0 / 128.0))
    scale = factor / jnp.full((1, 128), total, F32)
    sums, running = [], jnp.zeros((1, 128), F32)
    for value in tap:
        exact = value * scale
        running = running + (exact.astype(BF16).astype(F32) - exact)
        sums.append(running)
    error = jnp.zeros((1, 128), F32)
    for partial in sums:
        rest = running - partial
        error = error + partial * partial + rest * rest
    error = error / (factor * factor)
    best = error == jnp.min(error, axis=1, keepdims=True)
    factor = jnp.max(jnp.where(best, factor, 0.0), axis=1, keepdims=True)
    scale = jnp.max(jnp.where(best, scale, 0.0), axis=1, keepdims=True)
    return jnp.broadcast_to(scale, (1, 128)), jnp.broadcast_to(factor, (1, 128))


def matrices_kernel(place_ref, taps_ref, z_ref, x_ref, y_ref, scale_ref):
    views, taps = taps_ref.shape[0], taps_ref.shape[3]
    half = (taps - 1) // 2
    rows = x_ref.shape[2] // 2
    place = place_ref[0]
    zeros = jnp.zeros((rows, rows), BF16)

    for v in range(views):
        tap = {
            (d, r): [taps_ref[v, d, r, j] for j in range(taps)] for d in range(3) for r in range(2)
        }
        scale = {}
        for r in range(2):
            undo = jnp.ones((1, 128), F32)
            for d in range(3):
                values = tap[d, r] if d < 2 else tap[2, 0] + tap[2, 1]
                total = values[0]
                for value in values[1:]:
                    total = total + value
                scale[d, r], factor = rounded_scale(tap[d, r], total)
                undo = undo / factor
            scale_ref[v, r] = undo
        for direction in range(2):
            for r in range(2):
                other = 1 - r
                x_ref[direction, v, r * rows : (r + 1) * rows, other * rows : (other + 1) * rows] = zeros
        step = 32
        for first in range(0, rows, step):
            diff = (
                lax.broadcasted_iota(jnp.int32, (step, rows), 0)
                - lax.broadcasted_iota(jnp.int32, (step, rows), 1)
                + (first + half)
            )
            made = {(d, r, m): jnp.zeros((step, rows), F32) for d in range(2) for r in range(2) for m in range(2)}
            for j in range(taps):
                here = diff == j
                for d, r, m in made:
                    pick = tap[d, r][j] if m == 0 else tap[d, r][taps - 1 - j]
                    made[d, r, m] = jnp.where(here, pick, made[d, r, m])
            for (d, r, m), value in made.items():
                value = (value * scale[d, r]).astype(BF16)
                lanes = slice(r * rows, (r + 1) * rows)
                if d == 0:
                    x_ref[m, v, r * rows + first : r * rows + first + step, lanes] = value
                elif m == 1:
                    y_ref[0, v, first : first + step, lanes] = value
                else:
                    target = pl.multiple_of(jnp.bitwise_xor(first // step, place) * step, step)
                    y_ref[1, v, pl.ds(target, step), lanes] = value
        tall = z_ref.shape[1] // (2 * views)
        wide = z_ref.shape[2]
        step = 16
        for first in range(0, tall, step):
            diff = (
                lax.broadcasted_iota(jnp.int32, (step, wide), 1)
                - lax.broadcasted_iota(jnp.int32, (step, wide), 0)
                - first
            )
            made = {(r, m): jnp.zeros((step, wide), F32) for r in range(2) for m in range(2)}
            for j in range(taps):
                here = diff == 8 * j
                for r, m in made:
                    pick = tap[2, r][j] if m == 0 else tap[2, r][taps - 1 - j]
                    made[r, m] = jnp.where(here, pick, made[r, m])
            for (r, m), value in made.items():
                top = (2 * v + r) * tall + first
                z_ref[m, top : top + step, :] = (value * scale[2, r][0:1, 0:1]).astype(BF16)


def dot(a, b):
    return jnp.dot(a, b, preferred_element_type=F32)


CHUNK = 4


def inverted(value):
    guess = pl.reciprocal(value, approx=True)
    return guess * (2.0 - value * guess)


def filter_to(load, views, groups, z_ref, x_ref, y_ref, scale_ref, e_ref, g_ref, exact, emit):
    tall = z_ref.shape[0] // (2 * views)
    z_out = tall // 8
    rows = y_ref.shape[1]
    for pair in range(rows // 16):
        block = load(slice(pair * 16, pair * 16 + 16))
        planes = block.shape[0]
        depth = (planes - (groups - 1) * z_out) * 8
        octets = [block[:, 8 * o : 8 * o + 8, :].reshape(planes * 8, rows).astype(BF16) for o in range(2)]
        octets = jnp.concatenate(octets, axis=1)
        for part in range(groups):
            data = octets[part * z_out * 8 : part * z_out * 8 + depth]
            all_e = dot(z_ref[:, :depth], data)
            for v in range(views):
                for r in range(2):
                    top = (2 * v + r) * tall
                    e = all_e[top : top + tall]
                    e = jnp.concatenate([e[:, :rows], e[:, rows:]], axis=0)
                    lanes = slice(r * rows, (r + 1) * rows)
                    if exact:
                        high, low = split(e)
                        e_ref[v, 0, pair * groups + part, :, lanes] = high
                        e_ref[v, 1, pair * groups + part, :, lanes] = low
                    else:
                        e_ref[v, 0, pair * groups + part, :, lanes] = e.astype(BF16)
    for v in range(views):
        for first in range(0, rows // 16 * groups, CHUNK):
            e = e_ref[v, 0, first : first + CHUNK].reshape(CHUNK * 2 * tall, 2 * rows)
            all_g = dot(e, x_ref[v])
            if exact:
                e = e_ref[v, 1, first : first + CHUNK].reshape(CHUNK * 2 * tall, 2 * rows)
                all_g = all_g + dot(e, x_ref[v])
            for index in range(first, first + CHUNK):
                pair, part = index // groups, index % groups
                g = all_g[(index - first) * 2 * tall : (index - first + 1) * 2 * tall]
                for r in range(2):
                    lanes = slice(r * rows, (r + 1) * rows)
                    g_rows = jnp.concatenate(
                        [g[o * tall : (o + 1) * tall, lanes].reshape(z_out, 8, rows) for o in range(2)], axis=1
                    )
                    g_rows = g_rows * scale_ref[v, r]
                    target = slice(r * rows + pair * 16, r * rows + pair * 16 + 16)
                    planes_at = slice(part * z_out, (part + 1) * z_out)
                    if exact:
                        high, low = split(g_rows)
                        g_ref[v, 0, planes_at, target, :] = high
                        g_ref[v, 1, planes_at, target, :] = low
                    else:
                        g_ref[v, 0, planes_at, target, :] = g_rows.astype(BF16)
    for v in range(views):
        for z in range(0, groups * z_out, 2):
            data = jnp.concatenate([g_ref[v, 0, z], g_ref[v, 0, z + 1]], axis=1)
            out = dot(y_ref[v], data)
            if exact:
                data = jnp.concatenate([g_ref[v, 1, z], g_ref[v, 1, z + 1]], axis=1)
                out = out + dot(y_ref[v], data)
            emit(v, z, out[:, :rows])
            emit(v, z + 1, out[:, rows:])


def scratch(views, groups, halves, z_out, rows, cols):
    return [
        pltpu.VMEM((views, halves, rows // 16 * groups, 2 * z_out * 8, 2 * cols), BF16),
        pltpu.VMEM((views, halves, groups * z_out, 2 * rows, cols), BF16),
    ]


def inverse_kernel(early, place_ref, low_ref, high_ref, own_ref, z_ref, x_ref, y_ref, scale_ref, out_ref, e_ref, g_ref):
    side_first = (place_ref[0] % 2 == 0) == early

    def load(at):
        side = jnp.concatenate([low_ref[:, at, :], high_ref[:, at, :]], axis=0).astype(F32)
        own = own_ref[:, at, :].astype(F32)
        return jnp.concatenate([jnp.where(side_first, side, own), jnp.where(side_first, own, side)], axis=0)

    def emit(v, z, blurred):
        out_ref[v, z] = inverted(blurred)

    views = out_ref.shape[0]
    filter_to(load, views, 2, z_ref.at[0], x_ref.at[0], y_ref.at[0], scale_ref, e_ref, g_ref, False, emit)


def correction_kernel(
    place_ref,
    before_ref,
    rec_ref,
    after_ref,
    early_ref,
    late_ref,
    z_ref,
    x_ref,
    y_ref,
    scale_ref,
    keep_ref,
    send_ref,
    e_ref,
    g_ref,
    product_ref,
):
    views, planes = rec_ref.shape[:2]
    part = keep_ref.shape[2]
    tall = z_ref.shape[1] // views
    early_first = place_ref[0] % 2 == 0
    most = [jnp.zeros((8, product_ref.shape[2]), F32)]
    for v in range(views):

        def load(at, v=v):
            rec = [ref[v, :, at, :].astype(F32) for ref in (before_ref, rec_ref, after_ref)]
            early, late = early_ref[v, :, at, :], late_ref[v, :, at, :]
            inverse = [jnp.where(early_first, early, late), jnp.where(early_first, late, early)]
            return jnp.concatenate(rec, axis=0) * jnp.concatenate(inverse, axis=0)

        def emit(_, z, value, v=v):
            if v > 0:
                value = value * product_ref[z]
            product_ref[z] = value
            if v == views - 1:
                for top in range(0, value.shape[0], 8):
                    most[0] = jnp.maximum(most[0], value[top : top + 8])

        z_view = z_ref.at[1, v * tall : (v + 1) * tall]
        filter_to(
            load,
            1,
            2,
            z_view,
            x_ref.at[1, v : v + 1],
            y_ref.at[1, v : v + 1],
            scale_ref.at[v : v + 1],
            e_ref,
            g_ref,
            True,
            emit,
        )
    top = jnp.maximum(jnp.max(most[0], axis=(0, 1), keepdims=True), 1e-30)
    quarter = jnp.ceil(jnp.log2(top) * 0.25)
    scale = jnp.exp2(-4.0 * quarter)
    root = jnp.broadcast_to(jnp.exp2(quarter), (part, product_ref.shape[2]))
    for z in range(planes):
        value = product_ref[z] * scale
        for b in range(4):
            (keep_ref, send_ref)[b % 2][b // 2, z] = value[b * part : (b + 1) * part]
    for ref in (keep_ref, send_ref):
        for b in range(2):
            ref[b, planes] = root


def local(estimate, recordings, psf_taps):
    planes, rows, cols = estimate.shape
    taps = psf_taps.shape[-1]
    margin = (taps - 1) // 2
    views = recordings.shape[0]
    devices = lax.axis_size("gz")
    place = lax.axis_index("view")
    place_array = place.reshape(1).astype(jnp.int32)
    up = [(i, i + 1) for i in range(devices - 1)]
    down = [(i + 1, i) for i in range(devices - 1)]
    swap = [(i, i ^ 1) for i in range(4)]
    z_out = planes // 2
    shape = jax.ShapeDtypeStruct

    rounded = pl.pallas_call(
        prepare_kernel,
        out_shape=shape((planes, rows, cols), BF16),
        in_specs=[HBM],
        out_specs=HBM,
        scratch_shapes=[
            pltpu.VMEM((planes, rows, cols), F32),
            pltpu.VMEM((planes, rows, cols), BF16),
            pltpu.SemaphoreType.DMA((2, 5)),
        ],
        name="prepare",
        **params(10**6, 10**4, 58 * 1024 * 1024),
    )(estimate)
    both_ways = [(4 * i + w, 4 * j + w) for w in (0, 2) for i, j in up]
    both_ways += [(4 * i + w, 4 * j + w) for w in (1, 3) for i, j in down]
    mine = lax.ppermute(rounded, ("gz", "view"), both_ways)

    last, first = pl.pallas_call(
        edges_kernel,
        out_shape=[shape((views, margin, rows, cols), BF16)] * 2,
        in_specs=[HBM],
        out_specs=[HBM] * 2,
        scratch_shapes=[pltpu.SemaphoreType.DMA((2 * views,))],
        name="edges",
        **params(10**4, 10**4, 58 * 1024 * 1024),
    )(recordings)
    before = lax.ppermute(last, "gz", up)
    after = lax.ppermute(first, "gz", down)

    wide = -(-(z_out + taps - 1) * 8 // 128) * 128
    z_mat, x_mat, y_mat, scales = pl.pallas_call(
        matrices_kernel,
        out_shape=[
            shape((2, views * 2 * z_out * 8, wide), BF16),
            shape((2, views, 2 * cols, 2 * cols), BF16),
            shape((2, views, rows, 2 * rows), BF16),
            shape((views, 2, 1, 128), F32),
        ],
        in_specs=[SMEM, SMEM],
        out_specs=[VMEM] * 4,
        name="matrices",
        **params(10**6, 10**4),
    )(place_array, psf_taps)

    mine, z_mat = lax.optimization_barrier((mine, z_mat))
    mine = (mine[:margin], mine[margin:])
    other = [lax.ppermute(piece, "view", swap) for piece in mine]
    inverses = []
    for early, side in ((True, mine), (False, other)):
        inverses.append(
            pl.pallas_call(
                lambda *refs, early=early: inverse_kernel(early, *refs),
                out_shape=shape((views, planes, rows, cols), F32),
                in_specs=[SMEM] + [VMEM] * 7,
                out_specs=VMEM,
                scratch_shapes=scratch(views, 2, 1, z_out, rows, cols),
                name="inverses",
                **params(10**6, 10**4),
            )(place_array, *side, rounded, z_mat, x_mat, y_mat, scales)
        )
    part = rows // 4
    keep, send = pl.pallas_call(
        correction_kernel,
        out_shape=[shape((2, planes + 1, part, cols), F32)] * 2,
        in_specs=[SMEM] + [VMEM] * 9,
        out_specs=[VMEM] * 2,
        scratch_shapes=scratch(1, 2, 2, z_out, rows, cols) + [pltpu.VMEM((planes, rows, cols), F32)],
        name="corrections",
        **params(4 * 10**9, 5 * 10**6),
    )(place_array, before, recordings, after, *inverses, z_mat, x_mat, y_mat, scales)
    core = lax.ppermute(send, "view", swap)
    across = lax.ppermute((keep[1] * core[1]).astype(jnp.float16), "view", [(i, i ^ 2) for i in range(4)])
    own_rows = lax.dynamic_slice_in_dim(estimate, place * part, part, 1)
    root = keep[0, planes] * core[0, planes]
    partial = own_rows * (keep[0, :planes] * core[0, :planes])
    partial, root, across = lax.optimization_barrier((partial, root, across))
    root = root * across[planes].astype(F32)
    return partial * (across[:planes].astype(F32) * (root * root * root * root))


def solution(mesh):
    in_specs = (P("gz", None, None), P("view", "gz", None, None), P("view", None, None, None))
    out_specs = P("gz", "view", None)
    return jax.shard_map(local, mesh=mesh, in_specs=in_specs, out_specs=out_specs, check_vma=False)
```

```python
import jax
import jax.numpy as jnp
from jax import lax
from jax.experimental import pallas as pl
from jax.experimental.pallas import tpu as pltpu
from jax.sharding import PartitionSpec as P

F32 = jnp.float32
BF16 = jnp.bfloat16
VMEM = pl.BlockSpec(memory_space=pltpu.VMEM)
HBM = pl.BlockSpec(memory_space=pltpu.HBM)
SMEM = pl.BlockSpec(memory_space=pltpu.SMEM)
LIMIT = 20 * 1024 * 1024


def split(value):
    high = value.astype(BF16)
    return high, (value - high.astype(F32)).astype(BF16)


def params(flops, nbytes, limit=LIMIT):
    return dict(
        compiler_params=pltpu.CompilerParams(vmem_limit_bytes=limit),
        cost_estimate=pl.CostEstimate(flops=flops, bytes_accessed=nbytes, transcendentals=0),
    )


def edges_kernel(rec_ref, last_out, first_out, held, sems):
    views, planes = rec_ref.shape[:2]
    margin = last_out.shape[1]
    copies, outs = [], []
    for v in range(views):
        for out, begin in ((last_out, planes - margin), (first_out, 0)):
            i = len(copies)
            copies.append(pltpu.make_async_copy(rec_ref.at[v, pl.ds(begin, margin)], held.at[i], sems.at[0, i]))
            outs.append(pltpu.make_async_copy(held.at[i], out.at[v], sems.at[1, i]))
    for copy in copies:
        copy.start()
    for copy, out in zip(copies, outs):
        copy.wait()
        out.start()
    for out in outs:
        out.wait()


def rounded_scale(tap, total):
    factor = jnp.exp2(lax.broadcasted_iota(jnp.int32, (1, 128), 1).astype(F32) * (1.0 / 128.0))
    scale = factor / jnp.full((1, 128), total, F32)
    sums, running = [], jnp.zeros((1, 128), F32)
    for value in tap:
        exact = value * scale
        running = running + (exact.astype(BF16).astype(F32) - exact)
        sums.append(running)
    error = jnp.zeros((1, 128), F32)
    for partial in sums:
        rest = running - partial
        error = error + partial * partial + rest * rest
    error = error / (factor * factor)
    best = error == jnp.min(error, axis=1, keepdims=True)
    factor = jnp.max(jnp.where(best, factor, 0.0), axis=1, keepdims=True)
    scale = jnp.max(jnp.where(best, scale, 0.0), axis=1, keepdims=True)
    return jnp.broadcast_to(scale, (1, 128)), jnp.broadcast_to(factor, (1, 128))


def matrices_kernel(place_ref, taps_ref, z_ref, x_ref, y_ref, scale_ref):
    views, taps = taps_ref.shape[0], taps_ref.shape[3]
    half = (taps - 1) // 2
    rows = x_ref.shape[2] // 2
    place = place_ref[0]
    zeros = jnp.zeros((rows, rows), BF16)

    for v in range(views):
        tap = {
            (d, r): [taps_ref[v, d, r, j] for j in range(taps)] for d in range(3) for r in range(2)
        }
        scale = {}
        for r in range(2):
            undo = jnp.ones((1, 128), F32)
            for d in range(3):
                values = tap[d, r] if d < 2 else tap[2, 0] + tap[2, 1]
                total = values[0]
                for value in values[1:]:
                    total = total + value
                scale[d, r], factor = rounded_scale(tap[d, r], total)
                undo = undo / factor
            scale_ref[v, r] = undo
        for direction in range(2):
            for r in range(2):
                other = 1 - r
                x_ref[direction, v, r * rows : (r + 1) * rows, other * rows : (other + 1) * rows] = zeros
        step = 32
        for first in range(0, rows, step):
            diff = (
                lax.broadcasted_iota(jnp.int32, (step, rows), 0)
                - lax.broadcasted_iota(jnp.int32, (step, rows), 1)
                + (first + half)
            )
            made = {(d, r, m): jnp.zeros((step, rows), F32) for d in range(2) for r in range(2) for m in range(2)}
            for j in range(taps):
                here = diff == j
                for d, r, m in made:
                    pick = tap[d, r][j] if m == 0 else tap[d, r][taps - 1 - j]
                    made[d, r, m] = jnp.where(here, pick, made[d, r, m])
            for (d, r, m), value in made.items():
                value = (value * scale[d, r]).astype(BF16)
                lanes = slice(r * rows, (r + 1) * rows)
                if d == 0:
                    x_ref[m, v, r * rows + first : r * rows + first + step, lanes] = value
                elif m == 1:
                    y_ref[0, v, first : first + step, lanes] = value
                else:
                    target = pl.multiple_of(jnp.bitwise_xor(first // step, place) * step, step)
                    y_ref[1, v, pl.ds(target, step), lanes] = value
        tall = z_ref.shape[1] // (2 * views)
        wide = z_ref.shape[2]
        step = 16
        for first in range(0, tall, step):
            diff = (
                lax.broadcasted_iota(jnp.int32, (step, wide), 1)
                - lax.broadcasted_iota(jnp.int32, (step, wide), 0)
                - first
            )
            made = {(r, m): jnp.zeros((step, wide), F32) for r in range(2) for m in range(2)}
            for j in range(taps):
                here = diff == 8 * j
                for r, m in made:
                    pick = tap[2, r][j] if m == 0 else tap[2, r][taps - 1 - j]
                    made[r, m] = jnp.where(here, pick, made[r, m])
            for (r, m), value in made.items():
                top = (2 * v + r) * tall + first
                z_ref[m, top : top + step, :] = (value * scale[2, r][0:1, 0:1]).astype(BF16)


def dot(a, b):
    return jnp.dot(a, b, preferred_element_type=F32)


CHUNK = 4


def inverted(value):
    guess = pl.reciprocal(value, approx=True)
    return guess * (2.0 - value * guess)


def filter_to(load, views, groups, z_ref, x_ref, y_ref, scale_ref, e_ref, g_ref, exact, emit):
    tall = z_ref.shape[0] // (2 * views)
    z_out = tall // 8
    rows = y_ref.shape[1]
    for pair in range(rows // 16):
        block = load(slice(pair * 16, pair * 16 + 16))
        planes = block.shape[0]
        depth = (planes - (groups - 1) * z_out) * 8
        octets = [block[:, 8 * o : 8 * o + 8, :].reshape(planes * 8, rows).astype(BF16) for o in range(2)]
        octets = jnp.concatenate(octets, axis=1)
        for part in range(groups):
            data = octets[part * z_out * 8 : part * z_out * 8 + depth]
            all_e = dot(z_ref[:, :depth], data)
            for v in range(views):
                for r in range(2):
                    top = (2 * v + r) * tall
                    e = all_e[top : top + tall]
                    e = jnp.concatenate([e[:, :rows], e[:, rows:]], axis=0)
                    lanes = slice(r * rows, (r + 1) * rows)
                    if exact:
                        high, low = split(e)
                        e_ref[v, 0, pair * groups + part, :, lanes] = high
                        e_ref[v, 1, pair * groups + part, :, lanes] = low
                    else:
                        e_ref[v, 0, pair * groups + part, :, lanes] = e.astype(BF16)
    for v in range(views):
        for first in range(0, rows // 16 * groups, CHUNK):
            e = e_ref[v, 0, first : first + CHUNK].reshape(CHUNK * 2 * tall, 2 * rows)
            all_g = dot(e, x_ref[v])
            if exact:
                e = e_ref[v, 1, first : first + CHUNK].reshape(CHUNK * 2 * tall, 2 * rows)
                all_g = all_g + dot(e, x_ref[v])
            for index in range(first, first + CHUNK):
                pair, part = index // groups, index % groups
                g = all_g[(index - first) * 2 * tall : (index - first + 1) * 2 * tall]
                for r in range(2):
                    lanes = slice(r * rows, (r + 1) * rows)
                    g_rows = jnp.concatenate(
                        [g[o * tall : (o + 1) * tall, lanes].reshape(z_out, 8, rows) for o in range(2)], axis=1
                    )
                    g_rows = g_rows * scale_ref[v, r]
                    target = slice(r * rows + pair * 16, r * rows + pair * 16 + 16)
                    planes_at = slice(part * z_out, (part + 1) * z_out)
                    if exact:
                        high, low = split(g_rows)
                        g_ref[v, 0, planes_at, target, :] = high
                        g_ref[v, 1, planes_at, target, :] = low
                    else:
                        g_ref[v, 0, planes_at, target, :] = g_rows.astype(BF16)
    for v in range(views):
        for z in range(0, groups * z_out, 2):
            data = jnp.concatenate([g_ref[v, 0, z], g_ref[v, 0, z + 1]], axis=1)
            out = dot(y_ref[v], data)
            if exact:
                data = jnp.concatenate([g_ref[v, 1, z], g_ref[v, 1, z + 1]], axis=1)
                out = out + dot(y_ref[v], data)
            emit(v, z, out[:, :rows])
            emit(v, z + 1, out[:, rows:])


def scratch(views, groups, halves, z_out, rows, cols):
    return [
        pltpu.VMEM((views, halves, rows // 16 * groups, 2 * z_out * 8, 2 * cols), BF16),
        pltpu.VMEM((views, halves, groups * z_out, 2 * rows, cols), BF16),
    ]


def inverse_kernel(early, place_ref, low_ref, high_ref, own_ref, z_ref, x_ref, y_ref, scale_ref, out_ref, e_ref, g_ref):
    side_first = (place_ref[0] % 2 == 0) == early

    def load(at):
        side = jnp.concatenate([low_ref[:, at, :], high_ref[:, at, :]], axis=0).astype(F32)
        own = own_ref[:, at, :].astype(F32)
        return jnp.concatenate([jnp.where(side_first, side, own), jnp.where(side_first, own, side)], axis=0)

    def emit(v, z, blurred):
        out_ref[v, z] = inverted(blurred)

    views = out_ref.shape[0]
    filter_to(load, views, 2, z_ref.at[0], x_ref.at[0], y_ref.at[0], scale_ref, e_ref, g_ref, False, emit)


def correction_kernel(
    place_ref,
    before_ref,
    rec_ref,
    after_ref,
    early_ref,
    late_ref,
    z_ref,
    x_ref,
    y_ref,
    scale_ref,
    keep_ref,
    send_ref,
    e_ref,
    g_ref,
    product_ref,
):
    views, planes = rec_ref.shape[:2]
    part = keep_ref.shape[2]
    tall = z_ref.shape[1] // views
    early_first = place_ref[0] % 2 == 0
    most = [jnp.zeros((8, product_ref.shape[2]), F32)]
    for v in range(views):

        def load(at, v=v):
            rec = [ref[v, :, at, :].astype(F32) for ref in (before_ref, rec_ref, after_ref)]
            early, late = early_ref[v, :, at, :], late_ref[v, :, at, :]
            inverse = [jnp.where(early_first, early, late), jnp.where(early_first, late, early)]
            return jnp.concatenate(rec, axis=0) * jnp.concatenate(inverse, axis=0)

        def emit(_, z, value, v=v):
            if v > 0:
                value = value * product_ref[z]
            product_ref[z] = value
            if v == views - 1:
                for top in range(0, value.shape[0], 8):
                    most[0] = jnp.maximum(most[0], value[top : top + 8])

        z_view = z_ref.at[1, v * tall : (v + 1) * tall]
        filter_to(
            load,
            1,
            2,
            z_view,
            x_ref.at[1, v : v + 1],
            y_ref.at[1, v : v + 1],
            scale_ref.at[v : v + 1],
            e_ref,
            g_ref,
            True,
            emit,
        )
    top = jnp.maximum(jnp.max(most[0], axis=(0, 1), keepdims=True), 1e-30)
    quarter = jnp.ceil(jnp.log2(top) * 0.25)
    scale = jnp.exp2(-4.0 * quarter)
    root = jnp.broadcast_to(jnp.exp2(quarter), (part, product_ref.shape[2]))
    for z in range(planes):
        value = product_ref[z] * scale
        for b in range(4):
            (keep_ref, send_ref)[b % 2][b // 2, z] = value[b * part : (b + 1) * part]
    for ref in (keep_ref, send_ref):
        for b in range(2):
            ref[b, planes] = root


def local(estimate, recordings, psf_taps):
    planes, rows, cols = estimate.shape
    taps = psf_taps.shape[-1]
    margin = (taps - 1) // 2
    views = recordings.shape[0]
    devices = lax.axis_size("gz")
    place = lax.axis_index("view")
    place_array = place.reshape(1).astype(jnp.int32)
    up = [(i, i + 1) for i in range(devices - 1)]
    down = [(i + 1, i) for i in range(devices - 1)]
    swap = [(i, i ^ 1) for i in range(4)]
    z_out = planes // 2
    shape = jax.ShapeDtypeStruct

    rounded = estimate.astype(BF16)
    both_ways = [(4 * i + w, 4 * j + w) for w in (0, 2) for i, j in up]
    both_ways += [(4 * i + w, 4 * j + w) for w in (1, 3) for i, j in down]
    mine = lax.ppermute(rounded, ("gz", "view"), both_ways)

    last, first = pl.pallas_call(
        edges_kernel,
        out_shape=[shape((views, margin, rows, cols), BF16)] * 2,
        in_specs=[HBM],
        out_specs=[HBM] * 2,
        scratch_shapes=[
            pltpu.VMEM((2 * views, margin, rows, cols), BF16),
            pltpu.SemaphoreType.DMA((2, 2 * views)),
        ],
        name="edges",
        **params(10**4, 10**4, 58 * 1024 * 1024),
    )(recordings)
    before = lax.ppermute(last, "gz", up)
    after = lax.ppermute(first, "gz", down)

    wide = -(-(z_out + taps - 1) * 8 // 128) * 128
    z_mat, x_mat, y_mat, scales = pl.pallas_call(
        matrices_kernel,
        out_shape=[
            shape((2, views * 2 * z_out * 8, wide), BF16),
            shape((2, views, 2 * cols, 2 * cols), BF16),
            shape((2, views, rows, 2 * rows), BF16),
            shape((views, 2, 1, 128), F32),
        ],
        in_specs=[SMEM, SMEM],
        out_specs=[VMEM] * 4,
        name="matrices",
        **params(10**6, 10**4),
    )(place_array, psf_taps)

    mine, z_mat = lax.optimization_barrier((mine, z_mat))
    mine = (mine[:margin], mine[margin:])
    other = [lax.ppermute(piece, "view", swap) for piece in mine]
    inverses = []
    for early, side in ((True, mine), (False, other)):
        inverses.append(
            pl.pallas_call(
                lambda *refs, early=early: inverse_kernel(early, *refs),
                out_shape=shape((views, planes, rows, cols), F32),
                in_specs=[SMEM] + [VMEM] * 7,
                out_specs=VMEM,
                scratch_shapes=scratch(views, 2, 1, z_out, rows, cols),
                name="inverses",
                **params(10**6, 10**4),
            )(place_array, *side, rounded, z_mat, x_mat, y_mat, scales)
        )
    part = rows // 4
    keep, send = pl.pallas_call(
        correction_kernel,
        out_shape=[shape((2, planes + 1, part, cols), F32)] * 2,
        in_specs=[SMEM] + [VMEM] * 9,
        out_specs=[VMEM] * 2,
        scratch_shapes=scratch(1, 2, 2, z_out, rows, cols) + [pltpu.VMEM((planes, rows, cols), F32)],
        name="corrections",
        **params(4 * 10**9, 5 * 10**6),
    )(place_array, before, recordings, after, *inverses, z_mat, x_mat, y_mat, scales)
    core = lax.ppermute(send, "view", swap)
    across = lax.ppermute((keep[1] * core[1]).astype(jnp.float16), "view", [(i, i ^ 2) for i in range(4)])
    own_rows = lax.dynamic_slice_in_dim(estimate, place * part, part, 1)
    root = keep[0, planes] * core[0, planes]
    partial = own_rows * (keep[0, :planes] * core[0, :planes])
    partial, root, across = lax.optimization_barrier((partial, root, across))
    root = root * across[planes].astype(F32)
    return partial * (across[:planes].astype(F32) * (root * root * root * root))


def solution(mesh):
    in_specs = (P("gz", None, None), P("view", "gz", None, None), P("view", None, None, None))
    out_specs = P("gz", "view", None)
    return jax.shard_map(local, mesh=mesh, in_specs=in_specs, out_specs=out_specs, check_vma=False)
```

```python
import jax
import jax.numpy as jnp
from jax import lax
from jax.experimental import pallas as pl
from jax.experimental.pallas import tpu as pltpu
from jax.sharding import PartitionSpec as P

F32 = jnp.float32
BF16 = jnp.bfloat16
VMEM = pl.BlockSpec(memory_space=pltpu.VMEM)
HBM = pl.BlockSpec(memory_space=pltpu.HBM)
SMEM = pl.BlockSpec(memory_space=pltpu.SMEM)
LIMIT = 20 * 1024 * 1024


def split(value):
    high = value.astype(BF16)
    return high, (value - high.astype(F32)).astype(BF16)


def params(flops, nbytes, limit=LIMIT):
    return dict(
        compiler_params=pltpu.CompilerParams(vmem_limit_bytes=limit),
        cost_estimate=pl.CostEstimate(flops=flops, bytes_accessed=nbytes, transcendentals=0),
    )


def edges_kernel(rec_ref, last_out, first_out, held, sems):
    views, planes = rec_ref.shape[:2]
    margin = last_out.shape[1]
    copies, outs = [], []
    for v in range(views):
        for out, begin in ((last_out, planes - margin), (first_out, 0)):
            i = len(copies)
            copies.append(pltpu.make_async_copy(rec_ref.at[v, pl.ds(begin, margin)], held.at[i], sems.at[0, i]))
            outs.append(pltpu.make_async_copy(held.at[i], out.at[v], sems.at[1, i]))
    for copy in copies:
        copy.start()
    for copy, out in zip(copies, outs):
        copy.wait()
        out.start()
    for out in outs:
        out.wait()


def rounded_scale(tap, total):
    factor = jnp.exp2(lax.broadcasted_iota(jnp.int32, (1, 128), 1).astype(F32) * (1.0 / 128.0))
    scale = factor / jnp.full((1, 128), total, F32)
    sums, running = [], jnp.zeros((1, 128), F32)
    for value in tap:
        exact = value * scale
        running = running + (exact.astype(BF16).astype(F32) - exact)
        sums.append(running)
    error = jnp.zeros((1, 128), F32)
    for partial in sums:
        rest = running - partial
        error = error + partial * partial + rest * rest
    error = error / (factor * factor)
    best = error == jnp.min(error, axis=1, keepdims=True)
    factor = jnp.max(jnp.where(best, factor, 0.0), axis=1, keepdims=True)
    scale = jnp.max(jnp.where(best, scale, 0.0), axis=1, keepdims=True)
    return jnp.broadcast_to(scale, (1, 128)), jnp.broadcast_to(factor, (1, 128))


def matrices_kernel(place_ref, taps_ref, z_ref, x_ref, y_ref, scale_ref):
    views, taps = taps_ref.shape[0], taps_ref.shape[3]
    half = (taps - 1) // 2
    rows = x_ref.shape[2] // 2
    place = place_ref[0]
    zeros = jnp.zeros((rows, rows), BF16)

    for v in range(views):
        tap = {
            (d, r): [taps_ref[v, d, r, j] for j in range(taps)] for d in range(3) for r in range(2)
        }
        scale = {}
        for r in range(2):
            undo = jnp.ones((1, 128), F32)
            for d in range(3):
                values = tap[d, r] if d < 2 else tap[2, 0] + tap[2, 1]
                total = values[0]
                for value in values[1:]:
                    total = total + value
                scale[d, r], factor = rounded_scale(tap[d, r], total)
                undo = undo / factor
            scale_ref[v, r] = undo
        for direction in range(2):
            for r in range(2):
                other = 1 - r
                x_ref[direction, v, r * rows : (r + 1) * rows, other * rows : (other + 1) * rows] = zeros
        step = 32
        for first in range(0, rows, step):
            diff = (
                lax.broadcasted_iota(jnp.int32, (step, rows), 0)
                - lax.broadcasted_iota(jnp.int32, (step, rows), 1)
                + (first + half)
            )
            made = {(d, r, m): jnp.zeros((step, rows), F32) for d in range(2) for r in range(2) for m in range(2)}
            for j in range(taps):
                here = diff == j
                for d, r, m in made:
                    pick = tap[d, r][j] if m == 0 else tap[d, r][taps - 1 - j]
                    made[d, r, m] = jnp.where(here, pick, made[d, r, m])
            for (d, r, m), value in made.items():
                value = (value * scale[d, r]).astype(BF16)
                lanes = slice(r * rows, (r + 1) * rows)
                if d == 0:
                    x_ref[m, v, r * rows + first : r * rows + first + step, lanes] = value
                elif m == 1:
                    y_ref[0, v, first : first + step, lanes] = value
                else:
                    target = pl.multiple_of(jnp.bitwise_xor(first // step, place) * step, step)
                    y_ref[1, v, pl.ds(target, step), lanes] = value
        tall = z_ref.shape[1] // (2 * views)
        wide = z_ref.shape[2]
        step = 16
        for first in range(0, tall, step):
            diff = (
                lax.broadcasted_iota(jnp.int32, (step, wide), 1)
                - lax.broadcasted_iota(jnp.int32, (step, wide), 0)
                - first
            )
            made = {(r, m): jnp.zeros((step, wide), F32) for r in range(2) for m in range(2)}
            for j in range(taps):
                here = diff == 8 * j
                for r, m in made:
                    pick = tap[2, r][j] if m == 0 else tap[2, r][taps - 1 - j]
                    made[r, m] = jnp.where(here, pick, made[r, m])
            for (r, m), value in made.items():
                top = (2 * v + r) * tall + first
                z_ref[m, top : top + step, :] = (value * scale[2, r][0:1, 0:1]).astype(BF16)


def dot(a, b):
    return jnp.dot(a, b, preferred_element_type=F32)


CHUNK = 4


def inverted(value):
    guess = pl.reciprocal(value, approx=True)
    return guess * (2.0 - value * guess)


def filter_to(load, views, groups, z_ref, x_ref, y_ref, scale_ref, e_ref, g_ref, exact, emit):
    tall = z_ref.shape[0] // (2 * views)
    z_out = tall // 8
    rows = y_ref.shape[1]
    for pair in range(rows // 16):
        block = load(slice(pair * 16, pair * 16 + 16))
        planes = block.shape[0]
        depth = (planes - (groups - 1) * z_out) * 8
        octets = [block[:, 8 * o : 8 * o + 8, :].reshape(planes * 8, rows).astype(BF16) for o in range(2)]
        octets = jnp.concatenate(octets, axis=1)
        for part in range(groups):
            data = octets[part * z_out * 8 : part * z_out * 8 + depth]
            all_e = dot(z_ref[:, :depth], data)
            for v in range(views):
                for r in range(2):
                    top = (2 * v + r) * tall
                    e = all_e[top : top + tall]
                    e = jnp.concatenate([e[:, :rows], e[:, rows:]], axis=0)
                    lanes = slice(r * rows, (r + 1) * rows)
                    if exact:
                        high, low = split(e)
                        e_ref[v, 0, pair * groups + part, :, lanes] = high
                        e_ref[v, 1, pair * groups + part, :, lanes] = low
                    else:
                        e_ref[v, 0, pair * groups + part, :, lanes] = e.astype(BF16)
    for v in range(views):
        for first in range(0, rows // 16 * groups, CHUNK):
            e = e_ref[v, 0, first : first + CHUNK].reshape(CHUNK * 2 * tall, 2 * rows)
            all_g = dot(e, x_ref[v])
            if exact:
                e = e_ref[v, 1, first : first + CHUNK].reshape(CHUNK * 2 * tall, 2 * rows)
                all_g = all_g + dot(e, x_ref[v])
            for index in range(first, first + CHUNK):
                pair, part = index // groups, index % groups
                g = all_g[(index - first) * 2 * tall : (index - first + 1) * 2 * tall]
                for r in range(2):
                    lanes = slice(r * rows, (r + 1) * rows)
                    g_rows = jnp.concatenate(
                        [g[o * tall : (o + 1) * tall, lanes].reshape(z_out, 8, rows) for o in range(2)], axis=1
                    )
                    g_rows = g_rows * scale_ref[v, r]
                    target = slice(r * rows + pair * 16, r * rows + pair * 16 + 16)
                    planes_at = slice(part * z_out, (part + 1) * z_out)
                    if exact:
                        high, low = split(g_rows)
                        g_ref[v, 0, planes_at, target, :] = high
                        g_ref[v, 1, planes_at, target, :] = low
                    else:
                        g_ref[v, 0, planes_at, target, :] = g_rows.astype(BF16)
    for v in range(views):
        for z in range(0, groups * z_out, 2):
            data = jnp.concatenate([g_ref[v, 0, z], g_ref[v, 0, z + 1]], axis=1)
            out = dot(y_ref[v], data)
            if exact:
                data = jnp.concatenate([g_ref[v, 1, z], g_ref[v, 1, z + 1]], axis=1)
                out = out + dot(y_ref[v], data)
            emit(v, z, out[:, :rows])
            emit(v, z + 1, out[:, rows:])


def scratch(views, groups, halves, z_out, rows, cols):
    return [
        pltpu.VMEM((views, halves, rows // 16 * groups, 2 * z_out * 8, 2 * cols), BF16),
        pltpu.VMEM((views, halves, groups * z_out, 2 * rows, cols), BF16),
    ]


def inverse_kernel(early, place_ref, low_ref, high_ref, own_ref, z_ref, x_ref, y_ref, scale_ref, out_ref, e_ref, g_ref):
    side_first = (place_ref[0] % 2 == 0) == early

    def load(at):
        side = jnp.concatenate([low_ref[:, at, :], high_ref[:, at, :]], axis=0).astype(F32)
        own = own_ref[:, at, :].astype(F32)
        return jnp.concatenate([jnp.where(side_first, side, own), jnp.where(side_first, own, side)], axis=0)

    def emit(v, z, blurred):
        out_ref[v, z] = inverted(blurred)

    views = out_ref.shape[0]
    filter_to(load, views, 2, z_ref.at[0], x_ref.at[0], y_ref.at[0], scale_ref, e_ref, g_ref, False, emit)


def correction_kernel(
    upper,
    place_ref,
    halo_ref,
    rec_ref,
    early_ref,
    late_ref,
    z_ref,
    x_ref,
    y_ref,
    scale_ref,
    keep_ref,
    send_ref,
    e_ref,
    g_ref,
    product_ref,
):
    views = rec_ref.shape[0]
    planes, part = product_ref.shape[0], keep_ref.shape[2]
    margin = halo_ref.shape[1]
    tall = z_ref.shape[1] // views
    early_first = place_ref[0] % 2 == 0
    most = [jnp.zeros((8, product_ref.shape[2]), F32)]
    for v in range(views):

        def load(at, v=v):
            halo, own = halo_ref[v, :, at, :].astype(F32), rec_ref[v, :, at, :].astype(F32)
            early, late = early_ref[v, :, at, :], late_ref[v, :, at, :]
            inverse = [jnp.where(early_first, early, late), jnp.where(early_first, late, early)]
            inverse = jnp.concatenate(inverse, axis=0)
            if upper:
                return jnp.concatenate([own, halo], axis=0) * inverse[margin:]
            return jnp.concatenate([halo, own], axis=0) * inverse[: inverse.shape[0] - margin]

        def emit(_, z, value, v=v):
            if v > 0:
                value = value * product_ref[z]
            product_ref[z] = value
            if v == views - 1:
                for top in range(0, value.shape[0], 8):
                    most[0] = jnp.maximum(most[0], value[top : top + 8])

        z_view = z_ref.at[1, v * tall : (v + 1) * tall]
        filter_to(
            load,
            1,
            1,
            z_view,
            x_ref.at[1, v : v + 1],
            y_ref.at[1, v : v + 1],
            scale_ref.at[v : v + 1],
            e_ref,
            g_ref,
            True,
            emit,
        )
    top = jnp.maximum(jnp.max(most[0], axis=(0, 1), keepdims=True), 1e-30)
    quarter = jnp.ceil(jnp.log2(top) * 0.25)
    scale = jnp.exp2(-4.0 * quarter)
    root = jnp.broadcast_to(jnp.exp2(quarter), (part, product_ref.shape[2]))
    for z in range(planes):
        value = product_ref[z] * scale
        for b in range(4):
            (keep_ref, send_ref)[b % 2][b // 2, z] = value[b * part : (b + 1) * part]
    for ref in (keep_ref, send_ref):
        for b in range(2):
            ref[b, planes] = root


def local(estimate, recordings, psf_taps):
    planes, rows, cols = estimate.shape
    taps = psf_taps.shape[-1]
    margin = (taps - 1) // 2
    views = recordings.shape[0]
    devices = lax.axis_size("gz")
    place = lax.axis_index("view")
    place_array = place.reshape(1).astype(jnp.int32)
    up = [(i, i + 1) for i in range(devices - 1)]
    down = [(i + 1, i) for i in range(devices - 1)]
    swap = [(i, i ^ 1) for i in range(4)]
    z_out = planes // 2
    shape = jax.ShapeDtypeStruct

    rounded = estimate.astype(BF16)
    both_ways = [(4 * i + w, 4 * j + w) for w in (0, 2) for i, j in up]
    both_ways += [(4 * i + w, 4 * j + w) for w in (1, 3) for i, j in down]
    mine = lax.ppermute(rounded, ("gz", "view"), both_ways)

    last, first = pl.pallas_call(
        edges_kernel,
        out_shape=[shape((views, margin, rows, cols), BF16)] * 2,
        in_specs=[HBM],
        out_specs=[HBM] * 2,
        scratch_shapes=[
            pltpu.VMEM((2 * views, margin, rows, cols), BF16),
            pltpu.SemaphoreType.DMA((2, 2 * views)),
        ],
        name="edges",
        **params(10**4, 10**4, 58 * 1024 * 1024),
    )(recordings)
    before = lax.ppermute(last, "gz", up)
    after = lax.ppermute(first, "gz", down)

    wide = -(-(z_out + taps - 1) * 8 // 128) * 128
    z_mat, x_mat, y_mat, scales = pl.pallas_call(
        matrices_kernel,
        out_shape=[
            shape((2, views * 2 * z_out * 8, wide), BF16),
            shape((2, views, 2 * cols, 2 * cols), BF16),
            shape((2, views, rows, 2 * rows), BF16),
            shape((views, 2, 1, 128), F32),
        ],
        in_specs=[SMEM, SMEM],
        out_specs=[VMEM] * 4,
        name="matrices",
        **params(10**6, 10**4),
    )(place_array, psf_taps)

    mine, z_mat = lax.optimization_barrier((mine, z_mat))
    mine = (mine[:margin], mine[margin:])
    other = [lax.ppermute(piece, "view", swap) for piece in mine]
    inverses = []
    for early, side in ((True, mine), (False, other)):
        inverses.append(
            pl.pallas_call(
                lambda *refs, early=early: inverse_kernel(early, *refs),
                out_shape=shape((views, planes, rows, cols), F32),
                in_specs=[SMEM] + [VMEM] * 7,
                out_specs=VMEM,
                scratch_shapes=scratch(views, 2, 1, z_out, rows, cols),
                name="inverses",
                **params(10**6, 10**4),
            )(place_array, *side, rounded, z_mat, x_mat, y_mat, scales)
        )
    part = rows // 4
    halves = []
    for upper, halo in ((False, before), (True, after)):
        halves.append(
            pl.pallas_call(
                lambda *refs, upper=upper: correction_kernel(upper, *refs),
                out_shape=[shape((2, z_out + 1, part, cols), F32)] * 2,
                in_specs=[SMEM] + [VMEM] * 8,
                out_specs=[VMEM] * 2,
                scratch_shapes=scratch(1, 1, 2, z_out, rows, cols) + [pltpu.VMEM((z_out, rows, cols), F32)],
                name="corrections",
                **params(2 * 10**9, 2 * 10**6),
            )(place_array, halo, recordings, *inverses, z_mat, x_mat, y_mat, scales)
        )
    own_rows = lax.dynamic_slice_in_dim(estimate, place * part, part, 1)
    cores = [lax.ppermute(send, "view", swap) for _, send in halves]
    outs = []
    for half, ((keep, _), core) in enumerate(zip(halves, cores)):
        across = lax.ppermute((keep[1] * core[1]).astype(jnp.float16), "view", [(i, i ^ 2) for i in range(4)])
        root = keep[0, z_out] * core[0, z_out]
        partial = own_rows[half * z_out : (half + 1) * z_out] * (keep[0, :z_out] * core[0, :z_out])
        outs.append((partial, root, across))
    outs = lax.optimization_barrier(outs)
    results = []
    for partial, root, across in outs:
        root = root * across[z_out].astype(F32)
        results.append(partial * (across[:z_out].astype(F32) * (root * root * root * root)))
    return jnp.concatenate(results, axis=0)


def solution(mesh):
    in_specs = (P("gz", None, None), P("view", "gz", None, None), P("view", None, None, None))
    out_specs = P("gz", "view", None)
    return jax.shard_map(local, mesh=mesh, in_specs=in_specs, out_specs=out_specs, check_vma=False)
```

```python
import jax
import jax.numpy as jnp
from jax import lax
from jax.experimental import pallas as pl
from jax.experimental.pallas import tpu as pltpu
from jax.sharding import PartitionSpec as P

F32 = jnp.float32
BF16 = jnp.bfloat16
VMEM = pl.BlockSpec(memory_space=pltpu.VMEM)
HBM = pl.BlockSpec(memory_space=pltpu.HBM)
SMEM = pl.BlockSpec(memory_space=pltpu.SMEM)
LIMIT = 20 * 1024 * 1024


def split(value):
    high = value.astype(BF16)
    return high, (value - high.astype(F32)).astype(BF16)


def params(flops, nbytes, limit=LIMIT):
    return dict(
        compiler_params=pltpu.CompilerParams(vmem_limit_bytes=limit),
        cost_estimate=pl.CostEstimate(flops=flops, bytes_accessed=nbytes, transcendentals=0),
    )


def edges_kernel(rec_ref, last_out, first_out, held, sems):
    views, planes = rec_ref.shape[:2]
    margin = last_out.shape[1]
    copies, outs = [], []
    for v in range(views):
        for out, begin in ((last_out, planes - margin), (first_out, 0)):
            i = len(copies)
            copies.append(pltpu.make_async_copy(rec_ref.at[v, pl.ds(begin, margin)], held.at[i], sems.at[0, i]))
            outs.append(pltpu.make_async_copy(held.at[i], out.at[v], sems.at[1, i]))
    for copy in copies:
        copy.start()
    for copy, out in zip(copies, outs):
        copy.wait()
        out.start()
    for out in outs:
        out.wait()


def rounded_scale(tap, total):
    factor = jnp.exp2(lax.broadcasted_iota(jnp.int32, (1, 128), 1).astype(F32) * (1.0 / 128.0))
    scale = factor / jnp.full((1, 128), total, F32)
    sums, running = [], jnp.zeros((1, 128), F32)
    for value in tap:
        exact = value * scale
        running = running + (exact.astype(BF16).astype(F32) - exact)
        sums.append(running)
    error = jnp.zeros((1, 128), F32)
    for partial in sums:
        rest = running - partial
        error = error + partial * partial + rest * rest
    error = error / (factor * factor)
    best = error == jnp.min(error, axis=1, keepdims=True)
    factor = jnp.max(jnp.where(best, factor, 0.0), axis=1, keepdims=True)
    scale = jnp.max(jnp.where(best, scale, 0.0), axis=1, keepdims=True)
    return jnp.broadcast_to(scale, (1, 128)), jnp.broadcast_to(factor, (1, 128))


def matrices_kernel(place_ref, taps_ref, z_ref, x_ref, y_ref, scale_ref):
    views, taps = taps_ref.shape[0], taps_ref.shape[3]
    half = (taps - 1) // 2
    rows = x_ref.shape[2] // 2
    place = place_ref[0]
    zeros = jnp.zeros((rows, rows), BF16)

    for v in range(views):
        tap = {
            (d, r): [taps_ref[v, d, r, j] for j in range(taps)] for d in range(3) for r in range(2)
        }
        scale = {}
        for r in range(2):
            undo = jnp.ones((1, 128), F32)
            for d in range(3):
                values = tap[d, r] if d < 2 else tap[2, 0] + tap[2, 1]
                total = values[0]
                for value in values[1:]:
                    total = total + value
                scale[d, r], factor = rounded_scale(tap[d, r], total)
                undo = undo / factor
            scale_ref[v, r] = undo
        for direction in range(2):
            for r in range(2):
                other = 1 - r
                x_ref[direction, v, r * rows : (r + 1) * rows, other * rows : (other + 1) * rows] = zeros
        step = 32
        for first in range(0, rows, step):
            diff = (
                lax.broadcasted_iota(jnp.int32, (step, rows), 0)
                - lax.broadcasted_iota(jnp.int32, (step, rows), 1)
                + (first + half)
            )
            made = {(d, r, m): jnp.zeros((step, rows), F32) for d in range(2) for r in range(2) for m in range(2)}
            for j in range(taps):
                here = diff == j
                for d, r, m in made:
                    pick = tap[d, r][j] if m == 0 else tap[d, r][taps - 1 - j]
                    made[d, r, m] = jnp.where(here, pick, made[d, r, m])
            for (d, r, m), value in made.items():
                value = (value * scale[d, r]).astype(BF16)
                lanes = slice(r * rows, (r + 1) * rows)
                if d == 0:
                    x_ref[m, v, r * rows + first : r * rows + first + step, lanes] = value
                elif m == 1:
                    y_ref[0, v, first : first + step, lanes] = value
                else:
                    target = pl.multiple_of(jnp.bitwise_xor(first // step, place) * step, step)
                    y_ref[1, v, pl.ds(target, step), lanes] = value
        tall = z_ref.shape[1] // (2 * views)
        wide = z_ref.shape[2]
        step = 16
        for first in range(0, tall, step):
            diff = (
                lax.broadcasted_iota(jnp.int32, (step, wide), 1)
                - lax.broadcasted_iota(jnp.int32, (step, wide), 0)
                - first
            )
            made = {(r, m): jnp.zeros((step, wide), F32) for r in range(2) for m in range(2)}
            for j in range(taps):
                here = diff == 8 * j
                for r, m in made:
                    pick = tap[2, r][j] if m == 0 else tap[2, r][taps - 1 - j]
                    made[r, m] = jnp.where(here, pick, made[r, m])
            for (r, m), value in made.items():
                top = (2 * v + r) * tall + first
                z_ref[m, top : top + step, :] = (value * scale[2, r][0:1, 0:1]).astype(BF16)


def dot(a, b):
    return jnp.dot(a, b, preferred_element_type=F32)


CHUNK = 4


def inverted(value):
    guess = pl.reciprocal(value, approx=True)
    return guess * (2.0 - value * guess)


def filter_to(load, views, groups, z_ref, x_ref, y_ref, scale_ref, e_ref, g_ref, exact, emit):
    tall = z_ref.shape[0] // (2 * views)
    z_out = tall // 8
    rows = y_ref.shape[1]
    for pair in range(rows // 16):
        block = load(slice(pair * 16, pair * 16 + 16))
        planes = block.shape[0]
        depth = (planes - (groups - 1) * z_out) * 8
        octets = [block[:, 8 * o : 8 * o + 8, :].reshape(planes * 8, rows).astype(BF16) for o in range(2)]
        octets = jnp.concatenate(octets, axis=1)
        for part in range(groups):
            data = octets[part * z_out * 8 : part * z_out * 8 + depth]
            all_e = dot(z_ref[:, :depth], data)
            for v in range(views):
                for r in range(2):
                    top = (2 * v + r) * tall
                    e = all_e[top : top + tall]
                    e = jnp.concatenate([e[:, :rows], e[:, rows:]], axis=0)
                    lanes = slice(r * rows, (r + 1) * rows)
                    if exact:
                        high, low = split(e)
                        e_ref[v, 0, pair * groups + part, :, lanes] = high
                        e_ref[v, 1, pair * groups + part, :, lanes] = low
                    else:
                        e_ref[v, 0, pair * groups + part, :, lanes] = e.astype(BF16)
    for v in range(views):
        for first in range(0, rows // 16 * groups, CHUNK):
            e = e_ref[v, 0, first : first + CHUNK].reshape(CHUNK * 2 * tall, 2 * rows)
            all_g = dot(e, x_ref[v])
            if exact:
                e = e_ref[v, 1, first : first + CHUNK].reshape(CHUNK * 2 * tall, 2 * rows)
                all_g = all_g + dot(e, x_ref[v])
            for index in range(first, first + CHUNK):
                pair, part = index // groups, index % groups
                g = all_g[(index - first) * 2 * tall : (index - first + 1) * 2 * tall]
                for r in range(2):
                    lanes = slice(r * rows, (r + 1) * rows)
                    g_rows = jnp.concatenate(
                        [g[o * tall : (o + 1) * tall, lanes].reshape(z_out, 8, rows) for o in range(2)], axis=1
                    )
                    g_rows = g_rows * scale_ref[v, r]
                    target = slice(r * rows + pair * 16, r * rows + pair * 16 + 16)
                    planes_at = slice(part * z_out, (part + 1) * z_out)
                    if exact:
                        high, low = split(g_rows)
                        g_ref[v, 0, planes_at, target, :] = high
                        g_ref[v, 1, planes_at, target, :] = low
                    else:
                        g_ref[v, 0, planes_at, target, :] = g_rows.astype(BF16)
    for v in range(views):
        for z in range(0, groups * z_out, 2):
            data = jnp.concatenate([g_ref[v, 0, z], g_ref[v, 0, z + 1]], axis=1)
            out = dot(y_ref[v], data)
            if exact:
                data = jnp.concatenate([g_ref[v, 1, z], g_ref[v, 1, z + 1]], axis=1)
                out = out + dot(y_ref[v], data)
            emit(v, z, out[:, :rows])
            emit(v, z + 1, out[:, rows:])


def scratch(views, groups, halves, z_out, rows, cols):
    return [
        pltpu.VMEM((views, halves, rows // 16 * groups, 2 * z_out * 8, 2 * cols), BF16),
        pltpu.VMEM((views, halves, groups * z_out, 2 * rows, cols), BF16),
    ]


def inverse_kernel(early, place_ref, low_ref, high_ref, own_ref, z_ref, x_ref, y_ref, scale_ref, out_ref, e_ref, g_ref):
    side_first = (place_ref[0] % 2 == 0) == early

    def load(at):
        side = jnp.concatenate([low_ref[:, at, :], high_ref[:, at, :]], axis=0).astype(F32)
        own = own_ref[:, at, :].astype(F32)
        return jnp.concatenate([jnp.where(side_first, side, own), jnp.where(side_first, own, side)], axis=0)

    def emit(v, z, blurred):
        out_ref[v, z] = inverted(blurred)

    views = out_ref.shape[0]
    filter_to(load, views, 2, z_ref.at[0], x_ref.at[0], y_ref.at[0], scale_ref, e_ref, g_ref, False, emit)


def correction_kernel(
    upper,
    place_ref,
    halo_ref,
    rec_ref,
    early_ref,
    late_ref,
    z_ref,
    x_ref,
    y_ref,
    scale_ref,
    keep_ref,
    send_ref,
    e_ref,
    g_ref,
    product_ref,
):
    views = rec_ref.shape[0]
    planes, part = product_ref.shape[0], keep_ref.shape[2]
    margin = halo_ref.shape[1]
    tall = z_ref.shape[1] // views
    early_first = place_ref[0] % 2 == 0
    most = [jnp.zeros((8, product_ref.shape[2]), F32)]
    for v in range(views):

        def load(at, v=v):
            halo, own = halo_ref[v, :, at, :].astype(F32), rec_ref[v, :, at, :].astype(F32)
            early, late = early_ref[v, :, at, :], late_ref[v, :, at, :]
            inverse = [jnp.where(early_first, early, late), jnp.where(early_first, late, early)]
            inverse = jnp.concatenate(inverse, axis=0)
            if upper:
                return jnp.concatenate([own, halo], axis=0) * inverse[margin:]
            return jnp.concatenate([halo, own], axis=0) * inverse[: inverse.shape[0] - margin]

        def emit(_, z, value, v=v):
            if v > 0:
                value = value * product_ref[z]
            product_ref[z] = value
            if v == views - 1:
                for top in range(0, value.shape[0], 8):
                    most[0] = jnp.maximum(most[0], value[top : top + 8])

        z_view = z_ref.at[1, v * tall : (v + 1) * tall]
        filter_to(
            load,
            1,
            1,
            z_view,
            x_ref.at[1, v : v + 1],
            y_ref.at[1, v : v + 1],
            scale_ref.at[v : v + 1],
            e_ref,
            g_ref,
            True,
            emit,
        )
    top = jnp.maximum(jnp.max(most[0], axis=(0, 1), keepdims=True), 1e-30)
    quarter = jnp.ceil(jnp.log2(top) * 0.25)
    scale = jnp.exp2(-4.0 * quarter)
    root = jnp.broadcast_to(jnp.exp2(quarter), (part, product_ref.shape[2]))
    for z in range(planes):
        value = product_ref[z] * scale
        for b in range(4):
            (keep_ref, send_ref)[b % 2][b // 2, z] = value[b * part : (b + 1) * part]
    for ref in (keep_ref, send_ref):
        for b in range(2):
            ref[b, planes] = root


def local(estimate, recordings, psf_taps):
    planes, rows, cols = estimate.shape
    taps = psf_taps.shape[-1]
    margin = (taps - 1) // 2
    views = recordings.shape[0]
    devices = lax.axis_size("gz")
    place = lax.axis_index("view")
    place_array = place.reshape(1).astype(jnp.int32)
    up = [(i, i + 1) for i in range(devices - 1)]
    down = [(i + 1, i) for i in range(devices - 1)]
    swap = [(i, i ^ 1) for i in range(4)]
    z_out = planes // 2
    shape = jax.ShapeDtypeStruct

    rounded = estimate.astype(BF16)
    both_ways = [(4 * i + w, 4 * j + w) for w in (0, 2) for i, j in up]
    both_ways += [(4 * i + w, 4 * j + w) for w in (1, 3) for i, j in down]
    mine = lax.ppermute(rounded, ("gz", "view"), both_ways)

    last, first = pl.pallas_call(
        edges_kernel,
        out_shape=[shape((views, margin, rows, cols), BF16)] * 2,
        in_specs=[HBM],
        out_specs=[HBM] * 2,
        scratch_shapes=[
            pltpu.VMEM((2 * views, margin, rows, cols), BF16),
            pltpu.SemaphoreType.DMA((2, 2 * views)),
        ],
        name="edges",
        **params(10**4, 10**4, 58 * 1024 * 1024),
    )(recordings)
    before = lax.ppermute(last, "gz", up)
    after = lax.ppermute(first, "gz", down)

    wide = -(-(z_out + taps - 1) * 8 // 128) * 128
    z_mat, x_mat, y_mat, scales = pl.pallas_call(
        matrices_kernel,
        out_shape=[
            shape((2, views * 2 * z_out * 8, wide), BF16),
            shape((2, views, 2 * cols, 2 * cols), BF16),
            shape((2, views, rows, 2 * rows), BF16),
            shape((views, 2, 1, 128), F32),
        ],
        in_specs=[SMEM, SMEM],
        out_specs=[VMEM] * 4,
        name="matrices",
        **params(10**6, 10**4),
    )(place_array, psf_taps)

    mine, z_mat = lax.optimization_barrier((mine, z_mat))
    mine = (mine[:margin], mine[margin:])
    other = [lax.ppermute(piece, "view", swap) for piece in mine]
    inverses = []
    for early, side in ((True, mine), (False, other)):
        inverses.append(
            pl.pallas_call(
                lambda *refs, early=early: inverse_kernel(early, *refs),
                out_shape=shape((views, planes, rows, cols), F32),
                in_specs=[SMEM] + [VMEM] * 7,
                out_specs=VMEM,
                scratch_shapes=scratch(views, 2, 1, z_out, rows, cols),
                name="inverses",
                **params(10**6, 10**4),
            )(place_array, *side, rounded, z_mat, x_mat, y_mat, scales)
        )
    part = rows // 4
    halves = []
    for upper, halo in ((True, after), (False, before)):
        halves.append(
            pl.pallas_call(
                lambda *refs, upper=upper: correction_kernel(upper, *refs),
                out_shape=[shape((2, z_out + 1, part, cols), F32)] * 2,
                in_specs=[SMEM] + [VMEM] * 8,
                out_specs=[VMEM] * 2,
                scratch_shapes=scratch(1, 1, 2, z_out, rows, cols) + [pltpu.VMEM((z_out, rows, cols), F32)],
                name="corrections",
                **params(2 * 10**9, 2 * 10**6),
            )(place_array, halo, recordings, *inverses, z_mat, x_mat, y_mat, scales)
        )
    own_rows = lax.dynamic_slice_in_dim(estimate, place * part, part, 1)
    cores = [lax.ppermute(send, "view", swap) for _, send in halves]
    outs = []
    for half, ((keep, _), core) in enumerate(zip(halves, cores)):
        across = lax.ppermute((keep[1] * core[1]).astype(jnp.float16), "view", [(i, i ^ 2) for i in range(4)])
        root = keep[0, z_out] * core[0, z_out]
        partial = own_rows[(1 - half) * z_out : (2 - half) * z_out] * (keep[0, :z_out] * core[0, :z_out])
        outs.append((partial, root, across))
    outs = lax.optimization_barrier(outs)
    results = []
    for partial, root, across in outs:
        root = root * across[z_out].astype(F32)
        results.append(partial * (across[:z_out].astype(F32) * (root * root * root * root)))
    return jnp.concatenate(results[::-1], axis=0)


def solution(mesh):
    in_specs = (P("gz", None, None), P("view", "gz", None, None), P("view", None, None, None))
    out_specs = P("gz", "view", None)
    return jax.shard_map(local, mesh=mesh, in_specs=in_specs, out_specs=out_specs, check_vma=False)
```

```python
import jax
import jax.numpy as jnp
from jax import lax
from jax.experimental import pallas as pl
from jax.experimental.pallas import tpu as pltpu
from jax.sharding import PartitionSpec as P

F32 = jnp.float32
BF16 = jnp.bfloat16
VMEM = pl.BlockSpec(memory_space=pltpu.VMEM)
HBM = pl.BlockSpec(memory_space=pltpu.HBM)
SMEM = pl.BlockSpec(memory_space=pltpu.SMEM)
LIMIT = 20 * 1024 * 1024


def split(value):
    high = value.astype(BF16)
    return high, (value - high.astype(F32)).astype(BF16)


def params(flops, nbytes, limit=LIMIT):
    return dict(
        compiler_params=pltpu.CompilerParams(vmem_limit_bytes=limit),
        cost_estimate=pl.CostEstimate(flops=flops, bytes_accessed=nbytes, transcendentals=0),
    )


def edges_kernel(rec_ref, last_out, first_out, held, sems):
    views, planes = rec_ref.shape[:2]
    margin = last_out.shape[1]
    copies, outs = [], []
    for v in range(views):
        for out, begin in ((last_out, planes - margin), (first_out, 0)):
            i = len(copies)
            copies.append(pltpu.make_async_copy(rec_ref.at[v, pl.ds(begin, margin)], held.at[i], sems.at[0, i]))
            outs.append(pltpu.make_async_copy(held.at[i], out.at[v], sems.at[1, i]))
    for copy in copies:
        copy.start()
    for copy, out in zip(copies, outs):
        copy.wait()
        out.start()
    for out in outs:
        out.wait()


def rounded_scale(tap, total):
    factor = jnp.exp2(lax.broadcasted_iota(jnp.int32, (1, 128), 1).astype(F32) * (1.0 / 128.0))
    scale = factor / jnp.full((1, 128), total, F32)
    sums, running = [], jnp.zeros((1, 128), F32)
    for value in tap:
        exact = value * scale
        running = running + (exact.astype(BF16).astype(F32) - exact)
        sums.append(running)
    error = jnp.zeros((1, 128), F32)
    for partial in sums:
        rest = running - partial
        error = error + partial * partial + rest * rest
    error = error / (factor * factor)
    best = error == jnp.min(error, axis=1, keepdims=True)
    factor = jnp.max(jnp.where(best, factor, 0.0), axis=1, keepdims=True)
    scale = jnp.max(jnp.where(best, scale, 0.0), axis=1, keepdims=True)
    return jnp.broadcast_to(scale, (1, 128)), jnp.broadcast_to(factor, (1, 128))


def matrices_kernel(place_ref, taps_ref, z_ref, x_ref, y_ref, scale_ref):
    views, taps = taps_ref.shape[0], taps_ref.shape[3]
    half = (taps - 1) // 2
    rows = x_ref.shape[2] // 2
    place = place_ref[0]
    zeros = jnp.zeros((rows, rows), BF16)

    for v in range(views):
        tap = {
            (d, r): [taps_ref[v, d, r, j] for j in range(taps)] for d in range(3) for r in range(2)
        }
        scale = {}
        for r in range(2):
            undo = jnp.ones((1, 128), F32)
            for d in range(3):
                values = tap[d, r] if d < 2 else tap[2, 0] + tap[2, 1]
                total = values[0]
                for value in values[1:]:
                    total = total + value
                scale[d, r], factor = rounded_scale(tap[d, r], total)
                undo = undo / factor
            scale_ref[v, r] = undo
        for direction in range(2):
            for r in range(2):
                other = 1 - r
                x_ref[direction, v, r * rows : (r + 1) * rows, other * rows : (other + 1) * rows] = zeros
        step = 32
        for first in range(0, rows, step):
            diff = (
                lax.broadcasted_iota(jnp.int32, (step, rows), 0)
                - lax.broadcasted_iota(jnp.int32, (step, rows), 1)
                + (first + half)
            )
            made = {(d, r, m): jnp.zeros((step, rows), F32) for d in range(2) for r in range(2) for m in range(2)}
            for j in range(taps):
                here = diff == j
                for d, r, m in made:
                    pick = tap[d, r][j] if m == 0 else tap[d, r][taps - 1 - j]
                    made[d, r, m] = jnp.where(here, pick, made[d, r, m])
            for (d, r, m), value in made.items():
                value = (value * scale[d, r]).astype(BF16)
                lanes = slice(r * rows, (r + 1) * rows)
                if d == 0:
                    x_ref[m, v, r * rows + first : r * rows + first + step, lanes] = value
                elif m == 1:
                    y_ref[0, v, first : first + step, lanes] = value
                else:
                    target = pl.multiple_of(jnp.bitwise_xor(first // step, place) * step, step)
                    y_ref[1, v, pl.ds(target, step), lanes] = value
        tall = z_ref.shape[1] // (2 * views)
        wide = z_ref.shape[2]
        step = 16
        for first in range(0, tall, step):
            diff = (
                lax.broadcasted_iota(jnp.int32, (step, wide), 1)
                - lax.broadcasted_iota(jnp.int32, (step, wide), 0)
                - first
            )
            made = {(r, m): jnp.zeros((step, wide), F32) for r in range(2) for m in range(2)}
            for j in range(taps):
                here = diff == 8 * j
                for r, m in made:
                    pick = tap[2, r][j] if m == 0 else tap[2, r][taps - 1 - j]
                    made[r, m] = jnp.where(here, pick, made[r, m])
            for (r, m), value in made.items():
                top = (2 * v + r) * tall + first
                z_ref[m, top : top + step, :] = (value * scale[2, r][0:1, 0:1]).astype(BF16)


def dot(a, b):
    return jnp.dot(a, b, preferred_element_type=F32)


CHUNK = 4


def inverted(value):
    guess = pl.reciprocal(value, approx=True)
    return guess * (2.0 - value * guess)


def filter_to(load, views, groups, z_ref, x_ref, y_ref, scale_ref, e_ref, g_ref, exact, emit):
    tall = z_ref.shape[0] // (2 * views)
    z_out = tall // 8
    rows = y_ref.shape[1]
    for pair in range(rows // 16):
        block = load(slice(pair * 16, pair * 16 + 16))
        planes = block.shape[0]
        depth = (planes - (groups - 1) * z_out) * 8
        octets = [block[:, 8 * o : 8 * o + 8, :].reshape(planes * 8, rows).astype(BF16) for o in range(2)]
        octets = jnp.concatenate(octets, axis=1)
        for part in range(groups):
            data = octets[part * z_out * 8 : part * z_out * 8 + depth]
            all_e = dot(z_ref[:, :depth], data)
            for v in range(views):
                for r in range(2):
                    top = (2 * v + r) * tall
                    e = all_e[top : top + tall]
                    e = jnp.concatenate([e[:, :rows], e[:, rows:]], axis=0)
                    lanes = slice(r * rows, (r + 1) * rows)
                    if exact:
                        high, low = split(e)
                        e_ref[v, 0, pair * groups + part, :, lanes] = high
                        e_ref[v, 1, pair * groups + part, :, lanes] = low
                    else:
                        e_ref[v, 0, pair * groups + part, :, lanes] = e.astype(BF16)
    for v in range(views):
        for first in range(0, rows // 16 * groups, CHUNK):
            e = e_ref[v, 0, first : first + CHUNK].reshape(CHUNK * 2 * tall, 2 * rows)
            all_g = dot(e, x_ref[v])
            if exact:
                e = e_ref[v, 1, first : first + CHUNK].reshape(CHUNK * 2 * tall, 2 * rows)
                all_g = all_g + dot(e, x_ref[v])
            for index in range(first, first + CHUNK):
                pair, part = index // groups, index % groups
                g = all_g[(index - first) * 2 * tall : (index - first + 1) * 2 * tall]
                for r in range(2):
                    lanes = slice(r * rows, (r + 1) * rows)
                    g_rows = jnp.concatenate(
                        [g[o * tall : (o + 1) * tall, lanes].reshape(z_out, 8, rows) for o in range(2)], axis=1
                    )
                    g_rows = g_rows * scale_ref[v, r]
                    target = slice(r * rows + pair * 16, r * rows + pair * 16 + 16)
                    planes_at = slice(part * z_out, (part + 1) * z_out)
                    if exact:
                        high, low = split(g_rows)
                        g_ref[v, 0, planes_at, target, :] = high
                        g_ref[v, 1, planes_at, target, :] = low
                    else:
                        g_ref[v, 0, planes_at, target, :] = g_rows.astype(BF16)
    for v in range(views):
        for z in range(0, groups * z_out, 2):
            data = jnp.concatenate([g_ref[v, 0, z], g_ref[v, 0, z + 1]], axis=1)
            out = dot(y_ref[v], data)
            if exact:
                data = jnp.concatenate([g_ref[v, 1, z], g_ref[v, 1, z + 1]], axis=1)
                out = out + dot(y_ref[v], data)
            emit(v, z, out[:, :rows])
            emit(v, z + 1, out[:, rows:])


def scratch(views, groups, halves, z_out, rows, cols):
    return [
        pltpu.VMEM((views, halves, rows // 16 * groups, 2 * z_out * 8, 2 * cols), BF16),
        pltpu.VMEM((views, halves, groups * z_out, 2 * rows, cols), BF16),
    ]


def inverse_kernel(early, place_ref, low_ref, high_ref, own_ref, z_ref, x_ref, y_ref, scale_ref, out_ref, e_ref, g_ref):
    side_first = (place_ref[0] % 2 == 0) == early

    def load(at):
        side = jnp.concatenate([low_ref[:, at, :], high_ref[:, at, :]], axis=0).astype(F32)
        own = own_ref[:, at, :].astype(F32)
        return jnp.concatenate([jnp.where(side_first, side, own), jnp.where(side_first, own, side)], axis=0)

    def emit(v, z, blurred):
        out_ref[v, z] = inverted(blurred)

    views = out_ref.shape[0]
    filter_to(load, views, 2, z_ref.at[0], x_ref.at[0], y_ref.at[0], scale_ref, e_ref, g_ref, False, emit)


def arrange_kernel(place_ref, rec_ref, early_ref, late_ref, own_out, rim_out):
    views, planes = rec_ref.shape[:2]
    half = planes // 2
    early_first = place_ref[0] % 2 == 0
    for v in range(views):
        for z in range(planes):
            early, late = early_ref[v, z], late_ref[v, z]
            first, second = jnp.where(early_first, early, late), jnp.where(early_first, late, early)
            if z < half:
                rim_out[v, 0, z] = first
                own_out[v, half + z] = (rec_ref[v, half + z].astype(F32) * second).astype(BF16)
            else:
                own_out[v, z - half] = (rec_ref[v, z - half].astype(F32) * first).astype(BF16)
                rim_out[v, 1, z - half] = second


def correction_kernel(
    before_ref,
    own_ref,
    after_ref,
    rim_ref,
    z_ref,
    x_ref,
    y_ref,
    scale_ref,
    keep_ref,
    send_ref,
    e_ref,
    g_ref,
    product_ref,
):
    views, planes = own_ref.shape[:2]
    part = keep_ref.shape[2]
    tall = z_ref.shape[1] // views
    most = [jnp.zeros((8, product_ref.shape[2]), F32)]
    for v in range(views):

        def load(at, v=v):
            before = before_ref[v, :, at, :].astype(F32) * rim_ref[v, 0, :, at, :]
            after = after_ref[v, :, at, :].astype(F32) * rim_ref[v, 1, :, at, :]
            return jnp.concatenate([before, own_ref[v, :, at, :].astype(F32), after], axis=0)

        def emit(_, z, value, v=v):
            if v > 0:
                value = value * product_ref[z]
            product_ref[z] = value
            if v == views - 1:
                for top in range(0, value.shape[0], 8):
                    most[0] = jnp.maximum(most[0], value[top : top + 8])

        z_view = z_ref.at[1, v * tall : (v + 1) * tall]
        filter_to(
            load,
            1,
            2,
            z_view,
            x_ref.at[1, v : v + 1],
            y_ref.at[1, v : v + 1],
            scale_ref.at[v : v + 1],
            e_ref,
            g_ref,
            True,
            emit,
        )
    top = jnp.maximum(jnp.max(most[0], axis=(0, 1), keepdims=True), 1e-30)
    quarter = jnp.ceil(jnp.log2(top) * 0.25)
    scale = jnp.exp2(-4.0 * quarter)
    root = jnp.broadcast_to(jnp.exp2(quarter), (part, product_ref.shape[2]))
    for z in range(planes):
        value = product_ref[z] * scale
        for b in range(4):
            (keep_ref, send_ref)[b % 2][b // 2, z] = value[b * part : (b + 1) * part]
    for ref in (keep_ref, send_ref):
        for b in range(2):
            ref[b, planes] = root


def local(estimate, recordings, psf_taps):
    planes, rows, cols = estimate.shape
    taps = psf_taps.shape[-1]
    margin = (taps - 1) // 2
    views = recordings.shape[0]
    devices = lax.axis_size("gz")
    place = lax.axis_index("view")
    place_array = place.reshape(1).astype(jnp.int32)
    up = [(i, i + 1) for i in range(devices - 1)]
    down = [(i + 1, i) for i in range(devices - 1)]
    swap = [(i, i ^ 1) for i in range(4)]
    z_out = planes // 2
    shape = jax.ShapeDtypeStruct

    rounded = estimate.astype(BF16)
    both_ways = [(4 * i + w, 4 * j + w) for w in (0, 2) for i, j in up]
    both_ways += [(4 * i + w, 4 * j + w) for w in (1, 3) for i, j in down]
    mine = lax.ppermute(rounded, ("gz", "view"), both_ways)

    last, first = pl.pallas_call(
        edges_kernel,
        out_shape=[shape((views, margin, rows, cols), BF16)] * 2,
        in_specs=[HBM],
        out_specs=[HBM] * 2,
        scratch_shapes=[
            pltpu.VMEM((2 * views, margin, rows, cols), BF16),
            pltpu.SemaphoreType.DMA((2, 2 * views)),
        ],
        name="edges",
        **params(10**4, 10**4, 58 * 1024 * 1024),
    )(recordings)
    before = lax.ppermute(last, "gz", up)
    after = lax.ppermute(first, "gz", down)

    wide = -(-(z_out + taps - 1) * 8 // 128) * 128
    z_mat, x_mat, y_mat, scales = pl.pallas_call(
        matrices_kernel,
        out_shape=[
            shape((2, views * 2 * z_out * 8, wide), BF16),
            shape((2, views, 2 * cols, 2 * cols), BF16),
            shape((2, views, rows, 2 * rows), BF16),
            shape((views, 2, 1, 128), F32),
        ],
        in_specs=[SMEM, SMEM],
        out_specs=[VMEM] * 4,
        name="matrices",
        **params(10**6, 10**4),
    )(place_array, psf_taps)

    mine, z_mat = lax.optimization_barrier((mine, z_mat))
    mine = (mine[:margin], mine[margin:])
    other = [lax.ppermute(piece, "view", swap) for piece in mine]
    inverses = []
    for early, side in ((True, mine), (False, other)):
        inverses.append(
            pl.pallas_call(
                lambda *refs, early=early: inverse_kernel(early, *refs),
                out_shape=shape((views, planes, rows, cols), F32),
                in_specs=[SMEM] + [VMEM] * 7,
                out_specs=VMEM,
                scratch_shapes=scratch(views, 2, 1, z_out, rows, cols),
                name="inverses",
                **params(10**6, 10**4),
            )(place_array, *side, rounded, z_mat, x_mat, y_mat, scales)
        )
    own, rim = pl.pallas_call(
        arrange_kernel,
        out_shape=[shape((views, planes, rows, cols), BF16), shape((views, 2, margin, rows, cols), F32)],
        in_specs=[SMEM] + [VMEM] * 3,
        out_specs=[VMEM] * 2,
        name="arrange",
        **params(10**5, 10**4),
    )(place_array, recordings, *inverses)
    part = rows // 4
    keep, send = pl.pallas_call(
        correction_kernel,
        out_shape=[shape((2, planes + 1, part, cols), F32)] * 2,
        in_specs=[VMEM] * 8,
        out_specs=[VMEM] * 2,
        scratch_shapes=scratch(1, 2, 2, z_out, rows, cols) + [pltpu.VMEM((planes, rows, cols), F32)],
        name="corrections",
        **params(4 * 10**9, 5 * 10**6),
    )(before, own, after, rim, z_mat, x_mat, y_mat, scales)
    core = lax.ppermute(send, "view", swap)
    across = lax.ppermute((keep[1] * core[1]).astype(jnp.float16), "view", [(i, i ^ 2) for i in range(4)])
    own_rows = lax.dynamic_slice_in_dim(estimate, place * part, part, 1)
    root = keep[0, planes] * core[0, planes]
    partial = own_rows * (keep[0, :planes] * core[0, :planes])
    partial, root, across = lax.optimization_barrier((partial, root, across))
    root = root * across[planes].astype(F32)
    return partial * (across[:planes].astype(F32) * (root * root * root * root))


def solution(mesh):
    in_specs = (P("gz", None, None), P("view", "gz", None, None), P("view", None, None, None))
    out_specs = P("gz", "view", None)
    return jax.shard_map(local, mesh=mesh, in_specs=in_specs, out_specs=out_specs, check_vma=False)
```

```python
import jax
import jax.numpy as jnp
from jax import lax
from jax.experimental import pallas as pl
from jax.experimental.pallas import tpu as pltpu
from jax.sharding import PartitionSpec as P

F32 = jnp.float32
BF16 = jnp.bfloat16
VMEM = pl.BlockSpec(memory_space=pltpu.VMEM)
HBM = pl.BlockSpec(memory_space=pltpu.HBM)
SMEM = pl.BlockSpec(memory_space=pltpu.SMEM)
LIMIT = 20 * 1024 * 1024


def split(value):
    high = value.astype(BF16)
    return high, (value - high.astype(F32)).astype(BF16)


def params(flops, nbytes, limit=LIMIT):
    return dict(
        compiler_params=pltpu.CompilerParams(vmem_limit_bytes=limit),
        cost_estimate=pl.CostEstimate(flops=flops, bytes_accessed=nbytes, transcendentals=0),
    )


def edges_kernel(rec_ref, last_out, first_out, held, sems):
    views, planes = rec_ref.shape[:2]
    margin = last_out.shape[1]
    copies, outs = [], []
    for v in range(views):
        for out, begin in ((last_out, planes - margin), (first_out, 0)):
            i = len(copies)
            copies.append(pltpu.make_async_copy(rec_ref.at[v, pl.ds(begin, margin)], held.at[i], sems.at[0, i]))
            outs.append(pltpu.make_async_copy(held.at[i], out.at[v], sems.at[1, i]))
    for copy in copies:
        copy.start()
    for copy, out in zip(copies, outs):
        copy.wait()
        out.start()
    for out in outs:
        out.wait()


def rounded_scale(tap, total):
    factor = jnp.exp2(lax.broadcasted_iota(jnp.int32, (1, 128), 1).astype(F32) * (1.0 / 128.0))
    scale = factor / jnp.full((1, 128), total, F32)
    sums, running = [], jnp.zeros((1, 128), F32)
    for value in tap:
        exact = value * scale
        running = running + (exact.astype(BF16).astype(F32) - exact)
        sums.append(running)
    error = jnp.zeros((1, 128), F32)
    for partial in sums:
        rest = running - partial
        error = error + partial * partial + rest * rest
    error = error / (factor * factor)
    best = error == jnp.min(error, axis=1, keepdims=True)
    factor = jnp.max(jnp.where(best, factor, 0.0), axis=1, keepdims=True)
    scale = jnp.max(jnp.where(best, scale, 0.0), axis=1, keepdims=True)
    return jnp.broadcast_to(scale, (1, 128)), jnp.broadcast_to(factor, (1, 128))


def matrices_kernel(place_ref, taps_ref, z_ref, x_ref, y_ref, scale_ref):
    views, taps = taps_ref.shape[0], taps_ref.shape[3]
    half = (taps - 1) // 2
    rows = x_ref.shape[2] // 2
    place = place_ref[0]
    zeros = jnp.zeros((rows, rows), BF16)

    for v in range(views):
        tap = {
            (d, r): [taps_ref[v, d, r, j] for j in range(taps)] for d in range(3) for r in range(2)
        }
        scale = {}
        for r in range(2):
            undo = jnp.ones((1, 128), F32)
            for d in range(3):
                values = tap[d, r] if d < 2 else tap[2, 0] + tap[2, 1]
                total = values[0]
                for value in values[1:]:
                    total = total + value
                scale[d, r], factor = rounded_scale(tap[d, r], total)
                undo = undo / factor
            scale_ref[v, r] = undo
        for direction in range(2):
            for r in range(2):
                other = 1 - r
                x_ref[direction, v, r * rows : (r + 1) * rows, other * rows : (other + 1) * rows] = zeros
        step = 32
        for first in range(0, rows, step):
            diff = (
                lax.broadcasted_iota(jnp.int32, (step, rows), 0)
                - lax.broadcasted_iota(jnp.int32, (step, rows), 1)
                + (first + half)
            )
            made = {(d, r, m): jnp.zeros((step, rows), F32) for d in range(2) for r in range(2) for m in range(2)}
            for j in range(taps):
                here = diff == j
                for d, r, m in made:
                    pick = tap[d, r][j] if m == 0 else tap[d, r][taps - 1 - j]
                    made[d, r, m] = jnp.where(here, pick, made[d, r, m])
            for (d, r, m), value in made.items():
                value = (value * scale[d, r]).astype(BF16)
                lanes = slice(r * rows, (r + 1) * rows)
                if d == 0:
                    x_ref[m, v, r * rows + first : r * rows + first + step, lanes] = value
                elif m == 1:
                    y_ref[0, v, first : first + step, lanes] = value
                else:
                    target = pl.multiple_of(jnp.bitwise_xor(first // step, place) * step, step)
                    y_ref[1, v, pl.ds(target, step), lanes] = value
        tall = z_ref.shape[1] // (2 * views)
        wide = z_ref.shape[2]
        step = 16
        for first in range(0, tall, step):
            diff = (
                lax.broadcasted_iota(jnp.int32, (step, wide), 1)
                - lax.broadcasted_iota(jnp.int32, (step, wide), 0)
                - first
            )
            made = {(r, m): jnp.zeros((step, wide), F32) for r in range(2) for m in range(2)}
            for j in range(taps):
                here = diff == 8 * j
                for r, m in made:
                    pick = tap[2, r][j] if m == 0 else tap[2, r][taps - 1 - j]
                    made[r, m] = jnp.where(here, pick, made[r, m])
            for (r, m), value in made.items():
                top = (2 * v + r) * tall + first
                z_ref[m, top : top + step, :] = (value * scale[2, r][0:1, 0:1]).astype(BF16)


def dot(a, b):
    return jnp.dot(a, b, preferred_element_type=F32)


CHUNK = 4


def inverted(value):
    guess = pl.reciprocal(value, approx=True)
    return guess * (2.0 - value * guess)


def filter_to(load, views, groups, z_ref, x_ref, y_ref, scale_ref, e_ref, g_ref, exact, emit):
    tall = z_ref.shape[0] // (2 * views)
    z_out = tall // 8
    rows = y_ref.shape[1]
    for pair in range(rows // 16):
        block = load(slice(pair * 16, pair * 16 + 16))
        planes = block.shape[0]
        depth = (planes - (groups - 1) * z_out) * 8
        octets = [block[:, 8 * o : 8 * o + 8, :].reshape(planes * 8, rows).astype(BF16) for o in range(2)]
        octets = jnp.concatenate(octets, axis=1)
        for part in range(groups):
            data = octets[part * z_out * 8 : part * z_out * 8 + depth]
            all_e = dot(z_ref[:, :depth], data)
            for v in range(views):
                for r in range(2):
                    top = (2 * v + r) * tall
                    e = all_e[top : top + tall]
                    e = jnp.concatenate([e[:, :rows], e[:, rows:]], axis=0)
                    lanes = slice(r * rows, (r + 1) * rows)
                    if exact:
                        high, low = split(e)
                        e_ref[v, 0, pair * groups + part, :, lanes] = high
                        e_ref[v, 1, pair * groups + part, :, lanes] = low
                    else:
                        e_ref[v, 0, pair * groups + part, :, lanes] = e.astype(BF16)
    for v in range(views):
        for first in range(0, rows // 16 * groups, CHUNK):
            e = e_ref[v, 0, first : first + CHUNK].reshape(CHUNK * 2 * tall, 2 * rows)
            all_g = dot(e, x_ref[v])
            if exact:
                e = e_ref[v, 1, first : first + CHUNK].reshape(CHUNK * 2 * tall, 2 * rows)
                all_g = all_g + dot(e, x_ref[v])
            for index in range(first, first + CHUNK):
                pair, part = index // groups, index % groups
                g = all_g[(index - first) * 2 * tall : (index - first + 1) * 2 * tall]
                for r in range(2):
                    lanes = slice(r * rows, (r + 1) * rows)
                    g_rows = jnp.concatenate(
                        [g[o * tall : (o + 1) * tall, lanes].reshape(z_out, 8, rows) for o in range(2)], axis=1
                    )
                    g_rows = g_rows * scale_ref[v, r]
                    target = slice(r * rows + pair * 16, r * rows + pair * 16 + 16)
                    planes_at = slice(part * z_out, (part + 1) * z_out)
                    if exact:
                        high, low = split(g_rows)
                        g_ref[v, 0, planes_at, target, :] = high
                        g_ref[v, 1, planes_at, target, :] = low
                    else:
                        g_ref[v, 0, planes_at, target, :] = g_rows.astype(BF16)
    for v in range(views):
        for z in range(0, groups * z_out, 2):
            data = jnp.concatenate([g_ref[v, 0, z], g_ref[v, 0, z + 1]], axis=1)
            out = dot(y_ref[v], data)
            if exact:
                data = jnp.concatenate([g_ref[v, 1, z], g_ref[v, 1, z + 1]], axis=1)
                out = out + dot(y_ref[v], data)
            emit(v, z, out[:, :rows])
            emit(v, z + 1, out[:, rows:])


def scratch(views, groups, halves, z_out, rows, cols):
    return [
        pltpu.VMEM((views, halves, rows // 16 * groups, 2 * z_out * 8, 2 * cols), BF16),
        pltpu.VMEM((views, halves, groups * z_out, 2 * rows, cols), BF16),
    ]


def inverse_kernel(early, place_ref, low_ref, high_ref, own_ref, z_ref, x_ref, y_ref, scale_ref, out_ref, e_ref, g_ref):
    side_first = (place_ref[0] % 2 == 0) == early

    def load(at):
        side = jnp.concatenate([low_ref[:, at, :], high_ref[:, at, :]], axis=0).astype(F32)
        own = own_ref[:, at, :].astype(F32)
        return jnp.concatenate([jnp.where(side_first, side, own), jnp.where(side_first, own, side)], axis=0)

    def emit(v, z, blurred):
        out_ref[v, z] = inverted(blurred)

    views = out_ref.shape[0]
    filter_to(load, views, 2, z_ref.at[0], x_ref.at[0], y_ref.at[0], scale_ref, e_ref, g_ref, False, emit)


def arrange_kernel(place_ref, rec_ref, early_ref, late_ref, own_out, rim_out):
    views, planes = rec_ref.shape[:2]
    half = planes // 2
    early_first = place_ref[0] % 2 == 0
    for v in range(views):
        for z in range(planes):
            early, late = early_ref[v, z], late_ref[v, z]
            first, second = jnp.where(early_first, early, late), jnp.where(early_first, late, early)
            if z < half:
                rim_out[v, 0, z] = first
                own_out[v, half + z] = (rec_ref[v, half + z].astype(F32) * second).astype(BF16)
            else:
                own_out[v, z - half] = (rec_ref[v, z - half].astype(F32) * first).astype(BF16)
                rim_out[v, 1, z - half] = second


def correction_kernel(
    before_ref,
    own_ref,
    after_ref,
    rim_ref,
    z_ref,
    x_ref,
    y_ref,
    scale_ref,
    keep_ref,
    near_ref,
    far_ref,
    e_ref,
    g_ref,
    product_ref,
):
    views, planes = own_ref.shape[:2]
    part = keep_ref.shape[2]
    tall = z_ref.shape[1] // views
    most = [jnp.zeros((8, product_ref.shape[2]), F32)]
    for v in range(views):

        def load(at, v=v):
            before = before_ref[v, :, at, :].astype(F32) * rim_ref[v, 0, :, at, :]
            after = after_ref[v, :, at, :].astype(F32) * rim_ref[v, 1, :, at, :]
            return jnp.concatenate([before, own_ref[v, :, at, :].astype(F32), after], axis=0)

        def emit(_, z, value, v=v):
            if v > 0:
                value = value * product_ref[z]
            product_ref[z] = value
            if v == views - 1:
                for top in range(0, value.shape[0], 8):
                    most[0] = jnp.maximum(most[0], value[top : top + 8])

        z_view = z_ref.at[1, v * tall : (v + 1) * tall]
        filter_to(
            load,
            1,
            2,
            z_view,
            x_ref.at[1, v : v + 1],
            y_ref.at[1, v : v + 1],
            scale_ref.at[v : v + 1],
            e_ref,
            g_ref,
            True,
            emit,
        )
    top = jnp.maximum(jnp.max(most[0], axis=(0, 1), keepdims=True), 1e-30)
    quarter = jnp.ceil(jnp.log2(top) * 0.25)
    scale = jnp.exp2(-4.0 * quarter)
    root = jnp.broadcast_to(jnp.exp2(quarter), (part, product_ref.shape[2]))
    targets = (keep_ref.at[0], near_ref, keep_ref.at[1], far_ref)
    for z in range(planes):
        value = product_ref[z] * scale
        for b in range(4):
            targets[b][z] = value[b * part : (b + 1) * part]
    for target in targets:
        target[planes] = root


def local(estimate, recordings, psf_taps):
    planes, rows, cols = estimate.shape
    taps = psf_taps.shape[-1]
    margin = (taps - 1) // 2
    views = recordings.shape[0]
    devices = lax.axis_size("gz")
    place = lax.axis_index("view")
    place_array = place.reshape(1).astype(jnp.int32)
    up = [(i, i + 1) for i in range(devices - 1)]
    down = [(i + 1, i) for i in range(devices - 1)]
    swap = [(i, i ^ 1) for i in range(4)]
    z_out = planes // 2
    shape = jax.ShapeDtypeStruct

    rounded = estimate.astype(BF16)
    both_ways = [(4 * i + w, 4 * j + w) for w in (0, 2) for i, j in up]
    both_ways += [(4 * i + w, 4 * j + w) for w in (1, 3) for i, j in down]
    mine = lax.ppermute(rounded, ("gz", "view"), both_ways)

    last, first = pl.pallas_call(
        edges_kernel,
        out_shape=[shape((views, margin, rows, cols), BF16)] * 2,
        in_specs=[HBM],
        out_specs=[HBM] * 2,
        scratch_shapes=[
            pltpu.VMEM((2 * views, margin, rows, cols), BF16),
            pltpu.SemaphoreType.DMA((2, 2 * views)),
        ],
        name="edges",
        **params(10**4, 10**4, 58 * 1024 * 1024),
    )(recordings)
    before = lax.ppermute(last, "gz", up)
    after = lax.ppermute(first, "gz", down)

    wide = -(-(z_out + taps - 1) * 8 // 128) * 128
    z_mat, x_mat, y_mat, scales = pl.pallas_call(
        matrices_kernel,
        out_shape=[
            shape((2, views * 2 * z_out * 8, wide), BF16),
            shape((2, views, 2 * cols, 2 * cols), BF16),
            shape((2, views, rows, 2 * rows), BF16),
            shape((views, 2, 1, 128), F32),
        ],
        in_specs=[SMEM, SMEM],
        out_specs=[VMEM] * 4,
        name="matrices",
        **params(10**6, 10**4),
    )(place_array, psf_taps)

    mine, z_mat = lax.optimization_barrier((mine, z_mat))
    mine = (mine[:margin], mine[margin:])
    other = [lax.ppermute(piece, "view", swap) for piece in mine]
    inverses = []
    for early, side in ((True, mine), (False, other)):
        inverses.append(
            pl.pallas_call(
                lambda *refs, early=early: inverse_kernel(early, *refs),
                out_shape=shape((views, planes, rows, cols), F32),
                in_specs=[SMEM] + [VMEM] * 7,
                out_specs=VMEM,
                scratch_shapes=scratch(views, 2, 1, z_out, rows, cols),
                name="inverses",
                **params(10**6, 10**4),
            )(place_array, *side, rounded, z_mat, x_mat, y_mat, scales)
        )
    own, rim = pl.pallas_call(
        arrange_kernel,
        out_shape=[shape((views, planes, rows, cols), BF16), shape((views, 2, margin, rows, cols), F32)],
        in_specs=[SMEM] + [VMEM] * 3,
        out_specs=[VMEM] * 2,
        name="arrange",
        **params(10**5, 10**4),
    )(place_array, recordings, *inverses)
    part = rows // 4
    keep, near, far = pl.pallas_call(
        correction_kernel,
        out_shape=[shape((2, planes + 1, part, cols), F32)] + [shape((planes + 1, part, cols), F32)] * 2,
        in_specs=[VMEM] * 8,
        out_specs=[VMEM] * 3,
        scratch_shapes=scratch(1, 2, 2, z_out, rows, cols) + [pltpu.VMEM((planes, rows, cols), F32)],
        name="corrections",
        **params(4 * 10**9, 5 * 10**6),
    )(before, own, after, rim, z_mat, x_mat, y_mat, scales)
    core_far = lax.ppermute(far, "view", swap)
    core_near = lax.ppermute(near, "view", swap)
    across = lax.ppermute((keep[1] * core_far).astype(jnp.float16), "view", [(i, i ^ 2) for i in range(4)])
    own_rows = lax.dynamic_slice_in_dim(estimate, place * part, part, 1)
    root = keep[0, planes] * core_near[planes]
    partial = own_rows * (keep[0, :planes] * core_near[:planes])
    partial, root, across = lax.optimization_barrier((partial, root, across))
    root = root * across[planes].astype(F32)
    return partial * (across[:planes].astype(F32) * (root * root * root * root))


def solution(mesh):
    in_specs = (P("gz", None, None), P("view", "gz", None, None), P("view", None, None, None))
    out_specs = P("gz", "view", None)
    return jax.shard_map(local, mesh=mesh, in_specs=in_specs, out_specs=out_specs, check_vma=False)
```

```python
import jax
import jax.numpy as jnp
from jax import lax
from jax.experimental import pallas as pl
from jax.experimental.pallas import tpu as pltpu
from jax.sharding import PartitionSpec as P

F32 = jnp.float32
BF16 = jnp.bfloat16
VMEM = pl.BlockSpec(memory_space=pltpu.VMEM)
HBM = pl.BlockSpec(memory_space=pltpu.HBM)
SMEM = pl.BlockSpec(memory_space=pltpu.SMEM)
LIMIT = 20 * 1024 * 1024


def split(value):
    high = value.astype(BF16)
    return high, (value - high.astype(F32)).astype(BF16)


def params(flops, nbytes, limit=LIMIT):
    return dict(
        compiler_params=pltpu.CompilerParams(vmem_limit_bytes=limit),
        cost_estimate=pl.CostEstimate(flops=flops, bytes_accessed=nbytes, transcendentals=0),
    )


def edges_kernel(rec_ref, last_out, first_out, held, sems):
    views, planes = rec_ref.shape[:2]
    margin = last_out.shape[1]
    copies, outs = [], []
    for v in range(views):
        for out, begin in ((last_out, planes - margin), (first_out, 0)):
            i = len(copies)
            copies.append(pltpu.make_async_copy(rec_ref.at[v, pl.ds(begin, margin)], held.at[i], sems.at[0, i]))
            outs.append(pltpu.make_async_copy(held.at[i], out.at[v], sems.at[1, i]))
    for copy in copies:
        copy.start()
    for copy, out in zip(copies, outs):
        copy.wait()
        out.start()
    for out in outs:
        out.wait()


def rounded_scale(tap, total):
    factor = jnp.exp2(lax.broadcasted_iota(jnp.int32, (1, 128), 1).astype(F32) * (1.0 / 128.0))
    scale = factor / jnp.full((1, 128), total, F32)
    sums, running = [], jnp.zeros((1, 128), F32)
    for value in tap:
        exact = value * scale
        running = running + (exact.astype(BF16).astype(F32) - exact)
        sums.append(running)
    error = jnp.zeros((1, 128), F32)
    for partial in sums:
        rest = running - partial
        error = error + partial * partial + rest * rest
    error = error / (factor * factor)
    best = error == jnp.min(error, axis=1, keepdims=True)
    factor = jnp.max(jnp.where(best, factor, 0.0), axis=1, keepdims=True)
    scale = jnp.max(jnp.where(best, scale, 0.0), axis=1, keepdims=True)
    return jnp.broadcast_to(scale, (1, 128)), jnp.broadcast_to(factor, (1, 128))


def matrices_kernel(place_ref, taps_ref, z_ref, x_ref, y_ref, scale_ref):
    views, taps = taps_ref.shape[0], taps_ref.shape[3]
    half = (taps - 1) // 2
    rows = x_ref.shape[2] // 2
    place = place_ref[0]
    zeros = jnp.zeros((rows, rows), BF16)

    for v in range(views):
        tap = {
            (d, r): [taps_ref[v, d, r, j] for j in range(taps)] for d in range(3) for r in range(2)
        }
        scale = {}
        for r in range(2):
            undo = jnp.ones((1, 128), F32)
            for d in range(3):
                values = tap[d, r] if d < 2 else tap[2, 0] + tap[2, 1]
                total = values[0]
                for value in values[1:]:
                    total = total + value
                scale[d, r], factor = rounded_scale(tap[d, r], total)
                undo = undo / factor
            scale_ref[v, r] = undo
        for direction in range(2):
            for r in range(2):
                other = 1 - r
                x_ref[direction, v, r * rows : (r + 1) * rows, other * rows : (other + 1) * rows] = zeros
        step = 32
        for first in range(0, rows, step):
            diff = (
                lax.broadcasted_iota(jnp.int32, (step, rows), 0)
                - lax.broadcasted_iota(jnp.int32, (step, rows), 1)
                + (first + half)
            )
            made = {(d, r, m): jnp.zeros((step, rows), F32) for d in range(2) for r in range(2) for m in range(2)}
            for j in range(taps):
                here = diff == j
                for d, r, m in made:
                    pick = tap[d, r][j] if m == 0 else tap[d, r][taps - 1 - j]
                    made[d, r, m] = jnp.where(here, pick, made[d, r, m])
            for (d, r, m), value in made.items():
                value = (value * scale[d, r]).astype(BF16)
                lanes = slice(r * rows, (r + 1) * rows)
                if d == 0:
                    x_ref[m, v, r * rows + first : r * rows + first + step, lanes] = value
                elif m == 1:
                    y_ref[0, v, first : first + step, lanes] = value
                else:
                    target = pl.multiple_of(jnp.bitwise_xor(first // step, place) * step, step)
                    y_ref[1, v, pl.ds(target, step), lanes] = value
        tall = z_ref.shape[1] // (2 * views)
        wide = z_ref.shape[2]
        step = 16
        for first in range(0, tall, step):
            diff = (
                lax.broadcasted_iota(jnp.int32, (step, wide), 1)
                - lax.broadcasted_iota(jnp.int32, (step, wide), 0)
                - first
            )
            made = {(r, m): jnp.zeros((step, wide), F32) for r in range(2) for m in range(2)}
            for j in range(taps):
                here = diff == 8 * j
                for r, m in made:
                    pick = tap[2, r][j] if m == 0 else tap[2, r][taps - 1 - j]
                    made[r, m] = jnp.where(here, pick, made[r, m])
            for (r, m), value in made.items():
                top = (2 * v + r) * tall + first
                z_ref[m, top : top + step, :] = (value * scale[2, r][0:1, 0:1]).astype(BF16)


def dot(a, b):
    return jnp.dot(a, b, preferred_element_type=F32)


CHUNK = 4


def inverted(value):
    guess = pl.reciprocal(value, approx=True)
    return guess * (2.0 - value * guess)


def filter_to(loads, views, groups, z_ref, x_ref, y_ref, scale_ref, e_ref, g_ref, exact, emit):
    tall = z_ref.shape[0] // (2 * views)
    z_out = tall // 8
    rows = y_ref.shape[1]
    sets = len(loads)
    for pair, own in [(pair, own) for pair in range(rows // 16) for own in range(sets)]:
        block = loads[own](slice(pair * 16, pair * 16 + 16))
        of = range(views) if sets == 1 else range(own, own + 1)
        top_z, end_z = of.start * 2 * tall, of.stop * 2 * tall
        planes = block.shape[0]
        depth = (planes - (groups - 1) * z_out) * 8
        octets = [block[:, 8 * o : 8 * o + 8, :].reshape(planes * 8, rows).astype(BF16) for o in range(2)]
        octets = jnp.concatenate(octets, axis=1)
        for part in range(groups):
            data = octets[part * z_out * 8 : part * z_out * 8 + depth]
            all_e = dot(z_ref[top_z:end_z, :depth], data)
            for v in of:
                for r in range(2):
                    top = (2 * (v - of.start) + r) * tall
                    e = all_e[top : top + tall]
                    e = jnp.concatenate([e[:, :rows], e[:, rows:]], axis=0)
                    lanes = slice(r * rows, (r + 1) * rows)
                    if exact:
                        high, low = split(e)
                        e_ref[v, 0, pair * groups + part, :, lanes] = high
                        e_ref[v, 1, pair * groups + part, :, lanes] = low
                    else:
                        e_ref[v, 0, pair * groups + part, :, lanes] = e.astype(BF16)
    for v in range(views):
        for first in range(0, rows // 16 * groups, CHUNK):
            e = e_ref[v, 0, first : first + CHUNK].reshape(CHUNK * 2 * tall, 2 * rows)
            all_g = dot(e, x_ref[v])
            if exact:
                e = e_ref[v, 1, first : first + CHUNK].reshape(CHUNK * 2 * tall, 2 * rows)
                all_g = all_g + dot(e, x_ref[v])
            for index in range(first, first + CHUNK):
                pair, part = index // groups, index % groups
                g = all_g[(index - first) * 2 * tall : (index - first + 1) * 2 * tall]
                for r in range(2):
                    lanes = slice(r * rows, (r + 1) * rows)
                    g_rows = jnp.concatenate(
                        [g[o * tall : (o + 1) * tall, lanes].reshape(z_out, 8, rows) for o in range(2)], axis=1
                    )
                    g_rows = g_rows * scale_ref[v, r]
                    target = slice(r * rows + pair * 16, r * rows + pair * 16 + 16)
                    planes_at = slice(part * z_out, (part + 1) * z_out)
                    if exact:
                        high, low = split(g_rows)
                        g_ref[v, 0, planes_at, target, :] = high
                        g_ref[v, 1, planes_at, target, :] = low
                    else:
                        g_ref[v, 0, planes_at, target, :] = g_rows.astype(BF16)
    for v in range(views):
        for z in range(0, groups * z_out, 2):
            data = jnp.concatenate([g_ref[v, 0, z], g_ref[v, 0, z + 1]], axis=1)
            out = dot(y_ref[v], data)
            if exact:
                data = jnp.concatenate([g_ref[v, 1, z], g_ref[v, 1, z + 1]], axis=1)
                out = out + dot(y_ref[v], data)
            emit(v, z, out[:, :rows])
            emit(v, z + 1, out[:, rows:])


def scratch(views, groups, halves, z_out, rows, cols):
    return [
        pltpu.VMEM((views, halves, rows // 16 * groups, 2 * z_out * 8, 2 * cols), BF16),
        pltpu.VMEM((views, halves, groups * z_out, 2 * rows, cols), BF16),
    ]


def inverse_kernel(early, place_ref, low_ref, high_ref, own_ref, z_ref, x_ref, y_ref, scale_ref, out_ref, e_ref, g_ref):
    side_first = (place_ref[0] % 2 == 0) == early

    def load(at):
        side = jnp.concatenate([low_ref[:, at, :], high_ref[:, at, :]], axis=0).astype(F32)
        own = own_ref[:, at, :].astype(F32)
        return jnp.concatenate([jnp.where(side_first, side, own), jnp.where(side_first, own, side)], axis=0)

    def emit(v, z, blurred):
        out_ref[v, z] = inverted(blurred)

    views = out_ref.shape[0]
    filter_to([load], views, 2, z_ref.at[0], x_ref.at[0], y_ref.at[0], scale_ref, e_ref, g_ref, False, emit)


def arrange_kernel(place_ref, rec_ref, early_ref, late_ref, own_out, rim_out):
    views, planes = rec_ref.shape[:2]
    half = planes // 2
    early_first = place_ref[0] % 2 == 0
    for v in range(views):
        for z in range(planes):
            early, late = early_ref[v, z], late_ref[v, z]
            first, second = jnp.where(early_first, early, late), jnp.where(early_first, late, early)
            if z < half:
                rim_out[v, 0, z] = first
                own_out[v, half + z] = (rec_ref[v, half + z].astype(F32) * second).astype(BF16)
            else:
                own_out[v, z - half] = (rec_ref[v, z - half].astype(F32) * first).astype(BF16)
                rim_out[v, 1, z - half] = second


def correction_kernel(
    before_ref,
    own_ref,
    after_ref,
    rim_ref,
    z_ref,
    x_ref,
    y_ref,
    scale_ref,
    keep_ref,
    near_ref,
    far_ref,
    e_ref,
    g_ref,
    product_ref,
):
    views, planes = own_ref.shape[:2]
    part = keep_ref.shape[2]
    most = [jnp.zeros((8, product_ref.shape[2]), F32)]

    def load(at, v):
        before = before_ref[v, :, at, :].astype(F32) * rim_ref[v, 0, :, at, :]
        after = after_ref[v, :, at, :].astype(F32) * rim_ref[v, 1, :, at, :]
        return jnp.concatenate([before, own_ref[v, :, at, :].astype(F32), after], axis=0)

    def emit(v, z, value):
        if v > 0:
            value = value * product_ref[z]
        product_ref[z] = value
        if v == views - 1:
            for top in range(0, value.shape[0], 8):
                most[0] = jnp.maximum(most[0], value[top : top + 8])

    loads = [lambda at, v=v: load(at, v) for v in range(views)]
    filter_to(loads, views, 2, z_ref.at[1], x_ref.at[1], y_ref.at[1], scale_ref, e_ref, g_ref, True, emit)
    top = jnp.maximum(jnp.max(most[0], axis=(0, 1), keepdims=True), 1e-30)
    quarter = jnp.ceil(jnp.log2(top) * 0.25)
    scale = jnp.exp2(-4.0 * quarter)
    root = jnp.broadcast_to(jnp.exp2(quarter), (part, product_ref.shape[2]))
    targets = (keep_ref.at[0], near_ref, keep_ref.at[1], far_ref)
    for z in range(planes):
        value = product_ref[z] * scale
        for b in range(4):
            targets[b][z] = value[b * part : (b + 1) * part]
    for target in targets:
        target[planes] = root


def local(estimate, recordings, psf_taps):
    planes, rows, cols = estimate.shape
    taps = psf_taps.shape[-1]
    margin = (taps - 1) // 2
    views = recordings.shape[0]
    devices = lax.axis_size("gz")
    place = lax.axis_index("view")
    place_array = place.reshape(1).astype(jnp.int32)
    up = [(i, i + 1) for i in range(devices - 1)]
    down = [(i + 1, i) for i in range(devices - 1)]
    swap = [(i, i ^ 1) for i in range(4)]
    z_out = planes // 2
    shape = jax.ShapeDtypeStruct

    rounded = estimate.astype(BF16)
    both_ways = [(4 * i + w, 4 * j + w) for w in (0, 2) for i, j in up]
    both_ways += [(4 * i + w, 4 * j + w) for w in (1, 3) for i, j in down]
    mine = lax.ppermute(rounded, ("gz", "view"), both_ways)

    last, first = pl.pallas_call(
        edges_kernel,
        out_shape=[shape((views, margin, rows, cols), BF16)] * 2,
        in_specs=[HBM],
        out_specs=[HBM] * 2,
        scratch_shapes=[
            pltpu.VMEM((2 * views, margin, rows, cols), BF16),
            pltpu.SemaphoreType.DMA((2, 2 * views)),
        ],
        name="edges",
        **params(10**4, 10**4, 58 * 1024 * 1024),
    )(recordings)
    before = lax.ppermute(last, "gz", up)
    after = lax.ppermute(first, "gz", down)

    wide = -(-(z_out + taps - 1) * 8 // 128) * 128
    z_mat, x_mat, y_mat, scales = pl.pallas_call(
        matrices_kernel,
        out_shape=[
            shape((2, views * 2 * z_out * 8, wide), BF16),
            shape((2, views, 2 * cols, 2 * cols), BF16),
            shape((2, views, rows, 2 * rows), BF16),
            shape((views, 2, 1, 128), F32),
        ],
        in_specs=[SMEM, SMEM],
        out_specs=[VMEM] * 4,
        name="matrices",
        **params(10**6, 10**4),
    )(place_array, psf_taps)

    mine, z_mat = lax.optimization_barrier((mine, z_mat))
    mine = (mine[:margin], mine[margin:])
    other = [lax.ppermute(piece, "view", swap) for piece in mine]
    inverses = []
    for early, side in ((True, mine), (False, other)):
        inverses.append(
            pl.pallas_call(
                lambda *refs, early=early: inverse_kernel(early, *refs),
                out_shape=shape((views, planes, rows, cols), F32),
                in_specs=[SMEM] + [VMEM] * 7,
                out_specs=VMEM,
                scratch_shapes=scratch(views, 2, 1, z_out, rows, cols),
                name="inverses",
                **params(10**6, 10**4),
            )(place_array, *side, rounded, z_mat, x_mat, y_mat, scales)
        )
    own, rim = pl.pallas_call(
        arrange_kernel,
        out_shape=[shape((views, planes, rows, cols), BF16), shape((views, 2, margin, rows, cols), F32)],
        in_specs=[SMEM] + [VMEM] * 3,
        out_specs=[VMEM] * 2,
        name="arrange",
        **params(10**5, 10**4),
    )(place_array, recordings, *inverses)
    part = rows // 4
    keep, near, far = pl.pallas_call(
        correction_kernel,
        out_shape=[shape((2, planes + 1, part, cols), F32)] + [shape((planes + 1, part, cols), F32)] * 2,
        in_specs=[VMEM] * 8,
        out_specs=[VMEM] * 3,
        scratch_shapes=scratch(views, 2, 2, z_out, rows, cols) + [pltpu.VMEM((planes, rows, cols), F32)],
        name="corrections",
        **params(4 * 10**9, 5 * 10**6),
    )(before, own, after, rim, z_mat, x_mat, y_mat, scales)
    core_far = lax.ppermute(far, "view", swap)
    core_near = lax.ppermute(near, "view", swap)
    across = lax.ppermute((keep[1] * core_far).astype(jnp.float16), "view", [(i, i ^ 2) for i in range(4)])
    own_rows = lax.dynamic_slice_in_dim(estimate, place * part, part, 1)
    root = keep[0, planes] * core_near[planes]
    partial = own_rows * (keep[0, :planes] * core_near[:planes])
    partial, root, across = lax.optimization_barrier((partial, root, across))
    root = root * across[planes].astype(F32)
    return partial * (across[:planes].astype(F32) * (root * root * root * root))


def solution(mesh):
    in_specs = (P("gz", None, None), P("view", "gz", None, None), P("view", None, None, None))
    out_specs = P("gz", "view", None)
    return jax.shard_map(local, mesh=mesh, in_specs=in_specs, out_specs=out_specs, check_vma=False)
```

```python
import jax
import jax.numpy as jnp
from jax import lax
from jax.experimental import pallas as pl
from jax.experimental.pallas import tpu as pltpu
from jax.sharding import PartitionSpec as P

F32 = jnp.float32
BF16 = jnp.bfloat16
VMEM = pl.BlockSpec(memory_space=pltpu.VMEM)
HBM = pl.BlockSpec(memory_space=pltpu.HBM)
SMEM = pl.BlockSpec(memory_space=pltpu.SMEM)
LIMIT = 20 * 1024 * 1024


def split(value):
    high = value.astype(BF16)
    return high, (value - high.astype(F32)).astype(BF16)


def params(flops, nbytes, limit=LIMIT):
    return dict(
        compiler_params=pltpu.CompilerParams(vmem_limit_bytes=limit),
        cost_estimate=pl.CostEstimate(flops=flops, bytes_accessed=nbytes, transcendentals=0),
    )


def edges_kernel(rec_ref, last_out, first_out, held, sems):
    views, planes = rec_ref.shape[:2]
    margin = last_out.shape[1]
    copies, outs = [], []
    for v in range(views):
        for out, begin in ((last_out, planes - margin), (first_out, 0)):
            i = len(copies)
            copies.append(pltpu.make_async_copy(rec_ref.at[v, pl.ds(begin, margin)], held.at[i], sems.at[0, i]))
            outs.append(pltpu.make_async_copy(held.at[i], out.at[v], sems.at[1, i]))
    for copy in copies:
        copy.start()
    for copy, out in zip(copies, outs):
        copy.wait()
        out.start()
    for out in outs:
        out.wait()


def rounded_scales(taps, totals):
    factor = jnp.exp2(lax.broadcasted_iota(jnp.int32, (1, 128), 1).astype(F32) * (1.0 / 128.0))
    scales = [factor / jnp.full((1, 128), total, F32) for total in totals]
    error = jnp.zeros((1, 128), F32)
    for tap, scale in zip(taps, scales):
        sums, running = [], jnp.zeros((1, 128), F32)
        for value in tap:
            exact = value * scale
            running = running + (exact.astype(BF16).astype(F32) - exact)
            sums.append(running)
        for partial in sums:
            rest = running - partial
            error = error + partial * partial + rest * rest
    error = error / (factor * factor)
    best = error == jnp.min(error, axis=1, keepdims=True)
    chosen = [jnp.max(jnp.where(best, row, 0.0), axis=1, keepdims=True) for row in scales + [factor]]
    return [jnp.broadcast_to(row, (1, 128)) for row in chosen]


def matrices_kernel(place_ref, taps_ref, z_ref, x_ref, y_ref, scale_ref):
    views, taps = taps_ref.shape[0], taps_ref.shape[3]
    half = (taps - 1) // 2
    rows = x_ref.shape[2] // 2
    place = place_ref[0]
    zeros = jnp.zeros((rows, rows), BF16)

    for v in range(views):
        tap = {
            (d, r): [taps_ref[v, d, r, j] for j in range(taps)] for d in range(3) for r in range(2)
        }
        scale = {}
        undo = jnp.ones((1, 128), F32)
        for d in range(3):
            totals = []
            for r in range(2):
                values = tap[d, r] if d < 2 else tap[2, 0] + tap[2, 1]
                total = values[0]
                for value in values[1:]:
                    total = total + value
                totals.append(total)
            scale[d, 0], scale[d, 1], factor = rounded_scales([tap[d, 0], tap[d, 1]], totals)
            undo = undo / factor
        scale_ref[v] = undo
        for direction in range(2):
            for r in range(2):
                other = 1 - r
                x_ref[direction, v, r * rows : (r + 1) * rows, other * rows : (other + 1) * rows] = zeros
        step = 32
        for first in range(0, rows, step):
            diff = (
                lax.broadcasted_iota(jnp.int32, (step, rows), 0)
                - lax.broadcasted_iota(jnp.int32, (step, rows), 1)
                + (first + half)
            )
            made = {(d, r, m): jnp.zeros((step, rows), F32) for d in range(2) for r in range(2) for m in range(2)}
            for j in range(taps):
                here = diff == j
                for d, r, m in made:
                    pick = tap[d, r][j] if m == 0 else tap[d, r][taps - 1 - j]
                    made[d, r, m] = jnp.where(here, pick, made[d, r, m])
            for (d, r, m), value in made.items():
                value = (value * scale[d, r]).astype(BF16)
                lanes = slice(r * rows, (r + 1) * rows)
                if d == 0:
                    x_ref[m, v, r * rows + first : r * rows + first + step, lanes] = value
                elif m == 1:
                    y_ref[0, v, first : first + step, lanes] = value
                else:
                    target = pl.multiple_of(jnp.bitwise_xor(first // step, place) * step, step)
                    y_ref[1, v, pl.ds(target, step), lanes] = value
        tall = z_ref.shape[1] // (2 * views)
        wide = z_ref.shape[2]
        step = 16
        for first in range(0, tall, step):
            diff = (
                lax.broadcasted_iota(jnp.int32, (step, wide), 1)
                - lax.broadcasted_iota(jnp.int32, (step, wide), 0)
                - first
            )
            made = {(r, m): jnp.zeros((step, wide), F32) for r in range(2) for m in range(2)}
            for j in range(taps):
                here = diff == 8 * j
                for r, m in made:
                    pick = tap[2, r][j] if m == 0 else tap[2, r][taps - 1 - j]
                    made[r, m] = jnp.where(here, pick, made[r, m])
            for (r, m), value in made.items():
                top = (2 * v + r) * tall + first
                z_ref[m, top : top + step, :] = (value * scale[2, r][0:1, 0:1]).astype(BF16)


def dot(a, b):
    return jnp.dot(a, b, preferred_element_type=F32)


CHUNK = 4


def inverted(value):
    guess = pl.reciprocal(value, approx=True)
    return guess * (2.0 - value * guess)


def filter_to(loads, views, groups, z_ref, x_ref, y_ref, scale_ref, e_ref, g_ref, exact, emit):
    tall = z_ref.shape[0] // (2 * views)
    z_out = tall // 8
    rows = y_ref.shape[1]
    sets = len(loads)
    for pair, own in [(pair, own) for pair in range(rows // 16) for own in range(sets)]:
        block = loads[own](slice(pair * 16, pair * 16 + 16))
        of = range(views) if sets == 1 else range(own, own + 1)
        top_z, end_z = of.start * 2 * tall, of.stop * 2 * tall
        planes = block.shape[0]
        depth = (planes - (groups - 1) * z_out) * 8
        octets = [block[:, 8 * o : 8 * o + 8, :].reshape(planes * 8, rows).astype(BF16) for o in range(2)]
        octets = jnp.concatenate(octets, axis=1)
        for part in range(groups):
            data = octets[part * z_out * 8 : part * z_out * 8 + depth]
            all_e = dot(z_ref[top_z:end_z, :depth], data)
            for v in of:
                for r in range(2):
                    top = (2 * (v - of.start) + r) * tall
                    e = all_e[top : top + tall]
                    e = jnp.concatenate([e[:, :rows], e[:, rows:]], axis=0)
                    lanes = slice(r * rows, (r + 1) * rows)
                    if exact:
                        high, low = split(e)
                        e_ref[v, 0, pair * groups + part, :, lanes] = high
                        e_ref[v, 1, pair * groups + part, :, lanes] = low
                    else:
                        e_ref[v, 0, pair * groups + part, :, lanes] = e.astype(BF16)
    for v in range(views):
        for first in range(0, rows // 16 * groups, CHUNK):
            e = e_ref[v, 0, first : first + CHUNK].reshape(CHUNK * 2 * tall, 2 * rows)
            all_g = dot(e, x_ref[v])
            if exact:
                e = e_ref[v, 1, first : first + CHUNK].reshape(CHUNK * 2 * tall, 2 * rows)
                all_g = all_g + dot(e, x_ref[v])
            for index in range(first, first + CHUNK):
                pair, part = index // groups, index % groups
                g = all_g[(index - first) * 2 * tall : (index - first + 1) * 2 * tall]
                for r in range(2):
                    lanes = slice(r * rows, (r + 1) * rows)
                    g_rows = jnp.concatenate(
                        [g[o * tall : (o + 1) * tall, lanes].reshape(z_out, 8, rows) for o in range(2)], axis=1
                    )
                    target = slice(r * rows + pair * 16, r * rows + pair * 16 + 16)
                    planes_at = slice(part * z_out, (part + 1) * z_out)
                    if exact:
                        high, low = split(g_rows)
                        g_ref[v, 0, planes_at, target, :] = high
                        g_ref[v, 1, planes_at, target, :] = low
                    else:
                        g_ref[v, 0, planes_at, target, :] = g_rows.astype(BF16)
    for v in range(views):
        for z in range(0, groups * z_out, 2):
            data = jnp.concatenate([g_ref[v, 0, z], g_ref[v, 0, z + 1]], axis=1)
            out = dot(y_ref[v], data)
            if exact:
                data = jnp.concatenate([g_ref[v, 1, z], g_ref[v, 1, z + 1]], axis=1)
                out = out + dot(y_ref[v], data)
            emit(v, z, out[:, :rows] * scale_ref[v])
            emit(v, z + 1, out[:, rows:] * scale_ref[v])


def scratch(views, groups, halves, z_out, rows, cols):
    return [
        pltpu.VMEM((views, halves, rows // 16 * groups, 2 * z_out * 8, 2 * cols), BF16),
        pltpu.VMEM((views, halves, groups * z_out, 2 * rows, cols), BF16),
    ]


def inverse_kernel(early, place_ref, low_ref, high_ref, own_ref, z_ref, x_ref, y_ref, scale_ref, out_ref, e_ref, g_ref):
    side_first = (place_ref[0] % 2 == 0) == early

    def load(at):
        side = jnp.concatenate([low_ref[:, at, :], high_ref[:, at, :]], axis=0).astype(F32)
        own = own_ref[:, at, :].astype(F32)
        return jnp.concatenate([jnp.where(side_first, side, own), jnp.where(side_first, own, side)], axis=0)

    def emit(v, z, blurred):
        out_ref[v, z] = inverted(blurred)

    views = out_ref.shape[0]
    filter_to([load], views, 2, z_ref.at[0], x_ref.at[0], y_ref.at[0], scale_ref, e_ref, g_ref, False, emit)


def arrange_kernel(place_ref, rec_ref, early_ref, late_ref, own_out, rim_out):
    views, planes = rec_ref.shape[:2]
    half = planes // 2
    early_first = place_ref[0] % 2 == 0
    for v in range(views):
        for z in range(planes):
            early, late = early_ref[v, z], late_ref[v, z]
            first, second = jnp.where(early_first, early, late), jnp.where(early_first, late, early)
            if z < half:
                rim_out[v, 0, z] = first
                own_out[v, half + z] = (rec_ref[v, half + z].astype(F32) * second).astype(BF16)
            else:
                own_out[v, z - half] = (rec_ref[v, z - half].astype(F32) * first).astype(BF16)
                rim_out[v, 1, z - half] = second


def correction_kernel(
    before_ref,
    own_ref,
    after_ref,
    rim_ref,
    z_ref,
    x_ref,
    y_ref,
    scale_ref,
    keep_ref,
    near_ref,
    far_ref,
    e_ref,
    g_ref,
    product_ref,
):
    views, planes = own_ref.shape[:2]
    part = keep_ref.shape[2]
    most = [jnp.zeros((8, product_ref.shape[2]), F32)]

    def load(at, v):
        before = before_ref[v, :, at, :].astype(F32) * rim_ref[v, 0, :, at, :]
        after = after_ref[v, :, at, :].astype(F32) * rim_ref[v, 1, :, at, :]
        return jnp.concatenate([before, own_ref[v, :, at, :].astype(F32), after], axis=0)

    def emit(v, z, value):
        if v > 0:
            value = value * product_ref[z]
        product_ref[z] = value
        if v == views - 1:
            for top in range(0, value.shape[0], 8):
                most[0] = jnp.maximum(most[0], value[top : top + 8])

    loads = [lambda at, v=v: load(at, v) for v in range(views)]
    filter_to(loads, views, 2, z_ref.at[1], x_ref.at[1], y_ref.at[1], scale_ref, e_ref, g_ref, True, emit)
    top = jnp.maximum(jnp.max(most[0], axis=(0, 1), keepdims=True), 1e-30)
    quarter = jnp.ceil(jnp.log2(top) * 0.25)
    scale = jnp.exp2(-4.0 * quarter)
    root = jnp.broadcast_to(jnp.exp2(quarter), (part, product_ref.shape[2]))
    targets = (keep_ref.at[0], near_ref, keep_ref.at[1], far_ref)
    for z in range(planes):
        value = product_ref[z] * scale
        for b in range(4):
            targets[b][z] = value[b * part : (b + 1) * part]
    for target in targets:
        target[planes] = root


def local(estimate, recordings, psf_taps):
    planes, rows, cols = estimate.shape
    taps = psf_taps.shape[-1]
    margin = (taps - 1) // 2
    views = recordings.shape[0]
    devices = lax.axis_size("gz")
    place = lax.axis_index("view")
    place_array = place.reshape(1).astype(jnp.int32)
    up = [(i, i + 1) for i in range(devices - 1)]
    down = [(i + 1, i) for i in range(devices - 1)]
    swap = [(i, i ^ 1) for i in range(4)]
    z_out = planes // 2
    shape = jax.ShapeDtypeStruct

    rounded = estimate.astype(BF16)
    both_ways = [(4 * i + w, 4 * j + w) for w in (0, 2) for i, j in up]
    both_ways += [(4 * i + w, 4 * j + w) for w in (1, 3) for i, j in down]
    mine = lax.ppermute(rounded, ("gz", "view"), both_ways)

    last, first = pl.pallas_call(
        edges_kernel,
        out_shape=[shape((views, margin, rows, cols), BF16)] * 2,
        in_specs=[HBM],
        out_specs=[HBM] * 2,
        scratch_shapes=[
            pltpu.VMEM((2 * views, margin, rows, cols), BF16),
            pltpu.SemaphoreType.DMA((2, 2 * views)),
        ],
        name="edges",
        **params(10**4, 10**4, 58 * 1024 * 1024),
    )(recordings)
    before = lax.ppermute(last, "gz", up)
    after = lax.ppermute(first, "gz", down)

    wide = -(-(z_out + taps - 1) * 8 // 128) * 128
    z_mat, x_mat, y_mat, scales = pl.pallas_call(
        matrices_kernel,
        out_shape=[
            shape((2, views * 2 * z_out * 8, wide), BF16),
            shape((2, views, 2 * cols, 2 * cols), BF16),
            shape((2, views, rows, 2 * rows), BF16),
            shape((views, 1, 128), F32),
        ],
        in_specs=[SMEM, SMEM],
        out_specs=[VMEM] * 4,
        name="matrices",
        **params(10**6, 10**4),
    )(place_array, psf_taps)

    mine, z_mat = lax.optimization_barrier((mine, z_mat))
    mine = (mine[:margin], mine[margin:])
    other = [lax.ppermute(piece, "view", swap) for piece in mine]
    inverses = []
    for early, side in ((True, mine), (False, other)):
        inverses.append(
            pl.pallas_call(
                lambda *refs, early=early: inverse_kernel(early, *refs),
                out_shape=shape((views, planes, rows, cols), F32),
                in_specs=[SMEM] + [VMEM] * 7,
                out_specs=VMEM,
                scratch_shapes=scratch(views, 2, 1, z_out, rows, cols),
                name="inverses",
                **params(10**6, 10**4),
            )(place_array, *side, rounded, z_mat, x_mat, y_mat, scales)
        )
    own, rim = pl.pallas_call(
        arrange_kernel,
        out_shape=[shape((views, planes, rows, cols), BF16), shape((views, 2, margin, rows, cols), F32)],
        in_specs=[SMEM] + [VMEM] * 3,
        out_specs=[VMEM] * 2,
        name="arrange",
        **params(10**5, 10**4),
    )(place_array, recordings, *inverses)
    part = rows // 4
    keep, near, far = pl.pallas_call(
        correction_kernel,
        out_shape=[shape((2, planes + 1, part, cols), F32)] + [shape((planes + 1, part, cols), F32)] * 2,
        in_specs=[VMEM] * 8,
        out_specs=[VMEM] * 3,
        scratch_shapes=scratch(views, 2, 2, z_out, rows, cols) + [pltpu.VMEM((planes, rows, cols), F32)],
        name="corrections",
        **params(4 * 10**9, 5 * 10**6),
    )(before, own, after, rim, z_mat, x_mat, y_mat, scales)
    core_far = lax.ppermute(far, "view", swap)
    core_near = lax.ppermute(near, "view", swap)
    across = lax.ppermute((keep[1] * core_far).astype(jnp.float16), "view", [(i, i ^ 2) for i in range(4)])
    own_rows = lax.dynamic_slice_in_dim(estimate, place * part, part, 1)
    root = keep[0, planes] * core_near[planes]
    partial = own_rows * (keep[0, :planes] * core_near[:planes])
    partial, root, across = lax.optimization_barrier((partial, root, across))
    root = root * across[planes].astype(F32)
    return partial * (across[:planes].astype(F32) * (root * root * root * root))


def solution(mesh):
    in_specs = (P("gz", None, None), P("view", "gz", None, None), P("view", None, None, None))
    out_specs = P("gz", "view", None)
    return jax.shard_map(local, mesh=mesh, in_specs=in_specs, out_specs=out_specs, check_vma=False)
```

```python
import jax
import jax.numpy as jnp
from jax import lax
from jax.experimental import pallas as pl
from jax.experimental.pallas import tpu as pltpu
from jax.sharding import PartitionSpec as P

F32 = jnp.float32
BF16 = jnp.bfloat16
VMEM = pl.BlockSpec(memory_space=pltpu.VMEM)
HBM = pl.BlockSpec(memory_space=pltpu.HBM)
SMEM = pl.BlockSpec(memory_space=pltpu.SMEM)
LIMIT = 20 * 1024 * 1024


def split(value):
    high = value.astype(BF16)
    return high, (value - high.astype(F32)).astype(BF16)


def params(flops, nbytes, limit=LIMIT):
    return dict(
        compiler_params=pltpu.CompilerParams(vmem_limit_bytes=limit),
        cost_estimate=pl.CostEstimate(flops=flops, bytes_accessed=nbytes, transcendentals=0),
    )


def edges_kernel(rec_ref, last_out, first_out, held, sems):
    views, planes = rec_ref.shape[:2]
    margin = last_out.shape[1]
    copies, outs = [], []
    for v in range(views):
        for out, begin in ((last_out, planes - margin), (first_out, 0)):
            i = len(copies)
            copies.append(pltpu.make_async_copy(rec_ref.at[v, pl.ds(begin, margin)], held.at[i], sems.at[0, i]))
            outs.append(pltpu.make_async_copy(held.at[i], out.at[v], sems.at[1, i]))
    for copy in copies:
        copy.start()
    for copy, out in zip(copies, outs):
        copy.wait()
        out.start()
    for out in outs:
        out.wait()


def rounded_scales(taps, totals):
    factor = jnp.exp2(lax.broadcasted_iota(jnp.int32, (1, 128), 1).astype(F32) * (1.0 / 128.0))
    scales = [factor / jnp.full((1, 128), total, F32) for total in totals]
    error = jnp.zeros((1, 128), F32)
    for tap, scale in zip(taps, scales):
        sums, running = [], jnp.zeros((1, 128), F32)
        for value in tap:
            exact = value * scale
            running = running + (exact.astype(BF16).astype(F32) - exact)
            sums.append(running)
        for partial in sums:
            rest = running - partial
            error = error + partial * partial + rest * rest
    error = error / (factor * factor)
    best = error == jnp.min(error, axis=1, keepdims=True)
    chosen = [jnp.max(jnp.where(best, row, 0.0), axis=1, keepdims=True) for row in scales + [factor]]
    return [jnp.broadcast_to(row, (1, 128)) for row in chosen]


def matrices_kernel(place_ref, taps_ref, z_ref, x_ref, y_ref, scale_ref):
    views, taps = taps_ref.shape[0], taps_ref.shape[3]
    half = (taps - 1) // 2
    rows = x_ref.shape[2] // 2
    place = place_ref[0]
    zeros = jnp.zeros((rows, rows), BF16)

    for v in range(views):
        tap = {
            (d, r): [taps_ref[v, d, r, j] for j in range(taps)] for d in range(3) for r in range(2)
        }
        scale = {}
        undo = jnp.ones((1, 128), F32)
        for d in range(3):
            totals = []
            for r in range(2):
                values = tap[d, r] if d < 2 else tap[2, 0] + tap[2, 1]
                total = values[0]
                for value in values[1:]:
                    total = total + value
                totals.append(total)
            scale[d, 0], scale[d, 1], factor = rounded_scales([tap[d, 0], tap[d, 1]], totals)
            undo = undo / factor
        scale_ref[v] = undo
        for direction in range(2):
            for r in range(2):
                other = 1 - r
                x_ref[direction, v, r * rows : (r + 1) * rows, other * rows : (other + 1) * rows] = zeros
        step = 32
        for first in range(0, rows, step):
            diff = (
                lax.broadcasted_iota(jnp.int32, (step, rows), 0)
                - lax.broadcasted_iota(jnp.int32, (step, rows), 1)
                + (first + half)
            )
            made = {(d, r, m): jnp.zeros((step, rows), F32) for d in range(2) for r in range(2) for m in range(2)}
            for j in range(taps):
                here = diff == j
                for d, r, m in made:
                    pick = tap[d, r][j] if m == 0 else tap[d, r][taps - 1 - j]
                    made[d, r, m] = jnp.where(here, pick, made[d, r, m])
            for (d, r, m), value in made.items():
                value = (value * scale[d, r]).astype(BF16)
                lanes = slice(r * rows, (r + 1) * rows)
                if d == 0:
                    x_ref[m, v, r * rows + first : r * rows + first + step, lanes] = value
                elif m == 1:
                    y_ref[0, v, first : first + step, lanes] = value
                else:
                    target = pl.multiple_of(jnp.bitwise_xor(first // step, place) * step, step)
                    y_ref[1, v, pl.ds(target, step), lanes] = value
        tall = z_ref.shape[1] // (2 * views)
        wide = z_ref.shape[2]
        step = 16
        for first in range(0, tall, step):
            diff = (
                lax.broadcasted_iota(jnp.int32, (step, wide), 1)
                - lax.broadcasted_iota(jnp.int32, (step, wide), 0)
                - first
            )
            made = {(r, m): jnp.zeros((step, wide), F32) for r in range(2) for m in range(2)}
            for j in range(taps):
                here = diff == 8 * j
                for r, m in made:
                    pick = tap[2, r][j] if m == 0 else tap[2, r][taps - 1 - j]
                    made[r, m] = jnp.where(here, pick, made[r, m])
            for (r, m), value in made.items():
                top = (2 * v + r) * tall + first
                z_ref[m, top : top + step, :] = (value * scale[2, r][0:1, 0:1]).astype(BF16)


def dot(a, b):
    return jnp.dot(a, b, preferred_element_type=F32)


CHUNK = 8


def inverted(value):
    guess = pl.reciprocal(value, approx=True)
    return guess * (2.0 - value * guess)


def filter_to(loads, views, groups, z_ref, x_ref, y_ref, scale_ref, e_ref, g_ref, exact, emit):
    tall = z_ref.shape[0] // (2 * views)
    z_out = tall // 8
    rows = y_ref.shape[1]
    sets = len(loads)
    for pair, own in [(pair, own) for pair in range(rows // 16) for own in range(sets)]:
        block = loads[own](slice(pair * 16, pair * 16 + 16))
        of = range(views) if sets == 1 else range(own, own + 1)
        top_z, end_z = of.start * 2 * tall, of.stop * 2 * tall
        planes = block.shape[0]
        depth = (planes - (groups - 1) * z_out) * 8
        octets = [block[:, 8 * o : 8 * o + 8, :].reshape(planes * 8, rows).astype(BF16) for o in range(2)]
        octets = jnp.concatenate(octets, axis=1)
        for part in range(groups):
            data = octets[part * z_out * 8 : part * z_out * 8 + depth]
            all_e = dot(z_ref[top_z:end_z, :depth], data)
            for v in of:
                for r in range(2):
                    top = (2 * (v - of.start) + r) * tall
                    e = all_e[top : top + tall]
                    e = jnp.concatenate([e[:, :rows], e[:, rows:]], axis=0)
                    lanes = slice(r * rows, (r + 1) * rows)
                    if exact:
                        high, low = split(e)
                        e_ref[v, 0, pair * groups + part, :, lanes] = high
                        e_ref[v, 1, pair * groups + part, :, lanes] = low
                    else:
                        e_ref[v, 0, pair * groups + part, :, lanes] = e.astype(BF16)
    for v in range(views):
        for first in range(0, rows // 16 * groups, CHUNK):
            e = e_ref[v, 0, first : first + CHUNK].reshape(CHUNK * 2 * tall, 2 * rows)
            all_g = dot(e, x_ref[v])
            if exact:
                e = e_ref[v, 1, first : first + CHUNK].reshape(CHUNK * 2 * tall, 2 * rows)
                all_g = all_g + dot(e, x_ref[v])
            for index in range(first, first + CHUNK):
                pair, part = index // groups, index % groups
                g = all_g[(index - first) * 2 * tall : (index - first + 1) * 2 * tall]
                for r in range(2):
                    lanes = slice(r * rows, (r + 1) * rows)
                    g_rows = jnp.concatenate(
                        [g[o * tall : (o + 1) * tall, lanes].reshape(z_out, 8, rows) for o in range(2)], axis=1
                    )
                    target = slice(r * rows + pair * 16, r * rows + pair * 16 + 16)
                    planes_at = slice(part * z_out, (part + 1) * z_out)
                    if exact:
                        high, low = split(g_rows)
                        g_ref[v, 0, planes_at, target, :] = high
                        g_ref[v, 1, planes_at, target, :] = low
                    else:
                        g_ref[v, 0, planes_at, target, :] = g_rows.astype(BF16)
    for v in range(views):
        for z in range(0, groups * z_out, 2):
            data = jnp.concatenate([g_ref[v, 0, z], g_ref[v, 0, z + 1]], axis=1)
            out = dot(y_ref[v], data)
            if exact:
                data = jnp.concatenate([g_ref[v, 1, z], g_ref[v, 1, z + 1]], axis=1)
                out = out + dot(y_ref[v], data)
            emit(v, z, out[:, :rows] * scale_ref[v])
            emit(v, z + 1, out[:, rows:] * scale_ref[v])


def scratch(views, groups, halves, z_out, rows, cols):
    return [
        pltpu.VMEM((views, halves, rows // 16 * groups, 2 * z_out * 8, 2 * cols), BF16),
        pltpu.VMEM((views, halves, groups * z_out, 2 * rows, cols), BF16),
    ]


def inverse_kernel(early, place_ref, low_ref, high_ref, own_ref, z_ref, x_ref, y_ref, scale_ref, out_ref, e_ref, g_ref):
    side_first = (place_ref[0] % 2 == 0) == early

    def load(at):
        side = jnp.concatenate([low_ref[:, at, :], high_ref[:, at, :]], axis=0).astype(F32)
        own = own_ref[:, at, :].astype(F32)
        return jnp.concatenate([jnp.where(side_first, side, own), jnp.where(side_first, own, side)], axis=0)

    def emit(v, z, blurred):
        out_ref[v, z] = inverted(blurred)

    views = out_ref.shape[0]
    filter_to([load], views, 2, z_ref.at[0], x_ref.at[0], y_ref.at[0], scale_ref, e_ref, g_ref, False, emit)


def arrange_kernel(place_ref, rec_ref, early_ref, late_ref, own_out, rim_out):
    views, planes = rec_ref.shape[:2]
    half = planes // 2
    early_first = place_ref[0] % 2 == 0
    for v in range(views):
        for z in range(planes):
            early, late = early_ref[v, z], late_ref[v, z]
            first, second = jnp.where(early_first, early, late), jnp.where(early_first, late, early)
            if z < half:
                rim_out[v, 0, z] = first
                own_out[v, half + z] = (rec_ref[v, half + z].astype(F32) * second).astype(BF16)
            else:
                own_out[v, z - half] = (rec_ref[v, z - half].astype(F32) * first).astype(BF16)
                rim_out[v, 1, z - half] = second


def correction_kernel(
    before_ref,
    own_ref,
    after_ref,
    rim_ref,
    z_ref,
    x_ref,
    y_ref,
    scale_ref,
    keep_ref,
    near_ref,
    far_ref,
    e_ref,
    g_ref,
    product_ref,
):
    views, planes = own_ref.shape[:2]
    part = keep_ref.shape[2]
    most = [jnp.zeros((8, product_ref.shape[2]), F32)]

    def load(at, v):
        before = before_ref[v, :, at, :].astype(F32) * rim_ref[v, 0, :, at, :]
        after = after_ref[v, :, at, :].astype(F32) * rim_ref[v, 1, :, at, :]
        return jnp.concatenate([before, own_ref[v, :, at, :].astype(F32), after], axis=0)

    def emit(v, z, value):
        if v > 0:
            value = value * product_ref[z]
        product_ref[z] = value
        if v == views - 1:
            for top in range(0, value.shape[0], 8):
                most[0] = jnp.maximum(most[0], value[top : top + 8])

    loads = [lambda at, v=v: load(at, v) for v in range(views)]
    filter_to(loads, views, 2, z_ref.at[1], x_ref.at[1], y_ref.at[1], scale_ref, e_ref, g_ref, True, emit)
    top = jnp.maximum(jnp.max(most[0], axis=(0, 1), keepdims=True), 1e-30)
    quarter = jnp.ceil(jnp.log2(top) * 0.25)
    scale = jnp.exp2(-4.0 * quarter)
    root = jnp.broadcast_to(jnp.exp2(quarter), (part, product_ref.shape[2]))
    targets = (keep_ref.at[0], near_ref, keep_ref.at[1], far_ref)
    for z in range(planes):
        value = product_ref[z] * scale
        for b in range(4):
            targets[b][z] = value[b * part : (b + 1) * part]
    for target in targets:
        target[planes] = root


def local(estimate, recordings, psf_taps):
    planes, rows, cols = estimate.shape
    taps = psf_taps.shape[-1]
    margin = (taps - 1) // 2
    views = recordings.shape[0]
    devices = lax.axis_size("gz")
    place = lax.axis_index("view")
    place_array = place.reshape(1).astype(jnp.int32)
    up = [(i, i + 1) for i in range(devices - 1)]
    down = [(i + 1, i) for i in range(devices - 1)]
    swap = [(i, i ^ 1) for i in range(4)]
    z_out = planes // 2
    shape = jax.ShapeDtypeStruct

    rounded = estimate.astype(BF16)
    both_ways = [(4 * i + w, 4 * j + w) for w in (0, 2) for i, j in up]
    both_ways += [(4 * i + w, 4 * j + w) for w in (1, 3) for i, j in down]
    mine = lax.ppermute(rounded, ("gz", "view"), both_ways)

    last, first = pl.pallas_call(
        edges_kernel,
        out_shape=[shape((views, margin, rows, cols), BF16)] * 2,
        in_specs=[HBM],
        out_specs=[HBM] * 2,
        scratch_shapes=[
            pltpu.VMEM((2 * views, margin, rows, cols), BF16),
            pltpu.SemaphoreType.DMA((2, 2 * views)),
        ],
        name="edges",
        **params(10**4, 10**4, 58 * 1024 * 1024),
    )(recordings)
    before = lax.ppermute(last, "gz", up)
    after = lax.ppermute(first, "gz", down)

    wide = -(-(z_out + taps - 1) * 8 // 128) * 128
    z_mat, x_mat, y_mat, scales = pl.pallas_call(
        matrices_kernel,
        out_shape=[
            shape((2, views * 2 * z_out * 8, wide), BF16),
            shape((2, views, 2 * cols, 2 * cols), BF16),
            shape((2, views, rows, 2 * rows), BF16),
            shape((views, 1, 128), F32),
        ],
        in_specs=[SMEM, SMEM],
        out_specs=[VMEM] * 4,
        name="matrices",
        **params(10**6, 10**4),
    )(place_array, psf_taps)

    mine, z_mat = lax.optimization_barrier((mine, z_mat))
    mine = (mine[:margin], mine[margin:])
    other = [lax.ppermute(piece, "view", swap) for piece in mine]
    inverses = []
    for early, side in ((True, mine), (False, other)):
        inverses.append(
            pl.pallas_call(
                lambda *refs, early=early: inverse_kernel(early, *refs),
                out_shape=shape((views, planes, rows, cols), F32),
                in_specs=[SMEM] + [VMEM] * 7,
                out_specs=VMEM,
                scratch_shapes=scratch(views, 2, 1, z_out, rows, cols),
                name="inverses",
                **params(10**6, 10**4),
            )(place_array, *side, rounded, z_mat, x_mat, y_mat, scales)
        )
    own, rim = pl.pallas_call(
        arrange_kernel,
        out_shape=[shape((views, planes, rows, cols), BF16), shape((views, 2, margin, rows, cols), F32)],
        in_specs=[SMEM] + [VMEM] * 3,
        out_specs=[VMEM] * 2,
        name="arrange",
        **params(10**5, 10**4),
    )(place_array, recordings, *inverses)
    part = rows // 4
    keep, near, far = pl.pallas_call(
        correction_kernel,
        out_shape=[shape((2, planes + 1, part, cols), F32)] + [shape((planes + 1, part, cols), F32)] * 2,
        in_specs=[VMEM] * 8,
        out_specs=[VMEM] * 3,
        scratch_shapes=scratch(views, 2, 2, z_out, rows, cols) + [pltpu.VMEM((planes, rows, cols), F32)],
        name="corrections",
        **params(4 * 10**9, 5 * 10**6),
    )(before, own, after, rim, z_mat, x_mat, y_mat, scales)
    core_far = lax.ppermute(far, "view", swap)
    core_near = lax.ppermute(near, "view", swap)
    across = lax.ppermute((keep[1] * core_far).astype(jnp.float16), "view", [(i, i ^ 2) for i in range(4)])
    own_rows = lax.dynamic_slice_in_dim(estimate, place * part, part, 1)
    root = keep[0, planes] * core_near[planes]
    partial = own_rows * (keep[0, :planes] * core_near[:planes])
    partial, root, across = lax.optimization_barrier((partial, root, across))
    root = root * across[planes].astype(F32)
    return partial * (across[:planes].astype(F32) * (root * root * root * root))


def solution(mesh):
    in_specs = (P("gz", None, None), P("view", "gz", None, None), P("view", None, None, None))
    out_specs = P("gz", "view", None)
    return jax.shard_map(local, mesh=mesh, in_specs=in_specs, out_specs=out_specs, check_vma=False)
```

```python
import jax
import jax.numpy as jnp
from jax import lax
from jax.experimental import pallas as pl
from jax.experimental.pallas import tpu as pltpu
from jax.sharding import PartitionSpec as P

F32 = jnp.float32
BF16 = jnp.bfloat16
VMEM = pl.BlockSpec(memory_space=pltpu.VMEM)
HBM = pl.BlockSpec(memory_space=pltpu.HBM)
SMEM = pl.BlockSpec(memory_space=pltpu.SMEM)
LIMIT = 20 * 1024 * 1024


def split(value):
    high = value.astype(BF16)
    return high, (value - high.astype(F32)).astype(BF16)


def params(flops, nbytes, limit=LIMIT):
    return dict(
        compiler_params=pltpu.CompilerParams(vmem_limit_bytes=limit),
        cost_estimate=pl.CostEstimate(flops=flops, bytes_accessed=nbytes, transcendentals=0),
    )


def edges_kernel(rec_ref, last_out, first_out, held, sems):
    views, planes = rec_ref.shape[:2]
    margin = last_out.shape[1]
    copies, outs = [], []
    for v in range(views):
        for out, begin in ((last_out, planes - margin), (first_out, 0)):
            i = len(copies)
            copies.append(pltpu.make_async_copy(rec_ref.at[v, pl.ds(begin, margin)], held.at[i], sems.at[0, i]))
            outs.append(pltpu.make_async_copy(held.at[i], out.at[v], sems.at[1, i]))
    for copy in copies:
        copy.start()
    for copy, out in zip(copies, outs):
        copy.wait()
        out.start()
    for out in outs:
        out.wait()


def rounded_scales(taps, totals):
    factor = jnp.exp2(lax.broadcasted_iota(jnp.int32, (1, 128), 1).astype(F32) * (1.0 / 128.0))
    scales = [factor / jnp.full((1, 128), total, F32) for total in totals]
    error = jnp.zeros((1, 128), F32)
    for tap, scale in zip(taps, scales):
        sums, running = [], jnp.zeros((1, 128), F32)
        for value in tap:
            exact = value * scale
            running = running + (exact.astype(BF16).astype(F32) - exact)
            sums.append(running)
        for partial in sums:
            rest = running - partial
            error = error + partial * partial + rest * rest
    error = error / (factor * factor)
    best = error == jnp.min(error, axis=1, keepdims=True)
    chosen = [jnp.max(jnp.where(best, row, 0.0), axis=1, keepdims=True) for row in scales + [factor]]
    return [jnp.broadcast_to(row, (1, 128)) for row in chosen]


def matrices_kernel(place_ref, taps_ref, z_ref, x_ref, y_ref, scale_ref):
    views, taps = taps_ref.shape[0], taps_ref.shape[3]
    half = (taps - 1) // 2
    rows = x_ref.shape[2] // 2
    place = place_ref[0]
    zeros = jnp.zeros((rows, rows), BF16)

    for v in range(views):
        tap = {
            (d, r): [taps_ref[v, d, r, j] for j in range(taps)] for d in range(3) for r in range(2)
        }
        scale = {}
        undo = jnp.ones((1, 128), F32)
        for d in range(3):
            totals = []
            for r in range(2):
                values = tap[d, r] if d < 2 else tap[2, 0] + tap[2, 1]
                total = values[0]
                for value in values[1:]:
                    total = total + value
                totals.append(total)
            scale[d, 0], scale[d, 1], factor = rounded_scales([tap[d, 0], tap[d, 1]], totals)
            undo = undo / factor
        scale_ref[v] = undo
        for direction in range(2):
            for r in range(2):
                other = 1 - r
                x_ref[direction, v, r * rows : (r + 1) * rows, other * rows : (other + 1) * rows] = zeros
        step = 32
        for first in range(0, rows, step):
            diff = (
                lax.broadcasted_iota(jnp.int32, (step, rows), 0)
                - lax.broadcasted_iota(jnp.int32, (step, rows), 1)
                + (first + half)
            )
            made = {(d, r, m): jnp.zeros((step, rows), F32) for d in range(2) for r in range(2) for m in range(2)}
            for j in range(taps):
                here = diff == j
                for d, r, m in made:
                    pick = tap[d, r][j] if m == 0 else tap[d, r][taps - 1 - j]
                    made[d, r, m] = jnp.where(here, pick, made[d, r, m])
            for (d, r, m), value in made.items():
                value = (value * scale[d, r]).astype(BF16)
                lanes = slice(r * rows, (r + 1) * rows)
                if d == 0:
                    x_ref[m, v, r * rows + first : r * rows + first + step, lanes] = value
                elif m == 1:
                    y_ref[0, v, first : first + step, lanes] = value
                else:
                    target = pl.multiple_of(jnp.bitwise_xor(first // step, place) * step, step)
                    y_ref[1, v, pl.ds(target, step), lanes] = value
        tall = z_ref.shape[1] // (2 * views)
        wide = z_ref.shape[2]
        step = 16
        for first in range(0, tall, step):
            diff = (
                lax.broadcasted_iota(jnp.int32, (step, wide), 1)
                - lax.broadcasted_iota(jnp.int32, (step, wide), 0)
                - first
            )
            made = {(r, m): jnp.zeros((step, wide), F32) for r in range(2) for m in range(2)}
            for j in range(taps):
                here = diff == 8 * j
                for r, m in made:
                    pick = tap[2, r][j] if m == 0 else tap[2, r][taps - 1 - j]
                    made[r, m] = jnp.where(here, pick, made[r, m])
            for (r, m), value in made.items():
                top = (2 * v + r) * tall + first
                z_ref[m, top : top + step, :] = (value * scale[2, r][0:1, 0:1]).astype(BF16)


def dot(a, b):
    return jnp.dot(a, b, preferred_element_type=F32)


CHUNK = 2


def inverted(value):
    guess = pl.reciprocal(value, approx=True)
    return guess * (2.0 - value * guess)


def filter_to(loads, views, groups, z_ref, x_ref, y_ref, scale_ref, e_ref, g_ref, exact, emit):
    tall = z_ref.shape[0] // (2 * views)
    z_out = tall // 8
    rows = y_ref.shape[1]
    sets = len(loads)
    for pair, own in [(pair, own) for pair in range(rows // 16) for own in range(sets)]:
        block = loads[own](slice(pair * 16, pair * 16 + 16))
        of = range(views) if sets == 1 else range(own, own + 1)
        top_z, end_z = of.start * 2 * tall, of.stop * 2 * tall
        planes = block.shape[0]
        depth = (planes - (groups - 1) * z_out) * 8
        octets = [block[:, 8 * o : 8 * o + 8, :].reshape(planes * 8, rows).astype(BF16) for o in range(2)]
        octets = jnp.concatenate(octets, axis=1)
        for part in range(groups):
            data = octets[part * z_out * 8 : part * z_out * 8 + depth]
            all_e = dot(z_ref[top_z:end_z, :depth], data)
            for v in of:
                for r in range(2):
                    top = (2 * (v - of.start) + r) * tall
                    e = all_e[top : top + tall]
                    e = jnp.concatenate([e[:, :rows], e[:, rows:]], axis=0)
                    lanes = slice(r * rows, (r + 1) * rows)
                    if exact:
                        high, low = split(e)
                        e_ref[v, 0, pair * groups + part, :, lanes] = high
                        e_ref[v, 1, pair * groups + part, :, lanes] = low
                    else:
                        e_ref[v, 0, pair * groups + part, :, lanes] = e.astype(BF16)
    for v in range(views):
        for first in range(0, rows // 16 * groups, CHUNK):
            e = e_ref[v, 0, first : first + CHUNK].reshape(CHUNK * 2 * tall, 2 * rows)
            all_g = dot(e, x_ref[v])
            if exact:
                e = e_ref[v, 1, first : first + CHUNK].reshape(CHUNK * 2 * tall, 2 * rows)
                all_g = all_g + dot(e, x_ref[v])
            for index in range(first, first + CHUNK):
                pair, part = index // groups, index % groups
                g = all_g[(index - first) * 2 * tall : (index - first + 1) * 2 * tall]
                for r in range(2):
                    lanes = slice(r * rows, (r + 1) * rows)
                    g_rows = jnp.concatenate(
                        [g[o * tall : (o + 1) * tall, lanes].reshape(z_out, 8, rows) for o in range(2)], axis=1
                    )
                    target = slice(r * rows + pair * 16, r * rows + pair * 16 + 16)
                    planes_at = slice(part * z_out, (part + 1) * z_out)
                    if exact:
                        high, low = split(g_rows)
                        g_ref[v, 0, planes_at, target, :] = high
                        g_ref[v, 1, planes_at, target, :] = low
                    else:
                        g_ref[v, 0, planes_at, target, :] = g_rows.astype(BF16)
    for v in range(views):
        for z in range(0, groups * z_out, 2):
            data = jnp.concatenate([g_ref[v, 0, z], g_ref[v, 0, z + 1]], axis=1)
            out = dot(y_ref[v], data)
            if exact:
                data = jnp.concatenate([g_ref[v, 1, z], g_ref[v, 1, z + 1]], axis=1)
                out = out + dot(y_ref[v], data)
            emit(v, z, out[:, :rows] * scale_ref[v])
            emit(v, z + 1, out[:, rows:] * scale_ref[v])


def scratch(views, groups, halves, z_out, rows, cols):
    return [
        pltpu.VMEM((views, halves, rows // 16 * groups, 2 * z_out * 8, 2 * cols), BF16),
        pltpu.VMEM((views, halves, groups * z_out, 2 * rows, cols), BF16),
    ]


def inverse_kernel(early, place_ref, low_ref, high_ref, own_ref, z_ref, x_ref, y_ref, scale_ref, out_ref, e_ref, g_ref):
    side_first = (place_ref[0] % 2 == 0) == early

    def load(at):
        side = jnp.concatenate([low_ref[:, at, :], high_ref[:, at, :]], axis=0).astype(F32)
        own = own_ref[:, at, :].astype(F32)
        return jnp.concatenate([jnp.where(side_first, side, own), jnp.where(side_first, own, side)], axis=0)

    def emit(v, z, blurred):
        out_ref[v, z] = inverted(blurred)

    views = out_ref.shape[0]
    filter_to([load], views, 2, z_ref.at[0], x_ref.at[0], y_ref.at[0], scale_ref, e_ref, g_ref, False, emit)


def arrange_kernel(place_ref, rec_ref, early_ref, late_ref, own_out, rim_out):
    views, planes = rec_ref.shape[:2]
    half = planes // 2
    early_first = place_ref[0] % 2 == 0
    for v in range(views):
        for z in range(planes):
            early, late = early_ref[v, z], late_ref[v, z]
            first, second = jnp.where(early_first, early, late), jnp.where(early_first, late, early)
            if z < half:
                rim_out[v, 0, z] = first
                own_out[v, half + z] = (rec_ref[v, half + z].astype(F32) * second).astype(BF16)
            else:
                own_out[v, z - half] = (rec_ref[v, z - half].astype(F32) * first).astype(BF16)
                rim_out[v, 1, z - half] = second


def correction_kernel(
    before_ref,
    own_ref,
    after_ref,
    rim_ref,
    z_ref,
    x_ref,
    y_ref,
    scale_ref,
    keep_ref,
    near_ref,
    far_ref,
    e_ref,
    g_ref,
    product_ref,
):
    views, planes = own_ref.shape[:2]
    part = keep_ref.shape[2]
    most = [jnp.zeros((8, product_ref.shape[2]), F32)]

    def load(at, v):
        before = before_ref[v, :, at, :].astype(F32) * rim_ref[v, 0, :, at, :]
        after = after_ref[v, :, at, :].astype(F32) * rim_ref[v, 1, :, at, :]
        return jnp.concatenate([before, own_ref[v, :, at, :].astype(F32), after], axis=0)

    def emit(v, z, value):
        if v > 0:
            value = value * product_ref[z]
        product_ref[z] = value
        if v == views - 1:
            for top in range(0, value.shape[0], 8):
                most[0] = jnp.maximum(most[0], value[top : top + 8])

    loads = [lambda at, v=v: load(at, v) for v in range(views)]
    filter_to(loads, views, 2, z_ref.at[1], x_ref.at[1], y_ref.at[1], scale_ref, e_ref, g_ref, True, emit)
    top = jnp.maximum(jnp.max(most[0], axis=(0, 1), keepdims=True), 1e-30)
    quarter = jnp.ceil(jnp.log2(top) * 0.25)
    scale = jnp.exp2(-4.0 * quarter)
    root = jnp.broadcast_to(jnp.exp2(quarter), (part, product_ref.shape[2]))
    targets = (keep_ref.at[0], near_ref, keep_ref.at[1], far_ref)
    for z in range(planes):
        value = product_ref[z] * scale
        for b in range(4):
            targets[b][z] = value[b * part : (b + 1) * part]
    for target in targets:
        target[planes] = root


def local(estimate, recordings, psf_taps):
    planes, rows, cols = estimate.shape
    taps = psf_taps.shape[-1]
    margin = (taps - 1) // 2
    views = recordings.shape[0]
    devices = lax.axis_size("gz")
    place = lax.axis_index("view")
    place_array = place.reshape(1).astype(jnp.int32)
    up = [(i, i + 1) for i in range(devices - 1)]
    down = [(i + 1, i) for i in range(devices - 1)]
    swap = [(i, i ^ 1) for i in range(4)]
    z_out = planes // 2
    shape = jax.ShapeDtypeStruct

    rounded = estimate.astype(BF16)
    both_ways = [(4 * i + w, 4 * j + w) for w in (0, 2) for i, j in up]
    both_ways += [(4 * i + w, 4 * j + w) for w in (1, 3) for i, j in down]
    mine = lax.ppermute(rounded, ("gz", "view"), both_ways)

    last, first = pl.pallas_call(
        edges_kernel,
        out_shape=[shape((views, margin, rows, cols), BF16)] * 2,
        in_specs=[HBM],
        out_specs=[HBM] * 2,
        scratch_shapes=[
            pltpu.VMEM((2 * views, margin, rows, cols), BF16),
            pltpu.SemaphoreType.DMA((2, 2 * views)),
        ],
        name="edges",
        **params(10**4, 10**4, 58 * 1024 * 1024),
    )(recordings)
    before = lax.ppermute(last, "gz", up)
    after = lax.ppermute(first, "gz", down)

    wide = -(-(z_out + taps - 1) * 8 // 128) * 128
    z_mat, x_mat, y_mat, scales = pl.pallas_call(
        matrices_kernel,
        out_shape=[
            shape((2, views * 2 * z_out * 8, wide), BF16),
            shape((2, views, 2 * cols, 2 * cols), BF16),
            shape((2, views, rows, 2 * rows), BF16),
            shape((views, 1, 128), F32),
        ],
        in_specs=[SMEM, SMEM],
        out_specs=[VMEM] * 4,
        name="matrices",
        **params(10**6, 10**4),
    )(place_array, psf_taps)

    mine, z_mat = lax.optimization_barrier((mine, z_mat))
    mine = (mine[:margin], mine[margin:])
    other = [lax.ppermute(piece, "view", swap) for piece in mine]
    inverses = []
    for early, side in ((True, mine), (False, other)):
        inverses.append(
            pl.pallas_call(
                lambda *refs, early=early: inverse_kernel(early, *refs),
                out_shape=shape((views, planes, rows, cols), F32),
                in_specs=[SMEM] + [VMEM] * 7,
                out_specs=VMEM,
                scratch_shapes=scratch(views, 2, 1, z_out, rows, cols),
                name="inverses",
                **params(10**6, 10**4),
            )(place_array, *side, rounded, z_mat, x_mat, y_mat, scales)
        )
    own, rim = pl.pallas_call(
        arrange_kernel,
        out_shape=[shape((views, planes, rows, cols), BF16), shape((views, 2, margin, rows, cols), F32)],
        in_specs=[SMEM] + [VMEM] * 3,
        out_specs=[VMEM] * 2,
        name="arrange",
        **params(10**5, 10**4),
    )(place_array, recordings, *inverses)
    part = rows // 4
    keep, near, far = pl.pallas_call(
        correction_kernel,
        out_shape=[shape((2, planes + 1, part, cols), F32)] + [shape((planes + 1, part, cols), F32)] * 2,
        in_specs=[VMEM] * 8,
        out_specs=[VMEM] * 3,
        scratch_shapes=scratch(views, 2, 2, z_out, rows, cols) + [pltpu.VMEM((planes, rows, cols), F32)],
        name="corrections",
        **params(4 * 10**9, 5 * 10**6),
    )(before, own, after, rim, z_mat, x_mat, y_mat, scales)
    core_far = lax.ppermute(far, "view", swap)
    core_near = lax.ppermute(near, "view", swap)
    across = lax.ppermute((keep[1] * core_far).astype(jnp.float16), "view", [(i, i ^ 2) for i in range(4)])
    own_rows = lax.dynamic_slice_in_dim(estimate, place * part, part, 1)
    root = keep[0, planes] * core_near[planes]
    partial = own_rows * (keep[0, :planes] * core_near[:planes])
    partial, root, across = lax.optimization_barrier((partial, root, across))
    root = root * across[planes].astype(F32)
    return partial * (across[:planes].astype(F32) * (root * root * root * root))


def solution(mesh):
    in_specs = (P("gz", None, None), P("view", "gz", None, None), P("view", None, None, None))
    out_specs = P("gz", "view", None)
    return jax.shard_map(local, mesh=mesh, in_specs=in_specs, out_specs=out_specs, check_vma=False)
```
